32 devices in a mesh: grp: 2 (over core), ctx: 8 (over z, y), wsh: 2 (over x).
Axes of the slice: x: 2, y: 2, z: 4, core: 2. Of those that a mesh axis runs over, the one named last changes fastest.
Arguments:
- stream: bfloat16 [2, 2, 3072, 512], P('grp', 'wsh', 'ctx'), may hold values from -6 to 6
- memory: bfloat16 [2, 2, 1024, 512], P('grp', 'wsh', 'ctx'), may hold values from -6 to 6
- cotangent: bfloat16 [2, 2, 3072, 512], P('grp', 'wsh', 'ctx'), may hold values from -6 to 6
- deal_order: int32 [2, 2, 24], P('grp', 'wsh'), may hold values from 0 to 23, each once within a row
- offsets: int32 [2, 2, 1], P('grp', 'wsh'), may hold values from 128 to 1024
- context_mask: int32 [2, 2, 16, 8], P('grp', 'wsh'), may hold values 0 or 1
- w_qkv: bfloat16 [512, 1536], replicated, may hold values from -0.25 to 0.25
- w_out: bfloat16 [512, 512], replicated, may hold values from -3 to 3
- w_cq: bfloat16 [512, 512], replicated, may hold values from -0.25 to 0.25
- w_ckv: bfloat16 [512, 1024], replicated, may hold values from -0.25 to 0.25
- w_cout: bfloat16 [512, 512], replicated, may hold values from -3 to 3
- w_up: bfloat16 [512, 2048], replicated, may hold values from -0.25 to 0.25
- w_down: bfloat16 [2048, 512], replicated, may hold values from -0.125 to 0.125
- b_up: float32 [2048], replicated, may hold values from -3 to 3
- gains: float32 [3, 512], replicated, may hold values from 0.5 to 1.5
- biases: float32 [10, 512], replicated, may hold values from -3 to 3
Outputs:
- output: float32 [2, 2, 3072, 512], P('grp', 'wsh', 'ctx')
- grad_stream: float32 [2, 2, 3072, 512], P('grp', 'wsh', 'ctx')
- grad_memory: float32 [2, 2, 1024, 512], P('grp', 'wsh', 'ctx')
- grad_w_qkv: float32 [512, 1536], P(('ctx', 'wsh'))
- grad_w_out: float32 [512, 512], P(('ctx', 'wsh'))
- grad_w_cq: float32 [512, 512], P(('ctx', 'wsh'))
- grad_w_ckv: float32 [512, 1024], P(('ctx', 'wsh'))
- grad_w_cout: float32 [512, 512], P(('ctx', 'wsh'))
- grad_w_up: float32 [512, 2048], P(('ctx', 'wsh'))
- grad_w_down: float32 [2048, 512], P(('ctx', 'wsh'))
- grad_b_up: float32 [2048], P(('ctx', 'wsh'))
- grad_gains: float32 [3, 512], P(None, ('ctx', 'wsh'))
- grad_biases: float32 [10, 512], P(None, ('ctx', 'wsh'))
The draws below stay inside these ranges and needn't reach their ends.
Inputs may be any that keep to these rules, and one draw needn't show every extreme that they name: `deal_order`: each family's row is a permutation of the block numbers 0 to 23.
All inputs are finite; a program needn't handle non-finite values. No bound on the sum of `context_mask` on one device may be relied on, other than what follows from the above.
Results may differ from the reference program's by a relative error of at most 0.025.
Values may be sent and summed in bfloat16 or wider, within the bound.
A program may use at most 320 MiB of HBM per device.

```python
import jax
import jax.numpy as jnp
from jax import lax

D = 512
HEADS = 8
FF = 2048
BLK = 128
CBLK = 16
MEM = 1024
FB = 24
FTOK = 3072
CONTS = 1
PBLK = 8
PROMPT = 1024
N_GRP = 2
N_WSH = 2


def set_ends(values, stream_key, smallest, top_value):
    index_at = [jax.random.randint(jax.random.fold_in(stream_key, axis), (), 0, length) for axis, length in enumerate(values.shape)]
    longest = values.shape.index(max(values.shape))
    neighbour = index_at[:longest] + [(index_at[longest] + 1) % values.shape[longest]] + index_at[longest + 1:]
    return values.at[tuple(index_at)].set(smallest).at[tuple(neighbour)].set(top_value)


def steps_of(key, extent, shards, smallest, high):
    gain, own = 1.0, jax.random.fold_in(key, 6)
    for position, parts in shards:
        draws = jnp.exp(jax.random.uniform(jax.random.fold_in(own, position), (parts,), jnp.float32, smallest / len(shards), high / len(shards)))
        gain = gain * jnp.repeat(draws, extent[position] // parts).reshape([-1 if axis == position else 1 for axis in range(len(extent))])
    return gain


def centred(rng, dims, scale, most, cuts=(), kind=jnp.bfloat16):
    factor_of = steps_of(rng, dims, cuts, -0.22, 0.18) if cuts else 1.0
    values = jax.random.normal(rng, dims, jnp.float32) * scale * factor_of
    return jnp.minimum(jnp.maximum(values, -most), most).astype(kind)


def setup_inputs(seed: int = 0) -> dict:
    streams_of = jax.random.split(jax.random.key(seed), 17)
    return {
        "stream": centred(streams_of[0], (N_GRP, N_WSH, FTOK, D), 1.0, 6.0, ((0, 2), (1, 2), (2, 8))),
        "memory": centred(streams_of[1], (N_GRP, N_WSH, MEM, D), 1.0, 6.0, ((0, 2), (1, 2), (2, 8))),
        "cotangent": centred(streams_of[2], (N_GRP, N_WSH, FTOK, D), 1.0, 6.0, ((0, 2), (1, 2), (2, 8))),
        "deal_order": jax.vmap(lambda own: jax.random.permutation(own, FB))(jax.random.split(streams_of[3], N_GRP * N_WSH)).reshape((N_GRP, N_WSH, FB)).astype(jnp.int32),
        "offsets": set_ends(jax.random.randint(streams_of[4], (N_GRP, N_WSH, CONTS), BLK, PROMPT + 1), jax.random.fold_in(streams_of[4], 1), BLK, PROMPT).astype(jnp.int32),
        "context_mask": set_ends((jax.random.randint(streams_of[5], (N_GRP, N_WSH, CONTS * CBLK, PBLK), 0, 4) < 3).astype(jnp.int32), jax.random.fold_in(streams_of[5], 1), 0, 1),
        "w_qkv": centred(streams_of[6], (D, 3 * D), D ** -0.5, 0.25),
        "w_out": centred(streams_of[7], (D, D), (max(D // 128, 1)) ** -0.5, 3.0),
        "w_cq": centred(streams_of[8], (D, D), D ** -0.5, 0.25),
        "w_ckv": centred(streams_of[9], (D, 2 * D), D ** -0.5, 0.25),
        "w_cout": centred(streams_of[10], (D, D), (max(D // 128, 1)) ** -0.5, 3.0),
        "w_up": centred(streams_of[11], (D, FF), D ** -0.5, 0.25),
        "w_down": centred(streams_of[12], (FF, D), FF ** -0.5, 0.125),
        "b_up": centred(streams_of[13], (FF,), 0.3, 3.0, (), jnp.float32),
        "gains": jnp.clip(1.0 + 0.1 * jax.random.normal(streams_of[14], (3, D), jnp.float32), 0.5, 1.5),
        "biases": centred(streams_of[15], (10, D), 0.3, 3.0, (), jnp.float32),
    }


@jax.custom_vjp
def low(v):
    return lax.optimization_barrier(v.astype(jnp.bfloat16)).astype(jnp.float32)

@jax.custom_vjp
def low_back(v):
    return v

def low_keep(v):
    return (low(v), None)

def low_pass(kept, grad):
    return (grad,)

def back_keep(v):
    return (v, None)

def back_low(kept, grad):
    return (low(grad),)
low.defvjp(low_keep, low_pass)
low_back.defvjp(back_keep, back_low)
NEG_FILL = -1000000000.0
EPS_NORM = 1e-05

def matmul(left, right):
    return jnp.dot(left, right, precision=lax.Precision.HIGHEST)

def gelu_exact(values):
    return jax.nn.gelu(values, approximate=False)

def norm_rows(values, gain_vec, shift_vec):
    center = values - lax.optimization_barrier(jnp.mean(values, axis=-1, keepdims=True))
    spread = lax.optimization_barrier(jnp.mean(center * center, axis=-1, keepdims=True))
    return center * lax.rsqrt(spread + EPS_NORM) * gain_vec + shift_vec

def seq_index(positions, prompt_len, cont_len):
    later = (jnp.int32(1) + (positions - jnp.int32(prompt_len)) // jnp.int32(cont_len)).astype(jnp.int32)
    return jnp.where(positions < jnp.int32(prompt_len), jnp.zeros_like(later), later).astype(jnp.int32)

def visible(query_pos, key_ids, offsets, context_mask, block_len, prompt_blocks, cont_blocks):
    prompt_len = prompt_blocks * block_len
    cont_len = cont_blocks * block_len
    cont_count = offsets.shape[0]
    mask_rows_all = context_mask.shape[0]
    key_pos = (key_ids[:, None].astype(jnp.int32) * jnp.int32(block_len) + jnp.arange(block_len, dtype=jnp.int32)[None, :]).reshape(-1).astype(jnp.int32)
    query_pos = query_pos.astype(jnp.int32)
    query_seq = seq_index(query_pos, prompt_len, cont_len)
    key_seq = seq_index(key_pos, prompt_len, cont_len)
    inside = (query_seq[:, None] == key_seq[None, :]) & (key_pos[None, :] <= query_pos[:, None])
    cont_pick = jnp.clip(query_seq - jnp.int32(1), 0, cont_count - 1).astype(jnp.int32)
    cont_hit = (cont_pick[:, None] == jnp.arange(cont_count, dtype=jnp.int32)[None, :]).astype(jnp.int32)
    prompt_limit = lax.optimization_barrier(jnp.sum(cont_hit * offsets.astype(jnp.int32)[None, :], axis=1)).astype(jnp.int32)
    query_block = jnp.clip((query_pos - jnp.int32(prompt_len)) // jnp.int32(block_len), 0, mask_rows_all - 1).astype(jnp.int32)
    row_hit = (query_block[:, None] == jnp.arange(mask_rows_all, dtype=jnp.int32)[None, :]).astype(jnp.int32)
    mask_rows = jnp.dot(row_hit, context_mask.astype(jnp.int32)).astype(jnp.int32)
    key_block = jnp.clip(key_ids.astype(jnp.int32), 0, prompt_blocks - 1).astype(jnp.int32)
    col_hit = (key_block[:, None] == jnp.arange(prompt_blocks, dtype=jnp.int32)[None, :]).astype(jnp.int32)
    block_open = jnp.dot(mask_rows, col_hit.T).astype(jnp.int32) > 0
    block_open = jnp.repeat(block_open, block_len, axis=1) | (key_pos[None, :] < jnp.int32(block_len))
    from_prompt = (query_seq[:, None] > 0) & (key_seq[None, :] == 0) & (key_pos[None, :] < prompt_limit[:, None]) & block_open
    return inside | from_prompt

def attend(queries, key_rows, values, query_pos, masker):
    row_count = queries.shape[0]
    block_rows = min(512, row_count)
    head_width = queries.shape[1] // HEADS
    score_scale = head_width ** (-0.5)
    query_blocks = queries.reshape(row_count // block_rows, block_rows, HEADS, head_width)
    pos_blocks = query_pos.reshape(row_count // block_rows, block_rows)
    key_heads = key_rows.reshape(key_rows.shape[0], HEADS, head_width)
    value_heads = values.reshape(values.shape[0], HEADS, head_width)

    def one_block(pieces):
        query_blk, pos_blk = pieces
        scores = low_back(jnp.einsum('qhd,khd->hqk', query_blk, key_heads, precision=lax.Precision.HIGHEST) * score_scale)
        if masker is not None:
            filler = jnp.full(scores.shape, NEG_FILL, scores.dtype)
            scores = jnp.where(masker(pos_blk)[None], scores, filler)
        soft_weights = jax.nn.softmax(scores, axis=-1)
        mixed_heads = jnp.einsum('hqk,khd->qhd', low(soft_weights), value_heads, precision=lax.Precision.HIGHEST)
        return mixed_heads.reshape(block_rows, HEADS * head_width)
    result = lax.map(jax.checkpoint(one_block), (query_blocks, pos_blocks))
    return result.reshape(row_count, HEADS * head_width)

def family(params, stream, memory, deal_ids, offsets, context_mask):
    w_qkv, w_out, w_cq, w_ckv, w_cout, w_up, w_down, b_up, gains, biases = params
    model_width = stream.shape[1]
    positions = (deal_ids[:, None].astype(jnp.int32) * jnp.int32(BLK) + jnp.arange(BLK, dtype=jnp.int32)[None, :]).reshape(-1).astype(jnp.int32)
    zeros_row = jnp.zeros((model_width,), biases.dtype)
    projected = low(low_back(matmul(stream, w_qkv) + jnp.concatenate([biases[0], zeros_row, biases[1]])))

    def masker(pos_blk):
        return visible(pos_blk, deal_ids, offsets, context_mask, BLK, PBLK, CBLK)
    attended = low(low_back(attend(projected[:, :model_width], projected[:, model_width:2 * model_width], projected[:, 2 * model_width:], positions, masker)))
    first_sum = stream + low_back(matmul(attended, w_out) + biases[2])
    normed_one = norm_rows(first_sum, gains[0], biases[3])
    normed_low = low(normed_one)
    cross_query = low(low_back(matmul(normed_low, w_cq) + biases[4]))
    cross_kv = low(low_back(matmul(memory, w_ckv) + jnp.concatenate([zeros_row, biases[5]])))
    cross_attended = low(low_back(attend(cross_query, cross_kv[:, :model_width], cross_kv[:, model_width:], positions, None)))
    second_sum = normed_one + low_back(matmul(cross_attended, w_cout) + biases[6])
    normed_two = norm_rows(second_sum, gains[1], biases[7])
    normed_two_low = low(normed_two)
    hidden_pre = low_back(matmul(normed_two_low, w_up) + b_up)
    hidden = low(gelu_exact(hidden_pre))
    third_sum = normed_two + low_back(matmul(hidden, w_down) + biases[8])
    return norm_rows(third_sum, gains[2], biases[9])

def reference(stream, memory, cotangent, deal_order, offsets, context_mask, w_qkv, w_out, w_cq, w_ckv, w_cout, w_up, w_down, b_up, gains, biases):
    params = tuple((weight.astype(jnp.float32) for weight in (w_qkv, w_out, w_cq, w_ckv, w_cout, w_up, w_down, b_up, gains, biases)))
    groups = stream.shape[0] * stream.shape[1]
    flat_stream = stream.astype(jnp.float32).reshape(groups, FTOK, D)
    flat_memory = memory.astype(jnp.float32).reshape(groups, MEM, D)
    flat_deal = deal_order.astype(jnp.int32).reshape(groups, FB)
    flat_offsets = offsets.astype(jnp.int32).reshape(groups, CONTS)
    flat_mask = context_mask.astype(jnp.int32).reshape(groups, CONTS * CBLK, PBLK)

    def forward(weights, streams, memories):

        def one_family(pieces):
            return family(weights, pieces[0], pieces[1], pieces[2], pieces[3], pieces[4])
        return lax.map(one_family, (streams, memories, flat_deal, flat_offsets, flat_mask))
    output, pullback = jax.vjp(forward, params, flat_stream, flat_memory)
    grad_params, grad_stream, grad_memory = pullback(cotangent.astype(jnp.float32).reshape(output.shape))
    return (output.reshape(stream.shape), grad_stream.reshape(stream.shape), grad_memory.reshape(memory.shape), grad_params[0], grad_params[1], grad_params[2], grad_params[3], grad_params[4], grad_params[5], grad_params[6], grad_params[7], grad_params[8], grad_params[9])
```

```python
import functools

import jax
import jax.numpy as jnp
from jax import lax
from jax.experimental import pallas as pl
from jax.experimental.pallas import tpu as pltpu
from jax.sharding import PartitionSpec as P

HEADS = 8
BLK = 128
CBLK = 16


NEG_FILL = -1000000000.0
EPS_NORM = 1e-05


MESH_ID = pl.DeviceIdType.MESH
TILE = 512
BIG_VMEM = 56 << 20


def nn(left, right):
    return lax.dot_general(
        left, right, (((1,), (0,)), ((), ())), preferred_element_type=jnp.float32
    )


def nt(left, right):
    return lax.dot_general(
        left, right, (((1,), (1,)), ((), ())), preferred_element_type=jnp.float32
    )


def tn(left, right):
    return lax.dot_general(
        left, right, (((0,), (0,)), ((), ())), preferred_element_type=jnp.float32
    )


def swap(block):
    return block.astype(jnp.float32).T.astype(block.dtype)


def device_at(grp, ctx, wsh):
    return (grp, ctx, wsh)


def exchange_kernel(parts, src_ref, dst_ref, send_sem, recv_sem):
    grp, me, wsh = lax.axis_index("grp"), lax.axis_index("ctx"), lax.axis_index("wsh")
    barrier = pltpu.get_barrier_semaphore()
    for step in range(1, parts):
        pl.semaphore_signal(
            barrier,
            inc=1,
            device_id=(grp, lax.rem(me + step, parts), wsh),
            device_id_type=MESH_ID,
        )
    pl.semaphore_wait(barrier, parts - 1)
    copies = []
    for step in range(1, parts):
        peer = lax.rem(me + step, parts)
        copy = pltpu.make_async_remote_copy(
            src_ref=src_ref.at[peer],
            dst_ref=dst_ref.at[me],
            send_sem=send_sem.at[step - 1],
            recv_sem=recv_sem.at[step - 1],
            device_id=(grp, peer, wsh),
            device_id_type=MESH_ID,
        )
        copy.start()
        copies.append(copy)
    dst_ref[pl.ds(me, 1)] = src_ref[pl.ds(me, 1)]
    for copy in copies:
        copy.wait()


def exchange(block, collective_id):
    parts = block.shape[0]
    return pl.pallas_call(
        functools.partial(exchange_kernel, parts),
        out_shape=jax.ShapeDtypeStruct(block.shape, block.dtype),
        in_specs=[pl.BlockSpec(memory_space=pltpu.VMEM)],
        out_specs=pl.BlockSpec(memory_space=pltpu.VMEM),
        scratch_shapes=[
            pltpu.SemaphoreType.DMA((parts - 1,)),
            pltpu.SemaphoreType.DMA((parts - 1,)),
        ],
        compiler_params=pltpu.CompilerParams(
            collective_id=collective_id, has_side_effects=True, vmem_limit_bytes=BIG_VMEM
        ),
        name="exchange_%d" % collective_id,
    )(block)


def hide_later(scores):
    rows = lax.broadcasted_iota(jnp.int32, scores.shape, 0)
    cols = lax.broadcasted_iota(jnp.int32, scores.shape, 1)
    return jnp.where(rows <= cols, scores, NEG_FILL)


def hide_prompt(scores, lim_ref, tile, chunk, prompt_blocks):
    span = TILE // BLK
    rows = lax.broadcasted_iota(jnp.int32, (BLK, BLK), 0)
    columns = []
    for q_sub in range(span):
        pieces = []
        for k_sub in range(span):
            key_block = chunk * span + k_sub
            limit = lim_ref[tile * span + q_sub - prompt_blocks, key_block] - key_block * BLK
            part = scores[k_sub * BLK : (k_sub + 1) * BLK, q_sub * BLK : (q_sub + 1) * BLK]
            pieces.append(jnp.where(rows < limit, part, NEG_FILL))
        columns.append(jnp.concatenate(pieces, axis=0))
    return jnp.concatenate(columns, axis=1)


def self_fwd_kernel(prompt_blocks, inv_ref, deal_ref, lim_ref, land_ref, out_ref, exact_ref, lse_ref,
                    q_ref, k_ref, kt_ref, v_ref, vt_ref, qt_ref):
    blocks, width, _ = land_ref.shape
    head = width // 3
    prompt_tiles = prompt_blocks * BLK // TILE
    for pos in range(blocks):
        block = land_ref[inv_ref[pos]]
        at = slice(pos * BLK, (pos + 1) * BLK)
        qt_ref[:, at] = block[:head]
        kt_ref[:, at] = block[head : 2 * head]
        vt_ref[:, at] = block[2 * head :]
        flat = swap(block)
        q_ref[at, :] = flat[:, :head]
        k_ref[at, :] = flat[:, head : 2 * head]
        v_ref[at, :] = flat[:, 2 * head :]

    def tile_step(tile, carry):
        here = pl.ds(pl.multiple_of(tile * TILE, TILE), TILE)
        queries = qt_ref[:, here]

        def chunk_step(chunk, state, hide):
            top, total, mixed = state
            there = pl.ds(pl.multiple_of(chunk * TILE, TILE), TILE)
            scores = hide(nn(k_ref[there, :], queries), chunk)
            new_top = jnp.maximum(top, jnp.max(scores, axis=0, keepdims=True))
            weights = jnp.exp(scores - new_top)
            fade = jnp.exp(top - new_top)
            total = total * fade + jnp.sum(weights, axis=0, keepdims=True)
            mixed = mixed * fade + nn(vt_ref[:, there], weights.astype(jnp.bfloat16))
            return new_top, total, mixed

        state = (
            jnp.full((1, TILE), NEG_FILL, jnp.float32),
            jnp.zeros((1, TILE), jnp.float32),
            jnp.zeros((head, TILE), jnp.float32),
        )
        state = chunk_step(tile, state, lambda s, c: hide_later(s))
        later = tile >= prompt_tiles
        first = jnp.where(later, prompt_tiles, 0)
        state = lax.fori_loop(
            first, tile, lambda c, s: chunk_step(c, s, lambda x, _: x), state
        )
        state = lax.fori_loop(
            0,
            first,
            lambda c, s: chunk_step(
                c, s, lambda x, cc: hide_prompt(x, lim_ref, tile, cc, prompt_blocks)
            ),
            state,
        )
        top, total, mixed = state
        exact_ref[:, here] = mixed / total
        lse_ref[:, here] = top + jnp.log(total)
        return carry

    lax.fori_loop(0, blocks * BLK // TILE, tile_step, 0)
    for row in range(blocks):
        at = pl.ds(pl.multiple_of(deal_ref[row] * BLK, BLK), BLK)
        out_ref[row] = exact_ref[:, at].astype(jnp.bfloat16)


def self_bwd_kernel(prompt_blocks, inv_ref, deal_ref, lim_ref, land_ref, exact_ref, lse_ref,
                    q_ref, k_ref, kt_ref, v_ref, qt_ref, out_ref,
                    up_ref, upt_ref, dk_ref, dv_ref, dqt_ref):
    blocks, head, _ = land_ref.shape
    prompt_tiles = prompt_blocks * BLK // TILE
    score_scale = head ** (-0.5)
    for pos in range(blocks):
        block = land_ref[inv_ref[pos]]
        at = slice(pos * BLK, (pos + 1) * BLK)
        upt_ref[:, at] = block
        up_ref[at, :] = swap(block)
    dk_ref[...] = jnp.zeros_like(dk_ref)
    dv_ref[...] = jnp.zeros_like(dv_ref)

    def tile_step(tile, carry):
        here = pl.ds(pl.multiple_of(tile * TILE, TILE), TILE)
        queries_t = qt_ref[:, here]
        queries = q_ref[here, :]
        upstream_t = upt_ref[:, here]
        upstream = up_ref[here, :]
        lse = lse_ref[:, here]
        delta = jnp.sum(exact_ref[:, here] * upstream_t.astype(jnp.float32), axis=0, keepdims=True)

        def chunk_step(chunk, grad_q, hide):
            there = pl.ds(pl.multiple_of(chunk * TILE, TILE), TILE)
            scores = hide(nn(k_ref[there, :], queries_t), chunk)
            weights = jnp.exp(scores - lse)
            grad_weights = nn(v_ref[there, :], upstream_t)
            grad_scores = (weights * (grad_weights - delta)).astype(jnp.bfloat16)
            dv_ref[there, :] += nn(weights.astype(jnp.bfloat16), upstream)
            dk_ref[there, :] += nn(grad_scores, queries)
            return grad_q + nn(kt_ref[:, there], grad_scores)

        grad_q = jnp.zeros((head, TILE), jnp.float32)
        grad_q = chunk_step(tile, grad_q, lambda s, c: hide_later(s))
        later = tile >= prompt_tiles
        first = jnp.where(later, prompt_tiles, 0)
        grad_q = lax.fori_loop(
            first, tile, lambda c, s: chunk_step(c, s, lambda x, _: x), grad_q
        )
        grad_q = lax.fori_loop(
            0,
            first,
            lambda c, s: chunk_step(
                c, s, lambda x, cc: hide_prompt(x, lim_ref, tile, cc, prompt_blocks)
            ),
            grad_q,
        )
        dqt_ref[:, here] = (grad_q * score_scale).astype(jnp.bfloat16)
        return carry

    lax.fori_loop(0, blocks * BLK // TILE, tile_step, 0)
    for row in range(blocks):
        at = pl.ds(pl.multiple_of(deal_ref[row] * BLK, BLK), BLK)
        out_ref[row, :head] = dqt_ref[:, at]
        out_ref[row, head : 2 * head] = dk_ref[at, :].T.astype(jnp.bfloat16)
        out_ref[row, 2 * head :] = dv_ref[at, :].T.astype(jnp.bfloat16)


def self_forward_call(inverse, deal_ids, limits, land, prompt_blocks):
    blocks, width, _ = land.shape
    head = width // 3
    tokens = blocks * BLK
    smem = pl.BlockSpec(memory_space=pltpu.SMEM)
    vmem = pl.BlockSpec(memory_space=pltpu.VMEM)
    low, wide = jnp.bfloat16, jnp.float32
    return pl.pallas_call(
        functools.partial(self_fwd_kernel, prompt_blocks),
        out_shape=[
            jax.ShapeDtypeStruct((blocks, head, BLK), low),
            jax.ShapeDtypeStruct((head, tokens), wide),
            jax.ShapeDtypeStruct((1, tokens), wide),
            jax.ShapeDtypeStruct((tokens, head), low),
            jax.ShapeDtypeStruct((tokens, head), low),
            jax.ShapeDtypeStruct((head, tokens), low),
            jax.ShapeDtypeStruct((tokens, head), low),
            jax.ShapeDtypeStruct((head, tokens), low),
            jax.ShapeDtypeStruct((head, tokens), low),
        ],
        in_specs=[smem, smem, smem, vmem],
        out_specs=[vmem] * 9,
        compiler_params=pltpu.CompilerParams(vmem_limit_bytes=BIG_VMEM),
        name="self_forward",
    )(inverse, deal_ids, limits, land)


def self_backward_call(inverse, deal_ids, limits, land, kept, prompt_blocks):
    blocks, head, _ = land.shape
    tokens = blocks * BLK
    exact, lse, q, k, kt, v, vt, qt = kept
    smem = pl.BlockSpec(memory_space=pltpu.SMEM)
    vmem = pl.BlockSpec(memory_space=pltpu.VMEM)
    low, wide = jnp.bfloat16, jnp.float32
    return pl.pallas_call(
        functools.partial(self_bwd_kernel, prompt_blocks),
        out_shape=jax.ShapeDtypeStruct((blocks, 3 * head, BLK), low),
        in_specs=[smem, smem, smem] + [vmem] * 8,
        out_specs=vmem,
        scratch_shapes=[
            pltpu.VMEM((tokens, head), low),
            pltpu.VMEM((head, tokens), low),
            pltpu.VMEM((tokens, head), wide),
            pltpu.VMEM((tokens, head), wide),
            pltpu.VMEM((head, tokens), low),
        ],
        compiler_params=pltpu.CompilerParams(vmem_limit_bytes=BIG_VMEM),
        name="self_backward",
    )(inverse, deal_ids, limits, land, exact, lse, q, k, kt, v, qt)

def gelu_exact(values):
    return jax.nn.gelu(values, approximate=False)


def norm_rows(values, gain_vec, shift_vec):
    center = values - jnp.mean(values, axis=-1, keepdims=True)
    spread = jnp.mean(center * center, axis=-1, keepdims=True)
    return center * lax.rsqrt(spread + EPS_NORM) * gain_vec + shift_vec


def norm_back(values, gain_vec, shift_vec, upstream):
    _, pullback = jax.vjp(norm_rows, values, gain_vec, shift_vec)
    return pullback(upstream)


def seq_index(positions, prompt_len, cont_len):
    later = jnp.int32(1) + (positions - jnp.int32(prompt_len)) // jnp.int32(cont_len)
    return jnp.where(positions < prompt_len, jnp.zeros_like(later), later)


def visible(query_pos, key_ids, offsets, context_mask, block_len, prompt_blocks, cont_blocks):
    prompt_len = prompt_blocks * block_len
    cont_len = cont_blocks * block_len
    cont_count = offsets.shape[0]
    key_pos = (
        key_ids[:, None] * jnp.int32(block_len) + jnp.arange(block_len, dtype=jnp.int32)[None, :]
    ).reshape(-1)
    query_seq = seq_index(query_pos, prompt_len, cont_len)
    key_seq = seq_index(key_pos, prompt_len, cont_len)
    inside = (query_seq[:, None] == key_seq[None, :]) & (key_pos[None, :] <= query_pos[:, None])
    cont_pick = jnp.clip(query_seq - 1, 0, cont_count - 1)
    prompt_limit = jnp.take(offsets, cont_pick)
    query_block = jnp.clip(
        (query_pos - jnp.int32(prompt_len)) // jnp.int32(block_len), 0, cont_count * cont_blocks - 1
    )
    mask_rows = jnp.take(context_mask, query_block, axis=0)
    key_block = jnp.clip(key_ids, 0, prompt_blocks - 1)
    block_open = jnp.take(mask_rows, key_block, axis=1) > 0
    block_open = jnp.repeat(block_open, block_len, axis=1) | (key_pos[None, :] < block_len)
    from_prompt = (
        (query_seq[:, None] > 0)
        & (key_seq[None, :] == 0)
        & (key_pos[None, :] < prompt_limit[:, None])
        & block_open
    )
    return inside | from_prompt


def dot_first(left, right):
    return lax.dot_general(
        left, right, (((0,), (0,)), ((), ())), preferred_element_type=jnp.float32
    )


def dot_last(left, right):
    return lax.dot_general(
        left, right, (((1,), (1,)), ((), ())), preferred_element_type=jnp.float32
    )


def to_heads(matrix, head_count):
    row_count, model_width = matrix.shape
    return matrix.reshape(row_count, head_count, model_width // head_count).transpose(1, 0, 2)


def from_heads(stacked):
    head_count, row_count, head_width = stacked.shape
    return stacked.transpose(1, 0, 2).reshape(row_count, head_count * head_width)


def pair_heads(key_rows, value_rows, head_count):
    return jnp.concatenate(
        [to_heads(key_rows, head_count), to_heads(value_rows, head_count)], axis=2
    )


def head_scores(queries, key_rows, allowed):
    score_scale = queries.shape[1] ** (-0.5)
    scores = dot_last(queries, key_rows) * score_scale
    if allowed is not None:
        scores = jnp.where(allowed, scores, NEG_FILL)
    return scores


def head_forward(queries, keyval, allowed):
    head_width = queries.shape[1]
    scores = head_scores(queries, keyval[:, :head_width], allowed)
    row_top = jnp.max(scores, axis=1, keepdims=True)
    exp_scores = jnp.exp(scores - row_top)
    row_total = jnp.sum(exp_scores, axis=1, keepdims=True)
    soft_weights = (exp_scores / row_total).astype(jnp.bfloat16)
    mixed_heads = jnp.dot(soft_weights, keyval[:, head_width:], preferred_element_type=jnp.float32)
    return (mixed_heads, row_top + jnp.log(row_total))


def head_backward(queries, keyval, upstream, log_total, allowed):
    head_width = queries.shape[1]
    score_scale = head_width ** (-0.5)
    key_rows = keyval[:, :head_width]
    scores = head_scores(queries, key_rows, allowed)
    soft_weights = jnp.exp(scores - log_total)
    grad_soft = dot_last(upstream, keyval[:, head_width:])
    row_delta = jnp.sum(soft_weights * grad_soft, axis=1, keepdims=True)
    grad_scores = (soft_weights * (grad_soft - row_delta)).astype(jnp.bfloat16)
    grad_query = jnp.dot(grad_scores, key_rows, preferred_element_type=jnp.float32) * score_scale
    grad_keys = dot_first(grad_scores, queries) * score_scale
    grad_values = dot_first(soft_weights.astype(jnp.bfloat16), upstream)
    return (grad_query, jnp.concatenate([grad_keys, grad_values], axis=1))


PIECES = 4


def place():
    ctx = lax.axis_index("ctx")
    return lax.axis_index("grp"), ctx // 2, lax.rem(ctx, 2), lax.axis_index("wsh")


def device(grp, row, col, wsh):
    return (grp, row * 2 + col, wsh)


def remote(src_ref, dst_ref, send_sem, recv_sem, target):
    return pltpu.make_async_remote_copy(
        src_ref=src_ref,
        dst_ref=dst_ref,
        send_sem=send_sem,
        recv_sem=recv_sem,
        device_id=target,
        device_id_type=MESH_ID,
    )


def greet(targets):
    barrier = pltpu.get_barrier_semaphore()
    for target in targets:
        pl.semaphore_signal(barrier, inc=1, device_id=target, device_id_type=MESH_ID)
    pl.semaphore_wait(barrier, len(targets))


def plus(left, right):
    return left.astype(jnp.float32) + right.astype(jnp.float32)


def reduce_kernel(part_ref, few_ref, out_ref, few_out_ref,
                  core_land, hop_sum, hop_land, turn_sum, turn_land, row_land,
                  few_sum, few_land, send_sem, recv_sem, few_send, few_recv):
    grp, row, col, wsh = place()
    rows = 4
    core_peer = device(1 - grp, row, col, wsh)
    wsh_peer = device(grp, row, col, 1 - wsh)
    col_peer = device(grp, row, 1 - col, wsh)
    row_peers = [device(grp, lax.rem(row + step, rows), col, wsh) for step in range(1, rows)]
    near = row + 1 - 2 * lax.rem(row, 2)
    few_peers = [core_peer, wsh_peer, col_peer, device(grp, near, col, wsh), row_peers[1]]
    greet([core_peer, wsh_peer, col_peer] + row_peers)
    pieces = part_ref.shape[0]

    def few_copy(step):
        return remote(
            few_sum.at[step], few_land.at[step], few_send.at[step], few_recv.at[step],
            few_peers[step],
        )

    core_copies = []
    for piece in range(pieces):
        copy = remote(
            part_ref.at[piece, 1 - grp], core_land.at[piece],
            send_sem.at[piece, 0], recv_sem.at[piece, 0], core_peer,
        )
        copy.start()
        core_copies.append(copy)
    few_sum[0] = few_ref[...]
    few_copy(0).start()
    hop_copies = []
    for piece in range(pieces):
        core_copies[piece].wait()
        hop_sum[piece] = plus(part_ref[piece, grp], core_land[piece]).astype(jnp.bfloat16)
        if piece % 2 == 0:
            source, target = hop_sum.at[piece, :, :, 1 - wsh], wsh_peer
        else:
            source, target = hop_sum.at[piece, :, 1 - col], col_peer
        copy = remote(
            source, hop_land.at[piece], send_sem.at[piece, 1], recv_sem.at[piece, 1], target
        )
        copy.start()
        hop_copies.append(copy)
    few_copy(0).wait()
    few_sum[1] = few_sum[0] + few_land[0]
    few_copy(1).start()
    turn_copies = []
    for piece in range(pieces):
        hop_copies[piece].wait()
        if piece % 2 == 0:
            mine, source_at, target = hop_sum[piece, :, :, wsh], 1 - col, col_peer
        else:
            mine, source_at, target = hop_sum[piece, :, col], 1 - wsh, wsh_peer
        turn_sum[piece] = plus(mine, hop_land[piece]).astype(jnp.bfloat16)
        copy = remote(
            turn_sum.at[piece, :, source_at], turn_land.at[piece],
            send_sem.at[piece, 2], recv_sem.at[piece, 2], target,
        )
        copy.start()
        turn_copies.append(copy)
        if piece == 1:
            few_copy(1).wait()
            few_sum[2] = few_sum[1] + few_land[1]
            few_copy(2).start()
    few_copy(2).wait()
    few_sum[3] = few_sum[2] + few_land[2]
    few_copy(3).start()
    row_copies = []
    for piece in range(pieces):
        turn_copies[piece].wait()
        mine = turn_sum[piece, :, col] if piece % 2 == 0 else turn_sum[piece, :, wsh]
        turn_sum[piece, :, 0] = plus(mine, turn_land[piece]).astype(jnp.bfloat16)
        copies = []
        for step in range(1, rows):
            peer = lax.rem(row + step, rows)
            copy = remote(
                turn_sum.at[piece, peer, 0], row_land.at[piece, row],
                send_sem.at[piece, 2 + step], recv_sem.at[piece, 2 + step], row_peers[step - 1],
            )
            copy.start()
            copies.append(copy)
        row_copies.append(copies)
    few_copy(3).wait()
    few_sum[4] = few_sum[3] + few_land[3]
    few_copy(4).start()
    last_copies = []
    for piece in range(pieces):
        total = turn_sum[piece, row, 0].astype(jnp.float32)
        for step, copy in enumerate(row_copies[piece]):
            copy.wait()
            total = total + row_land[piece, lax.rem(row + rows - 1 - step, rows)].astype(jnp.float32)
        out_ref[piece, grp] = total
        copy = remote(
            out_ref.at[piece, grp], out_ref.at[piece, grp],
            send_sem.at[piece, 6], recv_sem.at[piece, 6], core_peer,
        )
        copy.start()
        last_copies.append(copy)
    few_copy(4).wait()
    few_out_ref[...] = few_sum[4] + few_land[4]
    for copy in last_copies:
        copy.wait()


def reduce_weights(parts, few, collective_id):
    pieces, _, shards_, half, width = parts.shape
    vmem = pl.BlockSpec(memory_space=pltpu.VMEM)
    low, wide = jnp.bfloat16, jnp.float32
    dma = pltpu.SemaphoreType.DMA
    return pl.pallas_call(
        reduce_kernel,
        out_shape=[
            jax.ShapeDtypeStruct((pieces, 2, half, width), wide),
            jax.ShapeDtypeStruct(few.shape, wide),
        ],
        in_specs=[vmem, vmem],
        out_specs=[vmem, vmem],
        scratch_shapes=[
            pltpu.VMEM((pieces, 4, 2, 2, half, width), low),
            pltpu.VMEM((pieces, 4, 2, 2, half, width), low),
            pltpu.VMEM((pieces, 4, 2, half, width), low),
            pltpu.VMEM((pieces, 4, 2, half, width), low),
            pltpu.VMEM((pieces, 4, half, width), low),
            pltpu.VMEM((pieces, 4, half, width), low),
            pltpu.VMEM((5,) + few.shape, wide),
            pltpu.VMEM((5,) + few.shape, wide),
            dma((pieces, 7)),
            dma((pieces, 7)),
            dma((5,)),
            dma((5,)),
        ],
        compiler_params=pltpu.CompilerParams(
            collective_id=collective_id, has_side_effects=True, vmem_limit_bytes=BIG_VMEM
        ),
        name="reduce_weights",
    )(parts.reshape(pieces, 2, 4, 2, 2, half, width), few)


def pack_weights(grads):
    wide = [g.reshape(16, 2, 16, g.shape[1]) for g in grads[:-1]]
    down = grads[-1].reshape(16, 4, 2, 16, grads[-1].shape[1])
    wide += [down[:, part] for part in range(4)]
    packed = jnp.concatenate([g.astype(jnp.bfloat16) for g in wide], axis=3)
    width = packed.shape[3] // PIECES
    return packed.reshape(16, 2, 16, PIECES, width).transpose(3, 1, 0, 2, 4)


def unpack_weights(total, widths):
    flat = total.transpose(1, 2, 0, 3).reshape(32, -1)
    out, at = [], 0
    for width in widths:
        out.append(flat[:, at : at + width])
        at += width
    down = flat[:, at:]
    out.append(down.reshape(32, 4, -1).transpose(1, 0, 2).reshape(128, -1))
    return out


def shards(
    stream,
    memory,
    cotangent,
    deal_order,
    offsets,
    context_mask,
    w_qkv,
    w_out,
    w_cq,
    w_ckv,
    w_cout,
    w_up,
    w_down,
    b_up,
    gains,
    biases,
):
    tokens = stream[0, 0]
    row_count, model_width = tokens.shape
    head_width = model_width // HEADS
    deal_ids = deal_order[0, 0]
    prompt_blocks = context_mask.shape[3]
    own_blocks = row_count // BLK
    own_ids = lax.dynamic_slice_in_dim(deal_ids, lax.axis_index("ctx") * own_blocks, own_blocks)
    query_pos = (
        own_ids[:, None] * jnp.int32(BLK) + jnp.arange(BLK, dtype=jnp.int32)[None, :]
    ).reshape(-1)
    allowed = visible(
        query_pos, deal_ids, offsets[0, 0], context_mask[0, 0], BLK, prompt_blocks, CBLK
    )
    zeros_row = jnp.zeros((model_width,), jnp.float32)
    projected = (
        jnp.dot(tokens, w_qkv, preferred_element_type=jnp.float32)
        + jnp.concatenate([biases[0], zeros_row, biases[1]])
    ).astype(jnp.bfloat16)
    query_heads = to_heads(projected[:, :model_width], HEADS)
    keyval_own = pair_heads(
        projected[:, model_width : 2 * model_width], projected[:, 2 * model_width :], HEADS
    )
    keyval_all = lax.all_gather(keyval_own, "ctx", axis=1, tiled=True)

    def self_forward(pieces):
        return head_forward(pieces[0], pieces[1], allowed)

    self_out, self_lse = lax.map(self_forward, (query_heads, keyval_all))
    attended = from_heads(self_out).astype(jnp.bfloat16)
    first_sum = (
        tokens.astype(jnp.float32)
        + jnp.dot(attended, w_out, preferred_element_type=jnp.float32)
        + biases[2]
    )
    normed_one = norm_rows(first_sum, gains[0], biases[3])
    normed_low = normed_one.astype(jnp.bfloat16)
    cross_query = (
        jnp.dot(normed_low, w_cq, preferred_element_type=jnp.float32) + biases[4]
    ).astype(jnp.bfloat16)
    cross_bias = jnp.concatenate([zeros_row, biases[5]])
    memory_own = memory[0, 0]
    memory_all = lax.all_gather(memory_own, "ctx", axis=0, tiled=True)
    cross_kv = (jnp.dot(memory_all, w_ckv, preferred_element_type=jnp.float32) + cross_bias).astype(
        jnp.bfloat16
    )
    cross_heads = pair_heads(cross_kv[:, :model_width], cross_kv[:, model_width:], HEADS)
    cross_query_heads = to_heads(cross_query, HEADS)

    def cross_forward(pieces):
        return head_forward(pieces[0], pieces[1], None)

    cross_out, cross_lse = lax.map(cross_forward, (cross_query_heads, cross_heads))
    cross_attended = from_heads(cross_out).astype(jnp.bfloat16)
    second_sum = (
        normed_one + jnp.dot(cross_attended, w_cout, preferred_element_type=jnp.float32) + biases[6]
    )
    normed_two = norm_rows(second_sum, gains[1], biases[7])
    normed_two_low = normed_two.astype(jnp.bfloat16)
    hidden_pre = jnp.dot(normed_two_low, w_up, preferred_element_type=jnp.float32) + b_up
    hidden = gelu_exact(hidden_pre).astype(jnp.bfloat16)
    third_sum = normed_two + jnp.dot(hidden, w_down, preferred_element_type=jnp.float32) + biases[8]
    output = norm_rows(third_sum, gains[2], biases[9])
    grad_third, grad_gain_three, grad_shift_three = norm_back(
        third_sum, gains[2], biases[9], cotangent[0, 0].astype(jnp.float32)
    )
    grad_down_in = grad_third.astype(jnp.bfloat16)
    grad_w_down = dot_first(hidden, grad_down_in)
    grad_b_down = jnp.sum(grad_down_in.astype(jnp.float32), axis=0)
    grad_hidden = dot_last(grad_down_in, w_down)
    _, gelu_pull = jax.vjp(gelu_exact, hidden_pre)
    grad_pre = gelu_pull(grad_hidden)[0].astype(jnp.bfloat16)
    grad_w_up = dot_first(normed_two_low, grad_pre)
    grad_b_up = jnp.sum(grad_pre.astype(jnp.float32), axis=0)
    grad_normed_two = grad_third + dot_last(grad_pre, w_up)
    grad_second, grad_gain_two, grad_shift_two = norm_back(
        second_sum, gains[1], biases[7], grad_normed_two
    )
    grad_cross_in = grad_second.astype(jnp.bfloat16)
    grad_w_cout = dot_first(cross_attended, grad_cross_in)
    grad_b_co = jnp.sum(grad_cross_in.astype(jnp.float32), axis=0)
    grad_cross_heads = to_heads(dot_last(grad_cross_in, w_cout).astype(jnp.bfloat16), HEADS)

    def cross_backward(pieces):
        return head_backward(pieces[0], pieces[1], pieces[2], pieces[3], None)

    grad_cq_heads, grad_ckv_all = lax.map(
        cross_backward, (cross_query_heads, cross_heads, grad_cross_heads, cross_lse)
    )
    grad_ckv_own = lax.psum_scatter(
        grad_ckv_all.astype(jnp.bfloat16), "ctx", scatter_dimension=1, tiled=True
    )
    grad_cv = from_heads(grad_ckv_own[:, :, head_width:])
    grad_ckv = jnp.concatenate([from_heads(grad_ckv_own[:, :, :head_width]), grad_cv], axis=1)
    grad_w_ckv = dot_first(memory_own, grad_ckv)
    grad_b_cv = jnp.sum(grad_cv.astype(jnp.float32), axis=0)
    grad_memory = dot_last(grad_ckv, w_ckv)
    grad_cq = from_heads(grad_cq_heads).astype(jnp.bfloat16)
    grad_w_cq = dot_first(normed_low, grad_cq)
    grad_b_cq = jnp.sum(grad_cq.astype(jnp.float32), axis=0)
    grad_normed_one = grad_second + dot_last(grad_cq, w_cq)
    grad_first, grad_gain_one, grad_shift_one = norm_back(
        first_sum, gains[0], biases[3], grad_normed_one
    )
    grad_att_in = grad_first.astype(jnp.bfloat16)
    grad_w_out = dot_first(attended, grad_att_in)
    grad_b_o = jnp.sum(grad_att_in.astype(jnp.float32), axis=0)
    grad_self_heads = to_heads(dot_last(grad_att_in, w_out).astype(jnp.bfloat16), HEADS)

    def self_backward(pieces):
        return head_backward(pieces[0], pieces[1], pieces[2], pieces[3], allowed)

    grad_q_heads, grad_kv_all = lax.map(
        self_backward, (query_heads, keyval_all, grad_self_heads, self_lse)
    )
    grad_kv_own = lax.psum_scatter(
        grad_kv_all.astype(jnp.bfloat16), "ctx", scatter_dimension=1, tiled=True
    )
    grad_values = from_heads(grad_kv_own[:, :, head_width:])
    grad_queries = from_heads(grad_q_heads).astype(jnp.bfloat16)
    grad_proj = jnp.concatenate(
        [grad_queries, from_heads(grad_kv_own[:, :, :head_width]), grad_values], axis=1
    )
    grad_w_qkv = dot_first(tokens, grad_proj)
    grad_b_q = jnp.sum(grad_queries.astype(jnp.float32), axis=0)
    grad_b_v = jnp.sum(grad_values.astype(jnp.float32), axis=0)
    grad_tokens = grad_first + dot_last(grad_proj, w_qkv)
    gain_grads = jnp.stack([grad_gain_one, grad_gain_two, grad_gain_three])
    shift_grads = jnp.stack(
        [
            grad_b_q,
            grad_b_v,
            grad_b_o,
            grad_shift_one,
            grad_b_cq,
            grad_b_cv,
            grad_b_co,
            grad_shift_two,
            grad_b_down,
            grad_shift_three,
        ]
    )
    (
        part_qkv,
        part_out,
        part_cq,
        part_ckv,
        part_cout,
        part_up,
        part_down,
        part_b_up,
        part_gains,
        part_biases,
    ) = (
        lax.psum_scatter(grad_w_qkv, ("ctx", "wsh"), scatter_dimension=0, tiled=True),
        lax.psum_scatter(grad_w_out, ("ctx", "wsh"), scatter_dimension=0, tiled=True),
        lax.psum_scatter(grad_w_cq, ("ctx", "wsh"), scatter_dimension=0, tiled=True),
        lax.psum_scatter(grad_w_ckv, ("ctx", "wsh"), scatter_dimension=0, tiled=True),
        lax.psum_scatter(grad_w_cout, ("ctx", "wsh"), scatter_dimension=0, tiled=True),
        lax.psum_scatter(grad_w_up, ("ctx", "wsh"), scatter_dimension=0, tiled=True),
        lax.psum_scatter(grad_w_down, ("ctx", "wsh"), scatter_dimension=0, tiled=True),
        lax.psum_scatter(grad_b_up, ("ctx", "wsh"), scatter_dimension=0, tiled=True),
        lax.psum_scatter(gain_grads, ("ctx", "wsh"), scatter_dimension=1, tiled=True),
        lax.psum_scatter(shift_grads, ("ctx", "wsh"), scatter_dimension=1, tiled=True),
    )
    (
        total_qkv,
        total_out,
        total_cq,
        total_ckv,
        total_cout,
        total_up,
        total_down,
        total_b_up,
        total_gains,
        total_biases,
    ) = (
        lax.psum(part_qkv.astype(jnp.bfloat16), "grp").astype(jnp.float32),
        lax.psum(part_out.astype(jnp.bfloat16), "grp").astype(jnp.float32),
        lax.psum(part_cq.astype(jnp.bfloat16), "grp").astype(jnp.float32),
        lax.psum(part_ckv.astype(jnp.bfloat16), "grp").astype(jnp.float32),
        lax.psum(part_cout.astype(jnp.bfloat16), "grp").astype(jnp.float32),
        lax.psum(part_up.astype(jnp.bfloat16), "grp").astype(jnp.float32),
        lax.psum(part_down.astype(jnp.bfloat16), "grp").astype(jnp.float32),
        lax.psum(part_b_up.astype(jnp.bfloat16), "grp").astype(jnp.float32),
        lax.psum(part_gains.astype(jnp.bfloat16), "grp").astype(jnp.float32),
        lax.psum(part_biases.astype(jnp.bfloat16), "grp").astype(jnp.float32),
    )
    return (
        output[None, None],
        grad_tokens[None, None],
        grad_memory[None, None],
        total_qkv,
        total_out,
        total_cq,
        total_ckv,
        total_cout,
        total_up,
        total_down,
        total_b_up,
        total_gains,
        total_biases,
    )


def fast_shards(
    stream,
    memory,
    cotangent,
    deal_order,
    offsets,
    context_mask,
    w_qkv,
    w_out,
    w_cq,
    w_ckv,
    w_cout,
    w_up,
    w_down,
    b_up,
    gains,
    biases,
):
    tokens = stream[0, 0]
    row_count, model_width = tokens.shape
    head_width = model_width // HEADS
    deal_ids = deal_order[0, 0]
    prompt_blocks = context_mask.shape[3]
    own_blocks = row_count // BLK
    total_blocks = deal_ids.shape[0]
    inverse = jnp.argsort(deal_ids).astype(jnp.int32)
    blocks_open = (context_mask[0, 0] > 0) | (jnp.arange(prompt_blocks)[None, :] == 0)
    limits = jnp.where(blocks_open, offsets[0, 0, 0], 0).astype(jnp.int32)
    zeros_row = jnp.zeros((model_width,), jnp.float32)
    projected = (
        jnp.dot(tokens, w_qkv, preferred_element_type=jnp.float32)
        + jnp.concatenate([biases[0], zeros_row, biases[1]])
    ).astype(jnp.bfloat16)
    scaled = jnp.concatenate(
        [projected[:, :model_width] * jnp.bfloat16(head_width**-0.5), projected[:, model_width:]],
        axis=1,
    )
    outgoing = (
        scaled.reshape(own_blocks, BLK, 3, HEADS, head_width)
        .transpose(3, 0, 2, 4, 1)
        .reshape(HEADS, own_blocks, 3 * head_width, BLK)
    )
    land = exchange(outgoing, 0).reshape(total_blocks, 3 * head_width, BLK)
    mixed, *kept = self_forward_call(inverse, deal_ids, limits, land, prompt_blocks)
    mixed = exchange(mixed.reshape(HEADS, own_blocks, head_width, BLK), 1)
    attended = mixed.transpose(1, 3, 0, 2).reshape(row_count, model_width)
    first_sum = (
        tokens.astype(jnp.float32)
        + jnp.dot(attended, w_out, preferred_element_type=jnp.float32)
        + biases[2]
    )
    normed_one = norm_rows(first_sum, gains[0], biases[3])
    normed_low = normed_one.astype(jnp.bfloat16)
    cross_query = (
        jnp.dot(normed_low, w_cq, preferred_element_type=jnp.float32) + biases[4]
    ).astype(jnp.bfloat16)
    cross_bias = jnp.concatenate([zeros_row, biases[5]])
    memory_own = memory[0, 0]
    memory_all = lax.all_gather(memory_own, "ctx", axis=0, tiled=True)
    cross_kv = (jnp.dot(memory_all, w_ckv, preferred_element_type=jnp.float32) + cross_bias).astype(
        jnp.bfloat16
    )
    cross_heads = pair_heads(cross_kv[:, :model_width], cross_kv[:, model_width:], HEADS)
    cross_query_heads = to_heads(cross_query, HEADS)

    def cross_forward(pieces):
        return head_forward(pieces[0], pieces[1], None)

    cross_out, cross_lse = lax.map(cross_forward, (cross_query_heads, cross_heads))
    cross_attended = from_heads(cross_out).astype(jnp.bfloat16)
    second_sum = (
        normed_one + jnp.dot(cross_attended, w_cout, preferred_element_type=jnp.float32) + biases[6]
    )
    normed_two = norm_rows(second_sum, gains[1], biases[7])
    normed_two_low = normed_two.astype(jnp.bfloat16)
    hidden_pre = jnp.dot(normed_two_low, w_up, preferred_element_type=jnp.float32) + b_up
    hidden = gelu_exact(hidden_pre).astype(jnp.bfloat16)
    third_sum = normed_two + jnp.dot(hidden, w_down, preferred_element_type=jnp.float32) + biases[8]
    output = norm_rows(third_sum, gains[2], biases[9])
    grad_third, grad_gain_three, grad_shift_three = norm_back(
        third_sum, gains[2], biases[9], cotangent[0, 0].astype(jnp.float32)
    )
    grad_down_in = grad_third.astype(jnp.bfloat16)
    grad_w_down = dot_first(hidden, grad_down_in)
    grad_b_down = jnp.sum(grad_down_in.astype(jnp.float32), axis=0)
    grad_hidden = dot_last(grad_down_in, w_down)
    _, gelu_pull = jax.vjp(gelu_exact, hidden_pre)
    grad_pre = gelu_pull(grad_hidden)[0].astype(jnp.bfloat16)
    grad_w_up = dot_first(normed_two_low, grad_pre)
    grad_b_up = jnp.sum(grad_pre.astype(jnp.float32), axis=0)
    grad_normed_two = grad_third + dot_last(grad_pre, w_up)
    grad_second, grad_gain_two, grad_shift_two = norm_back(
        second_sum, gains[1], biases[7], grad_normed_two
    )
    grad_cross_in = grad_second.astype(jnp.bfloat16)
    grad_w_cout = dot_first(cross_attended, grad_cross_in)
    grad_b_co = jnp.sum(grad_cross_in.astype(jnp.float32), axis=0)
    grad_cross_heads = to_heads(dot_last(grad_cross_in, w_cout).astype(jnp.bfloat16), HEADS)

    def cross_backward(pieces):
        return head_backward(pieces[0], pieces[1], pieces[2], pieces[3], None)

    grad_cq_heads, grad_ckv_all = lax.map(
        cross_backward, (cross_query_heads, cross_heads, grad_cross_heads, cross_lse)
    )
    grad_ckv_own = lax.psum_scatter(
        grad_ckv_all.astype(jnp.bfloat16), "ctx", scatter_dimension=1, tiled=True
    )
    grad_cv = from_heads(grad_ckv_own[:, :, head_width:])
    grad_ckv = jnp.concatenate([from_heads(grad_ckv_own[:, :, :head_width]), grad_cv], axis=1)
    grad_w_ckv = dot_first(memory_own, grad_ckv)
    grad_b_cv = jnp.sum(grad_cv.astype(jnp.float32), axis=0)
    grad_memory = dot_last(grad_ckv, w_ckv)
    grad_cq = from_heads(grad_cq_heads).astype(jnp.bfloat16)
    grad_w_cq = dot_first(normed_low, grad_cq)
    grad_b_cq = jnp.sum(grad_cq.astype(jnp.float32), axis=0)
    grad_normed_one = grad_second + dot_last(grad_cq, w_cq)
    grad_first, grad_gain_one, grad_shift_one = norm_back(
        first_sum, gains[0], biases[3], grad_normed_one
    )
    grad_att_in = grad_first.astype(jnp.bfloat16)
    grad_w_out = dot_first(attended, grad_att_in)
    grad_b_o = jnp.sum(grad_att_in.astype(jnp.float32), axis=0)
    grad_self = dot_last(grad_att_in, w_out).astype(jnp.bfloat16)
    grad_self = (
        grad_self.reshape(own_blocks, BLK, HEADS, head_width).transpose(2, 0, 3, 1)
    )
    grad_land = exchange(grad_self, 2).reshape(total_blocks, head_width, BLK)
    grad_heads = self_backward_call(inverse, deal_ids, limits, grad_land, kept, prompt_blocks)
    grad_heads = exchange(grad_heads.reshape(HEADS, own_blocks, 3 * head_width, BLK), 3)
    grad_proj = (
        grad_heads.reshape(HEADS, own_blocks, 3, head_width, BLK)
        .transpose(1, 4, 2, 0, 3)
        .reshape(row_count, 3 * model_width)
    )
    grad_queries = grad_proj[:, :model_width]
    grad_values = grad_proj[:, 2 * model_width :]
    grad_w_qkv = dot_first(tokens, grad_proj)
    grad_b_q = jnp.sum(grad_queries.astype(jnp.float32), axis=0)
    grad_b_v = jnp.sum(grad_values.astype(jnp.float32), axis=0)
    grad_tokens = grad_first + dot_last(grad_proj, w_qkv)
    gain_grads = jnp.stack([grad_gain_one, grad_gain_two, grad_gain_three])
    shift_grads = jnp.stack(
        [
            grad_b_q,
            grad_b_v,
            grad_b_o,
            grad_shift_one,
            grad_b_cq,
            grad_b_cv,
            grad_b_co,
            grad_shift_two,
            grad_b_down,
            grad_shift_three,
        ]
    )
    grads = [
        grad_w_qkv, grad_w_out, grad_w_cq, grad_w_ckv, grad_w_cout, grad_w_up, grad_w_down
    ]
    few = jnp.concatenate([grad_b_up.reshape(4, model_width), gain_grads, shift_grads], axis=0)
    few = jnp.pad(few, ((0, 24 - few.shape[0]), (0, 0)))
    total, few = reduce_weights(pack_weights(grads), few, 4)
    (
        total_qkv, total_out, total_cq, total_ckv, total_cout, total_up, total_down
    ) = unpack_weights(total, [g.shape[1] for g in grads[:-1]])
    own = lax.axis_index("ctx") * 2 + lax.axis_index("wsh")
    total_b_up = lax.dynamic_slice_in_dim(few[:4].reshape(-1), own * 128, 128)
    total_gains = lax.dynamic_slice_in_dim(few[4:7], own * 32, 32, axis=1)
    total_biases = lax.dynamic_slice_in_dim(few[7:17], own * 32, 32, axis=1)
    return (
        output[None, None],
        grad_tokens[None, None],
        grad_memory[None, None],
        total_qkv,
        total_out,
        total_cq,
        total_ckv,
        total_cout,
        total_up,
        total_down,
        total_b_up,
        total_gains,
        total_biases,
    )


def solution(mesh):
    in_specs = (
        P("grp", "wsh", "ctx", None),
        P("grp", "wsh", "ctx", None),
        P("grp", "wsh", "ctx", None),
        P("grp", "wsh", None),
        P("grp", "wsh", None),
        P("grp", "wsh", None, None),
        P(),
        P(),
        P(),
        P(),
        P(),
        P(),
        P(),
        P(),
        P(),
        P(),
    )
    out_specs = (
        P("grp", "wsh", "ctx", None),
        P("grp", "wsh", "ctx", None),
        P("grp", "wsh", "ctx", None),
        P(("ctx", "wsh"), None),
        P(("ctx", "wsh"), None),
        P(("ctx", "wsh"), None),
        P(("ctx", "wsh"), None),
        P(("ctx", "wsh"), None),
        P(("ctx", "wsh"), None),
        P(("ctx", "wsh"), None),
        P(("ctx", "wsh")),
        P(None, ("ctx", "wsh")),
        P(None, ("ctx", "wsh")),
    )
    body = fast_shards if mesh.shape["ctx"] == HEADS else shards
    return jax.shard_map(body, mesh=mesh, in_specs=in_specs, out_specs=out_specs, check_vma=False)
```

```python
import jax
import jax.numpy as jnp
from jax import lax
from jax.experimental import pallas as pl
from jax.experimental.pallas import tpu as pltpu
from jax.sharding import PartitionSpec as P

HEADS = 8
BLK = 128
CBLK = 16


NEG_FILL = -1000000000.0
EPS_NORM = 1e-05


MESH_ID = pl.DeviceIdType.MESH
TILE = 512
STEP = 256
BIG_VMEM = 62 << 20
LOW = jnp.bfloat16
WIDE = jnp.float32
SHARDS = 16
HALF = 16
ROWS = 4
PIECES = dict(
    up0=1024, up1=1024, down0=1024, down1=1024, cross=1024, out=512, ckv=1024, qkv0=768, qkv1=768
)
TURNS = dict(up0=0, up1=1, down0=0, down1=1, cross=0, out=1, ckv=1, qkv0=0, qkv1=1)
FEW_ROWS = 24


def nn(left, right):
    return lax.dot_general(
        left, right, (((1,), (0,)), ((), ())), preferred_element_type=WIDE
    )


def nt(left, right):
    return lax.dot_general(
        left, right, (((1,), (1,)), ((), ())), preferred_element_type=WIDE
    )


def swap(block):
    return block.astype(WIDE).T.astype(block.dtype)


def plus(left, right):
    return left.astype(WIDE) + right.astype(WIDE)


def column_sums(values):
    return jnp.sum(values.astype(WIDE), axis=0, keepdims=True)


def norm_parts(values):
    center = values - jnp.mean(values, axis=-1, keepdims=True)
    spread = jnp.mean(center * center, axis=-1, keepdims=True)
    scale = lax.rsqrt(spread + EPS_NORM)
    return center * scale, scale


def norm_pull(unit, scale, gain, upstream):
    inner = upstream * gain
    first = jnp.mean(inner, axis=-1, keepdims=True)
    second = jnp.mean(inner * unit, axis=-1, keepdims=True)
    return scale * (inner - first - unit * second)


def hide_later(scores):
    rows = lax.broadcasted_iota(jnp.int32, scores.shape, 0)
    cols = lax.broadcasted_iota(jnp.int32, scores.shape, 1)
    return jnp.where(rows <= cols, scores, NEG_FILL)


def hide_prompt(scores, lim_ref, tile, chunk, prompt_blocks):
    span = TILE // BLK
    rows = lax.broadcasted_iota(jnp.int32, (BLK, BLK), 0)
    columns = []
    for q_sub in range(span):
        pieces = []
        for k_sub in range(span):
            key_block = chunk * span + k_sub
            limit = lim_ref[tile * span + q_sub - prompt_blocks, key_block] - key_block * BLK
            part = scores[k_sub * BLK : (k_sub + 1) * BLK, q_sub * BLK : (q_sub + 1) * BLK]
            pieces.append(jnp.where(rows < limit, part, NEG_FILL))
        columns.append(jnp.concatenate(pieces, axis=0))
    return jnp.concatenate(columns, axis=1)


def apart(upper, lower):
    none = jnp.zeros_like(upper)
    return jnp.concatenate(
        [jnp.concatenate([upper, none], axis=1), jnp.concatenate([none, lower], axis=1)], axis=0
    )


def apart_columns(pair):
    lanes = lax.broadcasted_iota(jnp.int32, pair.shape, 1)
    wide = pair.astype(WIDE)
    left = jnp.where(lanes < pair.shape[1] // 2, wide, 0.0).astype(pair.dtype)
    right = jnp.where(lanes < pair.shape[1] // 2, 0.0, wide).astype(pair.dtype)
    return jnp.concatenate([left, right], axis=0)


def remote(src_ref, dst_ref, send_sem, recv_sem, target):
    return pltpu.make_async_remote_copy(
        src_ref=src_ref,
        dst_ref=dst_ref,
        send_sem=send_sem,
        recv_sem=recv_sem,
        device_id=target,
        device_id_type=MESH_ID,
    )


class Bag:
    def __init__(self, items):
        self.__dict__.update(items)


class Spot:
    def __init__(self):
        ctx = lax.axis_index("ctx")
        self.grp, self.ctx, self.wsh = lax.axis_index("grp"), ctx, lax.axis_index("wsh")
        self.row, self.col = ctx // 2, lax.rem(ctx, 2)
        self.core_peer = (1 - self.grp, ctx, self.wsh)
        self.wsh_peer = (self.grp, ctx, 1 - self.wsh)
        self.col_peer = self.at_row_col(self.row, 1 - self.col)
        self.rows_by_step = [lax.rem(self.row + step, ROWS) for step in range(ROWS)]
        self.row_peers = [self.at_row_col(row, self.col) for row in self.rows_by_step]
        near = self.row + 1 - 2 * lax.rem(self.row, 2)
        self.few_peers = [
            self.core_peer, self.wsh_peer, self.col_peer,
            self.at_row_col(near, self.col), self.row_peers[2],
        ]
        self.ctx_by_step = [lax.rem(ctx + step, HEADS) for step in range(HEADS)]
        self.ctx_peers = [(self.grp, peer, self.wsh) for peer in self.ctx_by_step]

    def at_row_col(self, row, col):
        return (self.grp, row * 2 + col, self.wsh)

    def greet(self):
        barrier = pltpu.get_barrier_semaphore()
        targets = [self.core_peer, self.wsh_peer] + self.ctx_peers[1:]
        for target in targets:
            pl.semaphore_signal(barrier, inc=1, device_id=target, device_id_type=MESH_ID)
        pl.semaphore_wait(barrier, len(targets))


class Exchange:
    def __init__(self, spot, source, target, sems):
        self.spot, self.source, self.target, self.sems = spot, source, target, sems
        self.copies = []

    def start(self):
        spot, own_blocks = self.spot, self.source.shape[1]
        here = pl.ds(spot.ctx * own_blocks, own_blocks)
        for step in range(1, HEADS):
            copy = remote(
                self.source.at[spot.ctx_by_step[step]], self.target.at[here],
                self.sems.at[0, step], self.sems.at[1, step], spot.ctx_peers[step],
            )
            copy.start()
            self.copies.append(copy)
        self.target[here] = self.source[spot.ctx]

    def wait(self):
        for copy in self.copies:
            copy.wait()


class Spread:
    def __init__(self, spot, source, target, sems):
        self.spot, self.source, self.target, self.sems = spot, source, target, sems
        self.copies = []

    def start(self):
        spot = self.spot
        for step in range(1, HEADS):
            copy = remote(
                self.source, self.target.at[spot.ctx],
                self.sems.at[0, step], self.sems.at[1, step], spot.ctx_peers[step],
            )
            copy.start()
            self.copies.append(copy)
        self.target[pl.ds(spot.ctx, 1)] = self.source[...][None]

    def wait(self):
        for copy in self.copies:
            copy.wait()


class Piece:
    def __init__(self, spot, turn, refs, outs):
        self.spot, self.turn, self.sems, self.outs = spot, turn, refs.sems, outs
        self.part, self.core_land, self.hop_land = refs.part, refs.core_land, refs.hop_land
        self.turn_land, self.row_land = refs.turn_land, refs.row_land
        self.turn_sum = self.core_land.at[:, 0]
        self.copies = []
        self.stage = 0

    def copy(self, index, source, target_ref, target):
        copy = remote(source, target_ref, self.sems.at[0, index], self.sems.at[1, index], target)
        copy.start()
        self.copies.append(copy)

    def finish(self):
        for copy in self.copies:
            copy.wait()
        self.copies = []

    def step(self):
        spot, part = self.spot, self.part
        own = spot.grp
        if self.stage == 0:
            self.copy(0, part.at[1 - own], self.core_land, spot.core_peer)
        elif self.stage == 1:
            self.finish()
            part[own] = plus(part[own], self.core_land[...]).astype(LOW)
            if self.turn == 0:
                self.copy(1, part.at[own, :, :, 1 - spot.wsh], self.hop_land, spot.wsh_peer)
            else:
                self.copy(1, part.at[own, :, 1 - spot.col], self.hop_land, spot.col_peer)
        elif self.stage == 2:
            self.finish()
            if self.turn == 0:
                mine = part[own, :, :, spot.wsh]
                away, target = 1 - spot.col, spot.col_peer
            else:
                mine = part[own, :, spot.col]
                away, target = 1 - spot.wsh, spot.wsh_peer
            self.turn_sum[...] = plus(mine, self.hop_land[...]).astype(LOW)
            self.copy(2, self.turn_sum.at[:, away], self.turn_land, target)
        elif self.stage == 3:
            self.finish()
            keep = spot.col if self.turn == 0 else spot.wsh
            self.turn_land[...] = plus(self.turn_sum[:, keep], self.turn_land[...]).astype(LOW)
            for step in range(1, ROWS):
                self.copy(
                    2 + step, self.turn_land.at[spot.rows_by_step[step]],
                    self.row_land.at[step - 1], spot.row_peers[step],
                )
        elif self.stage == 4:
            self.finish()
            total = self.turn_land[spot.row].astype(WIDE)
            for step in range(ROWS - 1):
                total = total + self.row_land[step].astype(WIDE)
            at = 0
            for index, (out_ref, row, column, width) in enumerate(self.outs):
                here = (
                    pl.ds(pl.multiple_of(row + own * HALF, HALF), HALF),
                    slice(column, column + width),
                )
                out_ref[here] = total[:, at : at + width]
                at += width
                self.copy(6 + index, out_ref.at[here], out_ref.at[here], spot.core_peer)
        elif self.stage == 5:
            self.finish()
        self.stage += 1


def layer_kernel(
    prompt_blocks,
    inv_ref, deal_ref, lim_ref, tokens_ref, memory_ref, cot_ref,
    w_qkv_hbm, w_out_hbm, w_cq_hbm, w_ckv_hbm, w_cout_hbm, w_up_hbm, w_down_hbm,
    b_up_ref, gains_ref, biases_ref,
    output_ref, g_stream_ref, g_memory_ref, o_qkv_ref, o_out_ref, o_cq_ref, o_ckv_ref, o_cout_ref,
    o_up_ref, o_down_ref, few_out_ref,
    refs,
):
    spot = Spot()
    row_count, width = tokens_ref.shape
    own_blocks = row_count // BLK
    head = width // HEADS
    blocks = own_blocks * HEADS
    mem_rows = memory_ref.shape[0]
    mem_total = mem_rows * HEADS
    hidden_width = b_up_ref.shape[1]
    chunks = hidden_width // width
    pairs = HEADS // 2
    score_scale = head ** (-0.5)
    prompt_tiles = prompt_blocks * BLK // TILE
    tiles = blocks * BLK // TILE

    sources = dict(
        w_qkv=w_qkv_hbm, w_ckv=w_ckv_hbm, w_out=w_out_hbm, w_cq=w_cq_hbm, w_cout=w_cout_hbm,
        w_up=w_up_hbm, w_down=w_down_hbm,
    )
    loads = Bag(
        {
            name: pltpu.make_async_copy(source, getattr(refs, name), refs.load_sem.at[index])
            for index, (name, source) in enumerate(sources.items())
        }
    )
    for name in sources:
        getattr(loads, name).start()

    outs = dict(
        up0=[(o_up_ref, 0, 0, 1024)],
        up1=[(o_up_ref, 0, 1024, 1024)],
        down0=[(o_down_ref, 0, 0, 512), (o_down_ref, 32, 0, 512)],
        down1=[(o_down_ref, 64, 0, 512), (o_down_ref, 96, 0, 512)],
        cross=[(o_cout_ref, 0, 0, 512), (o_cq_ref, 0, 0, 512)],
        out=[(o_out_ref, 0, 0, 512)],
        ckv=[(o_ckv_ref, 0, 0, 1024)],
        qkv0=[(o_qkv_ref, 0, 0, 768)],
        qkv1=[(o_qkv_ref, 0, 768, 768)],
    )
    piece = Bag(
        {
            name: Piece(spot, TURNS[name], Bag(refs.pieces[name]), outs[name])
            for name in PIECES
        }
    )
    ups, downs = (piece.up0, piece.up1), (piece.down0, piece.down1)

    def put_rows(to, values, column):
        span = values.shape[1]
        split = values.astype(LOW).reshape(ROWS, 2, 2, 2, HALF, span)
        for half in range(2):
            to.part[half, :, :, :, :, column : column + span] = split[:, :, :, half]

    few_ref = refs.few_sum
    few_ref[0] = jnp.zeros_like(few_ref[0])

    def few(row, values):
        few_ref[0, row : row + 1, :] = values

    def gain(row):
        return gains_ref[row : row + 1, :]

    def bias(row):
        return biases_ref[row : row + 1, :]

    send_ref = refs.head_send
    loads.w_qkv.wait()
    zeros_row = jnp.zeros((1, width), WIDE)
    projected_bias = jnp.concatenate([bias(0), zeros_row, bias(1)], axis=1)
    for block in range(own_blocks):
        rows = slice(block * BLK, (block + 1) * BLK)
        projected = (nn(tokens_ref[rows, :], refs.w_qkv[...]) + projected_bias).astype(LOW)
        turned = projected.astype(WIDE).T
        turned = jnp.concatenate([turned[:width] * score_scale, turned[width:]], axis=0).astype(LOW)
        for h in range(HEADS):
            for kind in range(3):
                at = kind * width + h * head
                send_ref[h, block, kind * head : (kind + 1) * head, :] = turned[at : at + head]
    spot.greet()
    to_heads_copy = Exchange(spot, send_ref, refs.head_land, refs.to_heads_sem)
    to_heads_copy.start()
    to_heads_copy.wait()
    spread = Spread(spot, memory_ref, refs.memory_all, refs.spread_sem)
    spread.start()

    q_ref, kv_ref = refs.q, refs.kv
    no_head = jnp.zeros((head, BLK), LOW)
    no_tile = jnp.zeros((head, TILE), LOW)
    qt_ref, kt_ref, vt_ref = refs.qt, refs.kt, refs.vt
    exact_ref, lse_ref = refs.exact, refs.lse
    for pos in range(blocks):
        block = refs.head_land[inv_ref[pos]]
        at = slice(pos * BLK, (pos + 1) * BLK)
        qt_ref[:, at] = block[:head]
        kt_ref[:, at] = block[head : 2 * head]
        vt_ref[:, at] = block[2 * head :]
        q_ref[at, :] = swap(jnp.concatenate([block[:head], no_head], axis=0))
        kv_ref[at, :] = swap(block[head:])

    def tile_spans(tile, chunk_step, state):
        state = chunk_step(tile, state, lambda s, c: hide_later(s))
        first = jnp.where(tile >= prompt_tiles, prompt_tiles, 0)
        state = lax.fori_loop(first, tile, lambda c, s: chunk_step(c, s, lambda x, _: x), state)
        return lax.fori_loop(
            0,
            first,
            lambda c, s: chunk_step(
                c, s, lambda x, cc: hide_prompt(x, lim_ref, tile, cc, prompt_blocks)
            ),
            state,
        )

    def forward_tile(tile, carry):
        here = pl.ds(pl.multiple_of(tile * TILE, TILE), TILE)
        queries = jnp.concatenate([qt_ref[:, here], no_tile], axis=0)

        def chunk_step(chunk, state, hide):
            top, total, mixed = state
            there = pl.ds(pl.multiple_of(chunk * TILE, TILE), TILE)
            scores = hide(nn(kv_ref[there, :], queries), chunk)
            new_top = jnp.maximum(top, jnp.max(scores, axis=0, keepdims=True))
            weights = jnp.exp(scores - new_top)
            fade = jnp.exp(top - new_top)
            total = total * fade + jnp.sum(weights, axis=0, keepdims=True)
            mixed = mixed * fade + nn(vt_ref[:, there], weights.astype(LOW))
            return new_top, total, mixed

        top, total, mixed = tile_spans(
            tile,
            chunk_step,
            (
                jnp.full((1, TILE), NEG_FILL, WIDE),
                jnp.zeros((1, TILE), WIDE),
                jnp.zeros((head, TILE), WIDE),
            ),
        )
        exact = mixed / total
        for sub in range(TILE // BLK):
            exact_ref[tile * (TILE // BLK) + sub] = exact[:, sub * BLK : (sub + 1) * BLK]
        lse_ref[:, here] = top + jnp.log(total)
        return carry

    lax.fori_loop(0, tiles, forward_tile, 0)
    mixed_ref = refs.mixed_send
    for row in range(blocks):
        mixed_ref[row // own_blocks, row % own_blocks] = exact_ref[deal_ref[row]].astype(LOW)
    from_heads_copy = Exchange(spot, mixed_ref, refs.mixed_land, refs.from_heads_sem)
    from_heads_copy.start()

    ck_ref, cv_ref, ckt_ref, cvt_ref = refs.ck, refs.cv, refs.ckt, refs.cvt
    loads.w_ckv.wait()
    spread.wait()
    for part in range(HEADS):
        rows = slice(part * mem_rows, (part + 1) * mem_rows)
        both = nn(refs.memory_all[part], refs.w_ckv[...])
        keys = both[:, :width].astype(LOW)
        values = (both[:, width:] + bias(5)).astype(LOW)
        ck_ref[rows, :] = keys
        cv_ref[rows, :] = values
        ckt_ref[:, rows] = swap(keys)
        cvt_ref[:, rows] = swap(values)

    loads.w_out.wait()
    from_heads_copy.wait()
    attended_t_ref = refs.attended_t
    unit_one_ref, unit_two_ref = refs.unit_one, refs.unit_two
    low_one_ref, low_two_ref = refs.low_one, refs.low_two
    for block in range(own_blocks):
        at = slice(block * BLK, (block + 1) * BLK)
        for h in range(HEADS):
            attended_t_ref[h * head : (h + 1) * head, at] = refs.mixed_land[h * own_blocks + block]
    cq_ref, cqt_ref = refs.cq, refs.cqt
    loads.w_cq.wait()

    def rows_at(block):
        return pl.ds(pl.multiple_of(block * BLK, BLK), BLK)

    def first_norm(block, carry):
        rows = rows_at(block)
        attended = swap(attended_t_ref[:, rows])
        first_sum = tokens_ref[rows, :].astype(WIDE) + nn(attended, refs.w_out[...]) + bias(2)
        unit, scale = norm_parts(first_sum)
        unit_one_ref[rows, :] = unit
        refs.scale_one[rows, :] = scale
        low_one = (unit * gain(0) + bias(3)).astype(LOW)
        low_one_ref[rows, :] = low_one
        cross_query = (nn(low_one, refs.w_cq[...]) + bias(4)).astype(LOW).astype(WIDE)
        cross_query = cross_query * score_scale
        cq_ref[rows, :] = cross_query.astype(LOW)
        cqt_ref[:, rows] = cross_query.T.astype(LOW)
        return carry

    lax.fori_loop(0, own_blocks, first_norm, 0)

    pair_width = 2 * head
    scores_ref, weights_ref = refs.scores, refs.weights
    cross_exact_ref, cross_lse_ref = refs.cross_exact, refs.cross_lse
    steps = mem_total // STEP

    def pair_at(pair):
        return pl.ds(pl.multiple_of(pair * pair_width, pair_width), pair_width)

    def step_at(step):
        return pl.ds(pl.multiple_of(step * STEP, STEP), STEP)

    def cross_forward(pair, carry):
        lanes = pair_at(pair)
        for side in range(2):
            at = pl.ds(pl.multiple_of(pair * pair_width + side * head, head), head)
            queries = cqt_ref[at, :]
            none = jnp.zeros_like(queries)
            queries = jnp.concatenate([none, queries] if side else [queries, none], axis=0)

            def first_pass(step, top):
                scores = nn(ck_ref[step_at(step), lanes], queries)
                scores_ref[step_at(step), :] = scores
                return jnp.maximum(top, jnp.max(scores, axis=0, keepdims=True))

            top = lax.fori_loop(
                0, steps, first_pass, jnp.full((1, row_count), NEG_FILL, WIDE), unroll=True
            )

            def second_pass(step, total):
                weights = jnp.exp(scores_ref[step_at(step), :] - top)
                weights_ref[step_at(step), :] = weights.astype(LOW)
                return total + jnp.sum(weights, axis=0, keepdims=True)

            total = lax.fori_loop(
                0, steps, second_pass, jnp.zeros((1, row_count), WIDE), unroll=True
            )
            across = slice(side * row_count, (side + 1) * row_count)
            cross_lse_ref[pl.ds(pair, 1), across] = top + jnp.log(total)
            cross_exact_ref[at, :] = nn(cvt_ref[at, :], weights_ref[...]) / total
        return carry

    lax.fori_loop(0, pairs, cross_forward, 0)
    cross_low_ref = refs.cross_low
    total_ref, hidden_ref, slope_ref = g_stream_ref, refs.hidden, refs.slope
    loads.w_cout.wait()

    def second_norm(block, carry):
        rows = rows_at(block)
        cross_low = cross_exact_ref[:, rows].T.astype(LOW)
        cross_low_ref[rows, :] = cross_low
        normed_one = unit_one_ref[rows, :] * gain(0) + bias(3)
        unit, scale = norm_parts(normed_one + nn(cross_low, refs.w_cout[...]) + bias(6))
        unit_two_ref[rows, :] = unit
        refs.scale_two[rows, :] = scale
        normed_two = unit * gain(1) + bias(7)
        low_two_ref[rows, :] = normed_two.astype(LOW)
        total_ref[rows, :] = normed_two + bias(8)
        return carry

    lax.fori_loop(0, own_blocks, second_norm, 0)

    loads.w_up.wait()
    loads.w_down.wait()
    w_up_ref, w_down_ref = refs.w_up, refs.w_down

    def chunk_at(chunk):
        return pl.ds(pl.multiple_of(chunk * width, width), width)

    def up_step(chunk, carry):
        pre = nn(low_two_ref[...], w_up_ref[:, chunk_at(chunk)]) + b_up_ref[:, chunk_at(chunk)]
        normal = 0.5 + 0.5 * lax.erf(pre * (2.0**-0.5))
        hidden = (pre * normal).astype(LOW)
        hidden_ref[chunk] = hidden
        slope = normal + pre * jnp.exp(-0.5 * pre * pre) * ((2.0 * jnp.pi) ** -0.5)
        slope_ref[chunk] = slope.astype(LOW)
        total_ref[...] += nn(hidden, w_down_ref[chunk_at(chunk), :])
        return carry

    lax.fori_loop(0, chunks, up_step, 0)

    low_third_ref = refs.low_third
    no_sums = (zeros_row, zeros_row, zeros_row)

    def third_norm(block, sums):
        rows = rows_at(block)
        unit, scale = norm_parts(total_ref[rows, :])
        output_ref[rows, :] = unit * gain(2) + bias(9)
        upstream = cot_ref[rows, :].astype(WIDE)
        grad = norm_pull(unit, scale, gain(2), upstream)
        low = grad.astype(LOW)
        low_third_ref[rows, :] = low
        total_ref[rows, :] = grad
        return (
            sums[0] + column_sums(upstream * unit),
            sums[1] + column_sums(upstream),
            sums[2] + column_sums(low),
        )

    sums = lax.fori_loop(0, own_blocks, third_norm, no_sums)
    few(6, sums[0])
    few(16, sums[1])
    few(15, sums[2])

    turned_ref = refs.turned
    turned_ref[...] = swap(low_two_ref[...])
    for chunk in range(chunks):
        rows = slice(chunk * width, (chunk + 1) * width)
        grad_hidden = nt(low_third_ref[...], w_down_ref[rows, :])
        grad_pre = (grad_hidden * slope_ref[chunk].astype(WIDE)).astype(LOW)
        few(chunk, column_sums(grad_pre))
        total_ref[...] += nt(grad_pre, w_up_ref[:, rows])
        grad_up = nn(turned_ref[...], grad_pre)
        put_rows(ups[chunk // 2], grad_up, (chunk % 2) * width)
        if chunk % 2 == 1:
            ups[chunk // 2].step()
        grad_down = nn(swap(hidden_ref[chunk]), low_third_ref[...])
        split = grad_down.astype(LOW).reshape(2, 2, 4, 2, HALF, width)
        for part in range(4):
            to = downs[part // 2].part
            column = (part % 2) * width
            for half in range(2):
                to[half, chunk, :, :, :, column : column + width] = split[:, :, part, half]
    piece.down0.step()
    piece.down1.step()

    dco_ref, dcot_ref = refs.dco, refs.dcot

    def second_back(block, sums):
        rows = rows_at(block)
        upstream = total_ref[rows, :]
        unit = unit_two_ref[rows, :]
        grad = norm_pull(unit, refs.scale_two[rows, :], gain(1), upstream)
        low = grad.astype(LOW)
        total_ref[rows, :] = grad
        low_third_ref[rows, :] = low
        dco_ref[rows, :] = nt(low, refs.w_cout[...]).astype(LOW)
        dcot_ref[:, rows] = nt(refs.w_cout[...], low).astype(LOW)
        return (
            sums[0] + column_sums(upstream * unit),
            sums[1] + column_sums(upstream),
            sums[2] + column_sums(low),
        )

    sums = lax.fori_loop(0, own_blocks, second_back, no_sums)
    few(5, sums[0])
    few(14, sums[1])
    few(13, sums[2])
    put_rows(piece.cross, nn(swap(cross_low_ref[...]), low_third_ref[...]), 0)
    piece.up0.step()
    piece.up1.step()

    dcqt_ref, dsend_ref, dland_ref = refs.dcqt, w_up_ref, refs.dkv_land
    side_width = ROWS * 2 * pair_width
    dkv_copies = []
    for pair in range(pairs):
        lanes = slice(pair * pair_width, (pair + 1) * pair_width)
        low_half = slice(pair * pair_width, pair * pair_width + head)
        high_half = slice(pair * pair_width + head, (pair + 1) * pair_width)
        queries_t = apart(cqt_ref[low_half, :], cqt_ref[high_half, :])
        upstream_t = apart(dcot_ref[low_half, :], dcot_ref[high_half, :])
        queries = apart_columns(cq_ref[:, lanes])
        upstream = apart_columns(dco_ref[:, lanes])
        dots = cross_exact_ref[lanes, :] * dcot_ref[lanes, :].astype(WIDE)
        delta = jnp.concatenate(
            [column_sums(dots[:head]), column_sums(dots[head:])], axis=1
        )
        lse = cross_lse_ref[pair : pair + 1, :]
        dcqt_ref[lanes, :] = jnp.zeros((pair_width, row_count), WIDE)

        def backward_step(step, carry):
            there = step_at(step)
            weights = jnp.exp(nn(ck_ref[there, lanes], queries_t) - lse)
            grad_weights = nn(cv_ref[there, lanes], upstream_t)
            grad_scores = (weights * (grad_weights - delta)).astype(LOW)
            grad_keys = nn(grad_scores, queries).astype(LOW)
            grad_values = nn(weights.astype(LOW), upstream).astype(LOW)
            for sub in range(STEP // mem_rows):
                rows = slice(sub * mem_rows, (sub + 1) * mem_rows)
                at = sub * side_width + step * 2 * pair_width
                at = pl.ds(pl.multiple_of(at, pair_width), 2 * pair_width)
                dsend_ref[pair * mem_rows : (pair + 1) * mem_rows, at] = jnp.concatenate(
                    [grad_keys[rows], grad_values[rows]], axis=1
                )
            dcqt_ref[low_half, :] += nn(ckt_ref[low_half, there], grad_scores[:, :row_count])
            dcqt_ref[high_half, :] += nn(ckt_ref[high_half, there], grad_scores[:, row_count:])
            return carry

        lax.fori_loop(0, steps, backward_step, 0)
        copy = remote(
            dsend_ref.at[
                pl.ds(pair * mem_rows, mem_rows),
                pl.ds(pl.multiple_of((1 - spot.col) * side_width, side_width), side_width),
            ],
            dland_ref.at[pair],
            refs.dkv_sem.at[0, pair], refs.dkv_sem.at[1, pair], spot.col_peer,
        )
        copy.start()
        dkv_copies.append(copy)
        (downs if pair < 2 else ups)[pair % 2].step()

    upstream_send = refs.mixed_send

    def first_back(block, sums):
        rows = rows_at(block)
        grad_cq = (dcqt_ref[:, rows].T * score_scale).astype(LOW)
        dco_ref[rows, :] = grad_cq
        upstream = total_ref[rows, :] + nt(grad_cq, refs.w_cq[...])
        unit = unit_one_ref[rows, :]
        grad = norm_pull(unit, refs.scale_one[rows, :], gain(0), upstream)
        low = grad.astype(LOW)
        total_ref[rows, :] = grad
        low_third_ref[rows, :] = low
        grad_attended_t = nt(refs.w_out[...], low).astype(LOW)
        for h in range(HEADS):
            upstream_send[h, block] = grad_attended_t[h * head : (h + 1) * head, :]
        return (
            sums[0] + column_sums(upstream * unit),
            sums[1] + column_sums(upstream),
            sums[2] + column_sums(low),
            sums[3] + column_sums(grad_cq),
        )

    sums = lax.fori_loop(0, own_blocks, first_back, no_sums + (zeros_row,))
    few(4, sums[0])
    few(10, sums[1])
    few(9, sums[2])
    few(11, sums[3])
    up_heads_copy = Exchange(spot, upstream_send, refs.up_land, refs.up_heads_sem)
    up_heads_copy.start()
    turned_ref[...] = swap(low_one_ref[...])
    put_rows(piece.cross, nn(turned_ref[...], dco_ref[...]), width)
    piece.cross.step()
    put_rows(piece.out, nn(attended_t_ref[...], low_third_ref[...]), 0)
    piece.out.step()
    piece.down0.step()
    piece.down1.step()
    piece.cross.step()
    up_heads_copy.wait()
    piece.up0.step()
    piece.up1.step()

    upq_ref, upt_ref = refs.up, refs.upt
    dkv_ref, dqt_ref = refs.dkv, refs.dqt
    for pos in range(blocks):
        block = refs.up_land[inv_ref[pos]]
        at = slice(pos * BLK, (pos + 1) * BLK)
        upt_ref[:, at] = block
        upq_ref[at, :] = swap(jnp.concatenate([no_head, block], axis=0))
    dkv_ref[...] = jnp.zeros_like(dkv_ref)

    def backward_tile(tile, carry):
        here = pl.ds(pl.multiple_of(tile * TILE, TILE), TILE)
        queries_t = jnp.concatenate([qt_ref[:, here], no_tile], axis=0)
        upstream_t = jnp.concatenate([no_tile, upt_ref[:, here]], axis=0)
        both = jnp.concatenate([q_ref[here, :], upq_ref[here, :]], axis=0)
        lse = lse_ref[:, here]
        exact = jnp.concatenate(
            [exact_ref[tile * (TILE // BLK) + sub] for sub in range(TILE // BLK)], axis=1
        )
        delta = column_sums(exact * upt_ref[:, here].astype(WIDE))

        def chunk_step(chunk, grad_q, hide):
            there = pl.ds(pl.multiple_of(chunk * TILE, TILE), TILE)
            scores = hide(nn(kv_ref[there, :], queries_t), chunk)
            weights = jnp.exp(scores - lse)
            grad_weights = nn(kv_ref[there, :], upstream_t)
            grad_scores = (weights * (grad_weights - delta)).astype(LOW)
            sides = jnp.concatenate([grad_scores, weights.astype(LOW)], axis=1)
            spread_at = pl.ds(chunk * (TILE // BLK), TILE // BLK)
            dkv_ref[spread_at] += nn(sides, both).reshape(TILE // BLK, BLK, 2 * head)
            return grad_q + nn(kt_ref[:, there], grad_scores)

        grad_q = tile_spans(tile, chunk_step, jnp.zeros((head, TILE), WIDE))
        grad_q = (grad_q * score_scale).astype(LOW)
        for sub in range(TILE // BLK):
            dqt_ref[tile * (TILE // BLK) + sub] = grad_q[:, sub * BLK : (sub + 1) * BLK]
        return carry

    lax.fori_loop(0, tiles // 2, backward_tile, 0)
    piece.out.step()
    piece.cross.step()
    piece.down0.step()
    piece.down1.step()
    dsum_ref, drow_ref = refs.dkv_sum, refs.dkv_row
    for copy in dkv_copies:
        copy.wait()
    own_side = pl.ds(pl.multiple_of(spot.col * side_width, side_width), side_width)
    for pair in range(pairs):
        own_rows = slice(pair * mem_rows, (pair + 1) * mem_rows)
        both = plus(dsend_ref[own_rows, own_side], dland_ref[pair]).astype(LOW)
        for row in range(ROWS):
            dsum_ref[row, pair] = both[:, row * 2 * pair_width : (row + 1) * 2 * pair_width]
    dkv_copies = []
    for step in range(1, ROWS):
        copy = remote(
            dsum_ref.at[spot.rows_by_step[step]], drow_ref.at[step - 1],
            refs.dkv_sem.at[0, 3 + step], refs.dkv_sem.at[1, 3 + step], spot.row_peers[step],
        )
        copy.start()
        dkv_copies.append(copy)
    lax.fori_loop(tiles // 2, tiles - 1, backward_tile, 0)
    piece.out.step()
    piece.cross.step()
    lax.fori_loop(tiles - 1, tiles, backward_tile, 0)

    back_send = refs.head_send
    for row in range(blocks):
        pos = deal_ref[row]
        to = (row // own_blocks, row % own_blocks)
        back_send[to[0], to[1], :head] = dqt_ref[pos]
        back_send[to[0], to[1], head:] = dkv_ref[pos].T.astype(LOW)
    back_copy = Exchange(spot, back_send, refs.head_land, refs.back_sem)
    back_copy.start()

    for copy in dkv_copies:
        copy.wait()
    for pair in range(pairs):
        total = dsum_ref[spot.row, pair].astype(WIDE)
        for step in range(ROWS - 1):
            total = total + drow_ref[step, pair].astype(WIDE)
        refs.dckv[:, pair * pair_width : (pair + 1) * pair_width] = total[:, :pair_width].astype(LOW)
        at = width + pair * pair_width
        refs.dckv[:, at : at + pair_width] = total[:, pair_width:].astype(LOW)
    dckv = refs.dckv[...]
    put_rows(piece.ckv, nn(swap(memory_ref[...]), dckv), 0)
    piece.ckv.step()
    few(12, column_sums(dckv[:, width:]))
    g_memory_ref[...] = nt(dckv, refs.w_ckv[...])
    piece.out.step()
    piece.cross.step()
    for item in ups + downs:
        item.step()
    piece.ckv.step()

    back_copy.wait()
    for block in range(own_blocks):
        rows = slice(block * BLK, (block + 1) * BLK)
        for kind in range(3):
            turned = jnp.concatenate(
                [
                    refs.head_land[h * own_blocks + block, kind * head : (kind + 1) * head, :]
                    for h in range(HEADS)
                ],
                axis=0,
            )
            hidden_ref[kind, rows, :] = swap(turned)
    turned_ref[...] = swap(tokens_ref[...])
    put_rows(piece.qkv0, nn(turned_ref[...], hidden_ref[0]), 0)
    grad_keys = nn(turned_ref[...], hidden_ref[1])
    put_rows(piece.qkv0, grad_keys[:, : width // 2], width)
    piece.qkv0.step()
    put_rows(piece.qkv1, grad_keys[:, width // 2 :], 0)
    put_rows(piece.qkv1, nn(turned_ref[...], hidden_ref[2]), width // 2)
    piece.qkv1.step()
    few(7, column_sums(hidden_ref[0]))
    few(8, column_sums(hidden_ref[2]))

    def few_copy(step):
        return remote(
            few_ref.at[step], refs.few_land.at[step],
            refs.few_sem.at[0, step], refs.few_sem.at[1, step], spot.few_peers[step],
        )

    few_copy(0).start()
    piece.ckv.step()
    grad_stream = total_ref[...]
    for kind in range(3):
        lanes = slice(kind * width, (kind + 1) * width)
        grad_stream = grad_stream + nt(hidden_ref[kind], refs.w_qkv[:, lanes])
    g_stream_ref[...] = grad_stream
    piece.qkv0.step()
    piece.qkv1.step()
    for step in range(5):
        few_copy(step).wait()
        total = few_ref[step] + refs.few_land[step]
        if step < 4:
            few_ref[step + 1] = total
            few_copy(step + 1).start()
        else:
            few_out_ref[...] = total
        if step < 3:
            piece.qkv0.step()
            piece.qkv1.step()
            if step < 2:
                piece.ckv.step()
    for name in PIECES:
        while getattr(piece, name).stage < 6:
            getattr(piece, name).step()


def layer_scratch(row_count, width, hidden_width, mem_rows):
    own_blocks = row_count // BLK
    blocks = own_blocks * HEADS
    head = width // HEADS
    tokens = blocks * BLK
    mem_total = mem_rows * HEADS
    dma = pltpu.SemaphoreType.DMA
    scratch = dict(
        w_qkv=((width, 3 * width), LOW), w_ckv=((width, 2 * width), LOW),
        w_out=((width, width), LOW), w_cq=((width, width), LOW),
        w_cout=((width, width), LOW), w_up=((width, hidden_width), LOW),
        w_down=((hidden_width, width), LOW),
        head_send=((HEADS, own_blocks, 3 * head, BLK), LOW),
        head_land=((blocks, 3 * head, BLK), LOW),
        memory_all=((HEADS, mem_rows, width), LOW),
        q=((tokens, 2 * head), LOW), kv=((tokens, 2 * head), LOW),
        qt=((head, tokens), LOW), kt=((head, tokens), LOW), vt=((head, tokens), LOW),
        exact=((blocks, head, BLK), WIDE), lse=((1, tokens), WIDE),
        mixed_send=((HEADS, own_blocks, head, BLK), LOW),
        mixed_land=((blocks, head, BLK), LOW),
        ck=((mem_total, width), LOW), cv=((mem_total, width), LOW),
        ckt=((width, mem_total), LOW), cvt=((width, mem_total), LOW),
        attended_t=((width, row_count), LOW),
        unit_one=((row_count, width), WIDE), unit_two=((row_count, width), WIDE),
        scale_one=((row_count, 1), WIDE), scale_two=((row_count, 1), WIDE),
        low_one=((row_count, width), LOW), low_two=((row_count, width), LOW),
        cq=((row_count, width), LOW), cqt=((width, row_count), LOW),
        scores=((mem_total, row_count), WIDE), weights=((mem_total, row_count), LOW),
        cross_exact=((width, row_count), WIDE),
        cross_lse=((HEADS // 2, 2 * row_count), WIDE),
        cross_low=((row_count, width), LOW),
        hidden=((hidden_width // width, row_count, width), LOW),
        slope=((hidden_width // width, row_count, width), LOW),
        low_third=((row_count, width), LOW),
        turned=((width, row_count), LOW),
        dco=((row_count, width), LOW), dcot=((width, row_count), LOW),
        dcqt=((width, row_count), WIDE),
        dkv_land=((HEADS // 2, mem_rows, ROWS * 4 * head), LOW),
        dkv_sum=((ROWS, HEADS // 2, mem_rows, 4 * head), LOW),
        dkv_row=((ROWS - 1, HEADS // 2, mem_rows, 4 * head), LOW),
        dckv=((mem_rows, 2 * width), LOW),
        up_land=((blocks, head, BLK), LOW),
        up=((tokens, 2 * head), LOW), upt=((head, tokens), LOW),
        dkv=((blocks, BLK, 2 * head), WIDE), dqt=((blocks, head, BLK), LOW),
        few_sum=((5, FEW_ROWS, width), WIDE), few_land=((5, FEW_ROWS, width), WIDE),
    )
    out = {name: pltpu.VMEM(shape, kind) for name, (shape, kind) in scratch.items()}
    out.update(
        load_sem=dma((7,)), to_heads_sem=dma((2, HEADS)), from_heads_sem=dma((2, HEADS)),
        up_heads_sem=dma((2, HEADS)), back_sem=dma((2, HEADS)), spread_sem=dma((2, HEADS)),
        dkv_sem=dma((2, HEADS)), few_sem=dma((2, 5)),
    )
    out.update(
        pieces={
            name: dict(
                part=pltpu.VMEM((2, ROWS, 2, 2, HALF, span), LOW),
                core_land=pltpu.VMEM((ROWS, 2, 2, HALF, span), LOW),
                hop_land=pltpu.VMEM((ROWS, 2, HALF, span), LOW),
                turn_land=pltpu.VMEM((ROWS, HALF, span), LOW),
                row_land=pltpu.VMEM((ROWS - 1, HALF, span), LOW),
                sems=dma((2, 8)),
            )
            for name, span in PIECES.items()
        }
    )
    return out


def layer_call(inverse, deal_ids, limits, tokens, memory, cotangent, weights, b_up, gains, biases, prompt_blocks):
    row_count, width = tokens.shape
    hidden_width = b_up.shape[1]
    mem_rows = memory.shape[0]
    smem = pl.BlockSpec(memory_space=pltpu.SMEM)
    vmem = pl.BlockSpec(memory_space=pltpu.VMEM)
    hbm = pl.BlockSpec(memory_space=pl.ANY)
    scratch = layer_scratch(row_count, width, hidden_width, mem_rows)
    leaves, tree = jax.tree.flatten(scratch, is_leaf=lambda leaf: not isinstance(leaf, dict))
    out_shapes = [
        (row_count, width), (row_count, width), (mem_rows, width),
        (32, 3 * width), (32, width), (32, width), (32, 2 * width), (32, width),
        (32, hidden_width), (hidden_width // SHARDS, width), (FEW_ROWS, width),
    ]

    def body(*args):
        count = len(args) - len(leaves)
        refs = Bag(jax.tree.unflatten(tree, args[count:]))
        layer_kernel(prompt_blocks, *args[:count], refs)

    return pl.pallas_call(
        body,
        out_shape=[jax.ShapeDtypeStruct(shape, WIDE) for shape in out_shapes],
        in_specs=[smem] * 3 + [vmem] * 3 + [hbm] * 7 + [vmem] * 3,
        out_specs=[vmem] * len(out_shapes),
        scratch_shapes=leaves,
        compiler_params=pltpu.CompilerParams(
            collective_id=0, has_side_effects=True, vmem_limit_bytes=BIG_VMEM
        ),
        name="layer",
    )(inverse, deal_ids, limits, tokens, memory, cotangent, *weights, b_up, gains, biases)


def layer_shards(
    stream, memory, cotangent, deal_order, offsets, context_mask,
    w_qkv, w_out, w_cq, w_ckv, w_cout, w_up, w_down, b_up, gains, biases,
):
    deal_ids = deal_order[0, 0]
    prompt_blocks = context_mask.shape[3]
    places = jnp.arange(deal_ids.shape[0], dtype=jnp.int32)
    inverse = jnp.sum(
        jnp.where(deal_ids[None, :] == places[:, None], places[None, :], 0), axis=1, dtype=jnp.int32
    )
    blocks_open = (context_mask[0, 0] > 0) | (jnp.arange(prompt_blocks)[None, :] == 0)
    limits = jnp.where(blocks_open, offsets[0, 0, 0], 0).astype(jnp.int32)
    *grads, few = layer_call(
        inverse, deal_ids, limits, stream[0, 0], memory[0, 0], cotangent[0, 0],
        (w_qkv, w_out, w_cq, w_ckv, w_cout, w_up, w_down),
        b_up[None, :], gains, biases, prompt_blocks,
    )
    output, grad_stream, grad_memory = grads[:3]
    own = lax.axis_index("ctx") * 2 + lax.axis_index("wsh")
    total_b_up = lax.dynamic_slice_in_dim(few[:4].reshape(-1), own * 128, 128)
    total_gains = lax.dynamic_slice_in_dim(few[4:7], own * 32, 32, axis=1)
    total_biases = lax.dynamic_slice_in_dim(few[7:17], own * 32, 32, axis=1)
    return (
        output[None, None], grad_stream[None, None], grad_memory[None, None],
        *grads[3:], total_b_up, total_gains, total_biases,
    )


def gelu_exact(values):
    return jax.nn.gelu(values, approximate=False)


def norm_rows(values, gain_vec, shift_vec):
    center = values - jnp.mean(values, axis=-1, keepdims=True)
    spread = jnp.mean(center * center, axis=-1, keepdims=True)
    return center * lax.rsqrt(spread + EPS_NORM) * gain_vec + shift_vec


def norm_back(values, gain_vec, shift_vec, upstream):
    _, pullback = jax.vjp(norm_rows, values, gain_vec, shift_vec)
    return pullback(upstream)


def seq_index(positions, prompt_len, cont_len):
    later = jnp.int32(1) + (positions - jnp.int32(prompt_len)) // jnp.int32(cont_len)
    return jnp.where(positions < prompt_len, jnp.zeros_like(later), later)


def visible(query_pos, key_ids, offsets, context_mask, block_len, prompt_blocks, cont_blocks):
    prompt_len = prompt_blocks * block_len
    cont_len = cont_blocks * block_len
    cont_count = offsets.shape[0]
    key_pos = (
        key_ids[:, None] * jnp.int32(block_len) + jnp.arange(block_len, dtype=jnp.int32)[None, :]
    ).reshape(-1)
    query_seq = seq_index(query_pos, prompt_len, cont_len)
    key_seq = seq_index(key_pos, prompt_len, cont_len)
    inside = (query_seq[:, None] == key_seq[None, :]) & (key_pos[None, :] <= query_pos[:, None])
    cont_pick = jnp.clip(query_seq - 1, 0, cont_count - 1)
    prompt_limit = jnp.take(offsets, cont_pick)
    query_block = jnp.clip(
        (query_pos - jnp.int32(prompt_len)) // jnp.int32(block_len), 0, cont_count * cont_blocks - 1
    )
    mask_rows = jnp.take(context_mask, query_block, axis=0)
    key_block = jnp.clip(key_ids, 0, prompt_blocks - 1)
    block_open = jnp.take(mask_rows, key_block, axis=1) > 0
    block_open = jnp.repeat(block_open, block_len, axis=1) | (key_pos[None, :] < block_len)
    from_prompt = (
        (query_seq[:, None] > 0)
        & (key_seq[None, :] == 0)
        & (key_pos[None, :] < prompt_limit[:, None])
        & block_open
    )
    return inside | from_prompt


def dot_first(left, right):
    return lax.dot_general(
        left, right, (((0,), (0,)), ((), ())), preferred_element_type=jnp.float32
    )


def dot_last(left, right):
    return lax.dot_general(
        left, right, (((1,), (1,)), ((), ())), preferred_element_type=jnp.float32
    )


def to_heads(matrix, head_count):
    row_count, model_width = matrix.shape
    return matrix.reshape(row_count, head_count, model_width // head_count).transpose(1, 0, 2)


def from_heads(stacked):
    head_count, row_count, head_width = stacked.shape
    return stacked.transpose(1, 0, 2).reshape(row_count, head_count * head_width)


def pair_heads(key_rows, value_rows, head_count):
    return jnp.concatenate(
        [to_heads(key_rows, head_count), to_heads(value_rows, head_count)], axis=2
    )


def head_scores(queries, key_rows, allowed):
    score_scale = queries.shape[1] ** (-0.5)
    scores = dot_last(queries, key_rows) * score_scale
    if allowed is not None:
        scores = jnp.where(allowed, scores, NEG_FILL)
    return scores


def head_forward(queries, keyval, allowed):
    head_width = queries.shape[1]
    scores = head_scores(queries, keyval[:, :head_width], allowed)
    row_top = jnp.max(scores, axis=1, keepdims=True)
    exp_scores = jnp.exp(scores - row_top)
    row_total = jnp.sum(exp_scores, axis=1, keepdims=True)
    soft_weights = (exp_scores / row_total).astype(jnp.bfloat16)
    mixed_heads = jnp.dot(soft_weights, keyval[:, head_width:], preferred_element_type=jnp.float32)
    return (mixed_heads, row_top + jnp.log(row_total))


def head_backward(queries, keyval, upstream, log_total, allowed):
    head_width = queries.shape[1]
    score_scale = head_width ** (-0.5)
    key_rows = keyval[:, :head_width]
    scores = head_scores(queries, key_rows, allowed)
    soft_weights = jnp.exp(scores - log_total)
    grad_soft = dot_last(upstream, keyval[:, head_width:])
    row_delta = jnp.sum(soft_weights * grad_soft, axis=1, keepdims=True)
    grad_scores = (soft_weights * (grad_soft - row_delta)).astype(jnp.bfloat16)
    grad_query = jnp.dot(grad_scores, key_rows, preferred_element_type=jnp.float32) * score_scale
    grad_keys = dot_first(grad_scores, queries) * score_scale
    grad_values = dot_first(soft_weights.astype(jnp.bfloat16), upstream)
    return (grad_query, jnp.concatenate([grad_keys, grad_values], axis=1))


def shards(
    stream,
    memory,
    cotangent,
    deal_order,
    offsets,
    context_mask,
    w_qkv,
    w_out,
    w_cq,
    w_ckv,
    w_cout,
    w_up,
    w_down,
    b_up,
    gains,
    biases,
):
    tokens = stream[0, 0]
    row_count, model_width = tokens.shape
    head_width = model_width // HEADS
    deal_ids = deal_order[0, 0]
    prompt_blocks = context_mask.shape[3]
    own_blocks = row_count // BLK
    own_ids = lax.dynamic_slice_in_dim(deal_ids, lax.axis_index("ctx") * own_blocks, own_blocks)
    query_pos = (
        own_ids[:, None] * jnp.int32(BLK) + jnp.arange(BLK, dtype=jnp.int32)[None, :]
    ).reshape(-1)
    allowed = visible(
        query_pos, deal_ids, offsets[0, 0], context_mask[0, 0], BLK, prompt_blocks, CBLK
    )
    zeros_row = jnp.zeros((model_width,), jnp.float32)
    projected = (
        jnp.dot(tokens, w_qkv, preferred_element_type=jnp.float32)
        + jnp.concatenate([biases[0], zeros_row, biases[1]])
    ).astype(jnp.bfloat16)
    query_heads = to_heads(projected[:, :model_width], HEADS)
    keyval_own = pair_heads(
        projected[:, model_width : 2 * model_width], projected[:, 2 * model_width :], HEADS
    )
    keyval_all = lax.all_gather(keyval_own, "ctx", axis=1, tiled=True)

    def self_forward(pieces):
        return head_forward(pieces[0], pieces[1], allowed)

    self_out, self_lse = lax.map(self_forward, (query_heads, keyval_all))
    attended = from_heads(self_out).astype(jnp.bfloat16)
    first_sum = (
        tokens.astype(jnp.float32)
        + jnp.dot(attended, w_out, preferred_element_type=jnp.float32)
        + biases[2]
    )
    normed_one = norm_rows(first_sum, gains[0], biases[3])
    normed_low = normed_one.astype(jnp.bfloat16)
    cross_query = (
        jnp.dot(normed_low, w_cq, preferred_element_type=jnp.float32) + biases[4]
    ).astype(jnp.bfloat16)
    cross_bias = jnp.concatenate([zeros_row, biases[5]])
    memory_own = memory[0, 0]
    memory_all = lax.all_gather(memory_own, "ctx", axis=0, tiled=True)
    cross_kv = (jnp.dot(memory_all, w_ckv, preferred_element_type=jnp.float32) + cross_bias).astype(
        jnp.bfloat16
    )
    cross_heads = pair_heads(cross_kv[:, :model_width], cross_kv[:, model_width:], HEADS)
    cross_query_heads = to_heads(cross_query, HEADS)

    def cross_forward(pieces):
        return head_forward(pieces[0], pieces[1], None)

    cross_out, cross_lse = lax.map(cross_forward, (cross_query_heads, cross_heads))
    cross_attended = from_heads(cross_out).astype(jnp.bfloat16)
    second_sum = (
        normed_one + jnp.dot(cross_attended, w_cout, preferred_element_type=jnp.float32) + biases[6]
    )
    normed_two = norm_rows(second_sum, gains[1], biases[7])
    normed_two_low = normed_two.astype(jnp.bfloat16)
    hidden_pre = jnp.dot(normed_two_low, w_up, preferred_element_type=jnp.float32) + b_up
    hidden = gelu_exact(hidden_pre).astype(jnp.bfloat16)
    third_sum = normed_two + jnp.dot(hidden, w_down, preferred_element_type=jnp.float32) + biases[8]
    output = norm_rows(third_sum, gains[2], biases[9])
    grad_third, grad_gain_three, grad_shift_three = norm_back(
        third_sum, gains[2], biases[9], cotangent[0, 0].astype(jnp.float32)
    )
    grad_down_in = grad_third.astype(jnp.bfloat16)
    grad_w_down = dot_first(hidden, grad_down_in)
    grad_b_down = jnp.sum(grad_down_in.astype(jnp.float32), axis=0)
    grad_hidden = dot_last(grad_down_in, w_down)
    _, gelu_pull = jax.vjp(gelu_exact, hidden_pre)
    grad_pre = gelu_pull(grad_hidden)[0].astype(jnp.bfloat16)
    grad_w_up = dot_first(normed_two_low, grad_pre)
    grad_b_up = jnp.sum(grad_pre.astype(jnp.float32), axis=0)
    grad_normed_two = grad_third + dot_last(grad_pre, w_up)
    grad_second, grad_gain_two, grad_shift_two = norm_back(
        second_sum, gains[1], biases[7], grad_normed_two
    )
    grad_cross_in = grad_second.astype(jnp.bfloat16)
    grad_w_cout = dot_first(cross_attended, grad_cross_in)
    grad_b_co = jnp.sum(grad_cross_in.astype(jnp.float32), axis=0)
    grad_cross_heads = to_heads(dot_last(grad_cross_in, w_cout).astype(jnp.bfloat16), HEADS)

    def cross_backward(pieces):
        return head_backward(pieces[0], pieces[1], pieces[2], pieces[3], None)

    grad_cq_heads, grad_ckv_all = lax.map(
        cross_backward, (cross_query_heads, cross_heads, grad_cross_heads, cross_lse)
    )
    grad_ckv_own = lax.psum_scatter(
        grad_ckv_all.astype(jnp.bfloat16), "ctx", scatter_dimension=1, tiled=True
    )
    grad_cv = from_heads(grad_ckv_own[:, :, head_width:])
    grad_ckv = jnp.concatenate([from_heads(grad_ckv_own[:, :, :head_width]), grad_cv], axis=1)
    grad_w_ckv = dot_first(memory_own, grad_ckv)
    grad_b_cv = jnp.sum(grad_cv.astype(jnp.float32), axis=0)
    grad_memory = dot_last(grad_ckv, w_ckv)
    grad_cq = from_heads(grad_cq_heads).astype(jnp.bfloat16)
    grad_w_cq = dot_first(normed_low, grad_cq)
    grad_b_cq = jnp.sum(grad_cq.astype(jnp.float32), axis=0)
    grad_normed_one = grad_second + dot_last(grad_cq, w_cq)
    grad_first, grad_gain_one, grad_shift_one = norm_back(
        first_sum, gains[0], biases[3], grad_normed_one
    )
    grad_att_in = grad_first.astype(jnp.bfloat16)
    grad_w_out = dot_first(attended, grad_att_in)
    grad_b_o = jnp.sum(grad_att_in.astype(jnp.float32), axis=0)
    grad_self_heads = to_heads(dot_last(grad_att_in, w_out).astype(jnp.bfloat16), HEADS)

    def self_backward(pieces):
        return head_backward(pieces[0], pieces[1], pieces[2], pieces[3], allowed)

    grad_q_heads, grad_kv_all = lax.map(
        self_backward, (query_heads, keyval_all, grad_self_heads, self_lse)
    )
    grad_kv_own = lax.psum_scatter(
        grad_kv_all.astype(jnp.bfloat16), "ctx", scatter_dimension=1, tiled=True
    )
    grad_values = from_heads(grad_kv_own[:, :, head_width:])
    grad_queries = from_heads(grad_q_heads).astype(jnp.bfloat16)
    grad_proj = jnp.concatenate(
        [grad_queries, from_heads(grad_kv_own[:, :, :head_width]), grad_values], axis=1
    )
    grad_w_qkv = dot_first(tokens, grad_proj)
    grad_b_q = jnp.sum(grad_queries.astype(jnp.float32), axis=0)
    grad_b_v = jnp.sum(grad_values.astype(jnp.float32), axis=0)
    grad_tokens = grad_first + dot_last(grad_proj, w_qkv)
    gain_grads = jnp.stack([grad_gain_one, grad_gain_two, grad_gain_three])
    shift_grads = jnp.stack(
        [
            grad_b_q,
            grad_b_v,
            grad_b_o,
            grad_shift_one,
            grad_b_cq,
            grad_b_cv,
            grad_b_co,
            grad_shift_two,
            grad_b_down,
            grad_shift_three,
        ]
    )
    (
        part_qkv,
        part_out,
        part_cq,
        part_ckv,
        part_cout,
        part_up,
        part_down,
        part_b_up,
        part_gains,
        part_biases,
    ) = (
        lax.psum_scatter(grad_w_qkv, ("ctx", "wsh"), scatter_dimension=0, tiled=True),
        lax.psum_scatter(grad_w_out, ("ctx", "wsh"), scatter_dimension=0, tiled=True),
        lax.psum_scatter(grad_w_cq, ("ctx", "wsh"), scatter_dimension=0, tiled=True),
        lax.psum_scatter(grad_w_ckv, ("ctx", "wsh"), scatter_dimension=0, tiled=True),
        lax.psum_scatter(grad_w_cout, ("ctx", "wsh"), scatter_dimension=0, tiled=True),
        lax.psum_scatter(grad_w_up, ("ctx", "wsh"), scatter_dimension=0, tiled=True),
        lax.psum_scatter(grad_w_down, ("ctx", "wsh"), scatter_dimension=0, tiled=True),
        lax.psum_scatter(grad_b_up, ("ctx", "wsh"), scatter_dimension=0, tiled=True),
        lax.psum_scatter(gain_grads, ("ctx", "wsh"), scatter_dimension=1, tiled=True),
        lax.psum_scatter(shift_grads, ("ctx", "wsh"), scatter_dimension=1, tiled=True),
    )
    (
        total_qkv,
        total_out,
        total_cq,
        total_ckv,
        total_cout,
        total_up,
        total_down,
        total_b_up,
        total_gains,
        total_biases,
    ) = (
        lax.psum(part_qkv.astype(jnp.bfloat16), "grp").astype(jnp.float32),
        lax.psum(part_out.astype(jnp.bfloat16), "grp").astype(jnp.float32),
        lax.psum(part_cq.astype(jnp.bfloat16), "grp").astype(jnp.float32),
        lax.psum(part_ckv.astype(jnp.bfloat16), "grp").astype(jnp.float32),
        lax.psum(part_cout.astype(jnp.bfloat16), "grp").astype(jnp.float32),
        lax.psum(part_up.astype(jnp.bfloat16), "grp").astype(jnp.float32),
        lax.psum(part_down.astype(jnp.bfloat16), "grp").astype(jnp.float32),
        lax.psum(part_b_up.astype(jnp.bfloat16), "grp").astype(jnp.float32),
        lax.psum(part_gains.astype(jnp.bfloat16), "grp").astype(jnp.float32),
        lax.psum(part_biases.astype(jnp.bfloat16), "grp").astype(jnp.float32),
    )
    return (
        output[None, None],
        grad_tokens[None, None],
        grad_memory[None, None],
        total_qkv,
        total_out,
        total_cq,
        total_ckv,
        total_cout,
        total_up,
        total_down,
        total_b_up,
        total_gains,
        total_biases,
    )


def solution(mesh):
    in_specs = (
        P("grp", "wsh", "ctx", None),
        P("grp", "wsh", "ctx", None),
        P("grp", "wsh", "ctx", None),
        P("grp", "wsh", None),
        P("grp", "wsh", None),
        P("grp", "wsh", None, None),
        P(),
        P(),
        P(),
        P(),
        P(),
        P(),
        P(),
        P(),
        P(),
        P(),
    )
    out_specs = (
        P("grp", "wsh", "ctx", None),
        P("grp", "wsh", "ctx", None),
        P("grp", "wsh", "ctx", None),
        P(("ctx", "wsh"), None),
        P(("ctx", "wsh"), None),
        P(("ctx", "wsh"), None),
        P(("ctx", "wsh"), None),
        P(("ctx", "wsh"), None),
        P(("ctx", "wsh"), None),
        P(("ctx", "wsh"), None),
        P(("ctx", "wsh")),
        P(None, ("ctx", "wsh")),
        P(None, ("ctx", "wsh")),
    )
    body = layer_shards if mesh.shape["ctx"] == HEADS else shards
    return jax.shard_map(body, mesh=mesh, in_specs=in_specs, out_specs=out_specs, check_vma=False)
```

```python
import functools

import jax
import jax.numpy as jnp
from jax import lax
from jax.experimental import pallas as pl
from jax.experimental.pallas import tpu as pltpu
from jax.sharding import PartitionSpec as P

HEADS = 8
BLK = 128
CBLK = 16


NEG_FILL = -1000000000.0
EPS_NORM = 1e-05


MESH_ID = pl.DeviceIdType.MESH
TILE = 512
STEP = 256
BIG_VMEM = 62 << 20
LOW = jnp.bfloat16
WIDE = jnp.float32
SHARDS = 16
HALF = 16
ROWS = 4
PIECES = dict(
    up0=1024, up1=1024, down0=1024, down1=1024, cross=1024, out=512, ckv=1024, wq=512, wk=512, wv=512
)
TURNS = dict(up0=0, up1=0, down0=0, down1=1, cross=0, out=1, ckv=1, wq=2, wk=2, wv=2)
FEW_ROWS = 24


def nn(left, right):
    return lax.dot_general(
        left, right, (((1,), (0,)), ((), ())), preferred_element_type=WIDE
    )


def nt(left, right):
    return lax.dot_general(
        left, right, (((1,), (1,)), ((), ())), preferred_element_type=WIDE
    )


def swap(block):
    return block.astype(WIDE).T.astype(block.dtype)


def plus(left, right):
    return left.astype(WIDE) + right.astype(WIDE)


def column_sums(values):
    return jnp.sum(values.astype(WIDE), axis=0, keepdims=True)


def norm_parts(values):
    center = values - jnp.mean(values, axis=-1, keepdims=True)
    spread = jnp.mean(center * center, axis=-1, keepdims=True)
    scale = lax.rsqrt(spread + EPS_NORM)
    return center * scale, scale


def norm_pull(unit, scale, gain, upstream):
    inner = upstream * gain
    first = jnp.mean(inner, axis=-1, keepdims=True)
    second = jnp.mean(inner * unit, axis=-1, keepdims=True)
    return scale * (inner - first - unit * second)


def hide_later(scores):
    rows = lax.broadcasted_iota(jnp.int32, scores.shape, 0)
    cols = lax.broadcasted_iota(jnp.int32, scores.shape, 1)
    return jnp.where(rows <= cols, scores, NEG_FILL)


def hide_prompt(scores, offset_ref, open_ref, tile, chunk, prompt_blocks):
    span = TILE // BLK
    rows = lax.broadcasted_iota(jnp.int32, (BLK, BLK), 0)
    columns = []
    for q_sub in range(span):
        pieces = []
        for k_sub in range(span):
            key_block = chunk * span + k_sub
            opened = open_ref[tile * span + q_sub - prompt_blocks, key_block]
            opened = jnp.where(key_block == 0, 1, opened)
            limit = jnp.where(opened > 0, offset_ref[0], 0) - key_block * BLK
            part = scores[k_sub * BLK : (k_sub + 1) * BLK, q_sub * BLK : (q_sub + 1) * BLK]
            pieces.append(jnp.where(rows < limit, part, NEG_FILL))
        columns.append(jnp.concatenate(pieces, axis=0))
    return jnp.concatenate(columns, axis=1)


def apart(upper, lower):
    none = jnp.zeros_like(upper)
    return jnp.concatenate(
        [jnp.concatenate([upper, none], axis=1), jnp.concatenate([none, lower], axis=1)], axis=0
    )


def apart_columns(pair):
    lanes = lax.broadcasted_iota(jnp.int32, pair.shape, 1)
    wide = pair.astype(WIDE)
    left = jnp.where(lanes < pair.shape[1] // 2, wide, 0.0).astype(pair.dtype)
    right = jnp.where(lanes < pair.shape[1] // 2, 0.0, wide).astype(pair.dtype)
    return jnp.concatenate([left, right], axis=0)


def remote(src_ref, dst_ref, send_sem, recv_sem, target):
    return pltpu.make_async_remote_copy(
        src_ref=src_ref,
        dst_ref=dst_ref,
        send_sem=send_sem,
        recv_sem=recv_sem,
        device_id=target,
        device_id_type=MESH_ID,
    )


class Bag:
    def __init__(self, items):
        self.__dict__.update(items)


class Spot:
    def __init__(self):
        ctx = lax.axis_index("ctx")
        self.grp, self.ctx, self.wsh = lax.axis_index("grp"), ctx, lax.axis_index("wsh")
        self.row, self.col = ctx // 2, lax.rem(ctx, 2)
        self.core_peer = (1 - self.grp, ctx, self.wsh)
        self.wsh_peer = (self.grp, ctx, 1 - self.wsh)
        self.col_peer = self.at_row_col(self.row, 1 - self.col)
        self.cross_peer = (self.grp, self.row * 2 + 1 - self.col, 1 - self.wsh)
        self.rows_by_step = [lax.rem(self.row + step, ROWS) for step in range(ROWS)]
        self.row_peers = [self.at_row_col(row, self.col) for row in self.rows_by_step]
        near = self.row + 1 - 2 * lax.rem(self.row, 2)
        self.few_peers = [
            self.core_peer, self.wsh_peer, self.col_peer,
            self.at_row_col(near, self.col), self.row_peers[2],
        ]
        self.ctx_by_step = [lax.rem(ctx + step, HEADS) for step in range(HEADS)]
        self.ctx_peers = [(self.grp, peer, self.wsh) for peer in self.ctx_by_step]

    def at_row_col(self, row, col):
        return (self.grp, row * 2 + col, self.wsh)

    def greet(self):
        barrier = pltpu.get_barrier_semaphore()
        targets = [self.core_peer, self.wsh_peer, self.cross_peer] + self.ctx_peers[1:]
        for target in targets:
            pl.semaphore_signal(barrier, inc=1, device_id=target, device_id_type=MESH_ID)
        return len(targets)


class Exchange:
    def __init__(self, spot, source, target, sems, cuts):
        self.spot, self.source, self.target, self.sems, self.cuts = spot, source, target, sems, cuts
        self.copies = [[] for _ in cuts]

    def start(self, part=0):
        spot, own_blocks = self.spot, self.source.shape[1]
        first, count, rows = self.cuts[part]
        here = (pl.ds(spot.ctx * own_blocks + first, count), rows)
        there = (pl.ds(first, count), rows)
        for step in range(1, HEADS):
            copy = remote(
                self.source.at[(spot.ctx_by_step[step],) + there], self.target.at[here],
                self.sems.at[0, step, part], self.sems.at[1, step, part], spot.ctx_peers[step],
            )
            copy.start()
            self.copies[part].append(copy)
        self.target[here] = self.source[(spot.ctx,) + there]

    def wait(self, part=0):
        for copy in self.copies[part]:
            copy.wait()


class Piece:
    def __init__(self, spot, turn, refs, outs):
        self.spot, self.turn, self.sems, self.outs = spot, turn, refs.sems, outs
        self.part, self.core_land, self.hop_land = refs.part, refs.core_land, refs.hop_land
        self.turn_land, self.row_land = refs.turn_land, refs.row_land
        self.turn_sum = self.core_land.at[:, 0]
        self.copies = []
        self.stage = 0

    def copy(self, index, source, target_ref, target):
        copy = remote(source, target_ref, self.sems.at[0, index], self.sems.at[1, index], target)
        copy.start()
        self.copies.append(copy)

    def finish(self):
        for copy in self.copies:
            copy.wait()
        self.copies = []

    def send_rows(self):
        spot = self.spot
        for step in range(1, ROWS):
            self.copy(
                2 + step, self.turn_land.at[spot.rows_by_step[step]],
                self.row_land.at[step - 1], spot.row_peers[step],
            )

    def steps(self, stage):
        while self.stage < stage:
            self.step()

    def step(self):
        spot, part = self.spot, self.part
        own = spot.grp
        if self.stage == 0:
            self.copy(0, part.at[1 - own], self.core_land, spot.core_peer)
        elif self.stage == 1:
            self.finish()
            part[own] = plus(part[own], self.core_land[...]).astype(LOW)
            if self.turn == 2:
                col, wsh = spot.col, spot.wsh
                ways = [
                    (spot.wsh_peer, col, 1 - wsh),
                    (spot.col_peer, 1 - col, wsh),
                    (spot.cross_peer, 1 - col, 1 - wsh),
                ]
                for way, (target, to_col, to_wsh) in enumerate(ways):
                    self.copy(
                        (1, 2, 6)[way], part.at[own, :, to_col, to_wsh], self.hop_land.at[way],
                        target,
                    )
            elif self.turn == 0:
                self.copy(1, part.at[own, :, :, 1 - spot.wsh], self.hop_land, spot.wsh_peer)
            else:
                self.copy(1, part.at[own, :, 1 - spot.col], self.hop_land, spot.col_peer)
        elif self.stage == 2:
            self.finish()
            if self.turn == 2:
                total = part[own, :, spot.col, spot.wsh].astype(WIDE)
                for way in range(3):
                    total = total + self.hop_land[way].astype(WIDE)
                self.turn_land[...] = total.astype(LOW)
                self.send_rows()
                self.stage = 4
                return
            if self.turn == 0:
                mine = part[own, :, :, spot.wsh]
                away, target = 1 - spot.col, spot.col_peer
            else:
                mine = part[own, :, spot.col]
                away, target = 1 - spot.wsh, spot.wsh_peer
            self.turn_sum[...] = plus(mine, self.hop_land[...]).astype(LOW)
            self.copy(2, self.turn_sum.at[:, away], self.turn_land, target)
        elif self.stage == 3:
            self.finish()
            keep = spot.col if self.turn == 0 else spot.wsh
            self.turn_land[...] = plus(self.turn_sum[:, keep], self.turn_land[...]).astype(LOW)
            self.send_rows()
        elif self.stage == 4:
            self.finish()
            total = self.turn_land[spot.row].astype(WIDE)
            for step in range(ROWS - 1):
                total = total + self.row_land[step].astype(WIDE)
            at = 0
            for index, (out_ref, row, column, width) in enumerate(self.outs):
                here = (
                    pl.ds(pl.multiple_of(row + own * HALF, HALF), HALF),
                    slice(column, column + width),
                )
                out_ref[here] = total[:, at : at + width]
                at += width
                self.copy(7 + index, out_ref.at[here], out_ref.at[here], spot.core_peer)
        elif self.stage == 5:
            self.finish()
        self.stage += 1


def layer_kernel(
    prompt_blocks,
    deal_ref, offset_ref, open_ref, tokens_ref, memory_ref, cot_ref,
    w_qkv_hbm, w_out_hbm, w_cq_hbm, w_ckv_hbm, w_cout_hbm, w_up_hbm, w_down_hbm,
    b_up_ref, gains_ref, biases_ref,
    output_ref, g_stream_ref, g_memory_ref, o_qkv_ref, o_out_ref, o_cq_ref, o_ckv_ref, o_cout_ref,
    o_up_ref, o_down_ref, o_b_up_ref, o_gains_ref, o_biases_ref,
    refs,
):
    spot = Spot()
    greeted = spot.greet()
    row_count, width = tokens_ref.shape
    own_blocks = row_count // BLK
    head = width // HEADS
    blocks = own_blocks * HEADS
    mem_rows = memory_ref.shape[0]
    mem_total = mem_rows * HEADS
    hidden_width = b_up_ref.shape[1]
    chunks = hidden_width // width
    pairs = HEADS // 2
    score_scale = head ** (-0.5)
    prompt_tiles = prompt_blocks * BLK // TILE
    tiles = blocks * BLK // TILE

    sources = dict(
        w_qkv=w_qkv_hbm, w_ckv=w_ckv_hbm, w_out=w_out_hbm, w_cq=w_cq_hbm, w_cout=w_cout_hbm,
        w_up=w_up_hbm, w_down=w_down_hbm,
    )
    loads = Bag(
        {
            name: pltpu.make_async_copy(source, getattr(refs, name), refs.load_sem.at[index])
            for index, (name, source) in enumerate(sources.items())
        }
    )
    for name in sources:
        getattr(loads, name).start()

    outs = dict(
        up0=[(o_up_ref, 0, 0, 1024)],
        up1=[(o_up_ref, 0, 1024, 1024)],
        down0=[(o_down_ref, 0, 0, 512), (o_down_ref, 32, 0, 512)],
        down1=[(o_down_ref, 64, 0, 512), (o_down_ref, 96, 0, 512)],
        cross=[(o_cout_ref, 0, 0, 512), (o_cq_ref, 0, 0, 512)],
        out=[(o_out_ref, 0, 0, 512)],
        ckv=[(o_ckv_ref, 0, 0, 1024)],
        wq=[(o_qkv_ref, 0, 0, 512)],
        wk=[(o_qkv_ref, 0, 512, 512)],
        wv=[(o_qkv_ref, 0, 1024, 512)],
    )
    piece = Bag(
        {
            name: Piece(spot, TURNS[name], Bag(refs.pieces[name]), outs[name])
            for name in PIECES
        }
    )
    ups, downs = (piece.up0, piece.up1), (piece.down0, piece.down1)

    def put_rows(to, values, column):
        span = values.shape[1]
        split = values.astype(LOW).reshape(ROWS, 2, 2, 2, HALF, span)
        for half in range(2):
            to.part[half, :, :, :, :, column : column + span] = split[:, :, :, half]

    few_ref = refs.few_sum
    few_ref[0] = jnp.zeros_like(few_ref[0])

    def few(row, values):
        few_ref[0, row : row + 1, :] = values

    def gain(row):
        return gains_ref[row : row + 1, :]

    def bias(row):
        return biases_ref[row : row + 1, :]

    send_ref = refs.head_send
    loads.w_qkv.wait()
    zeros_row = jnp.zeros((1, width), WIDE)
    projected_bias = jnp.concatenate([bias(0), zeros_row, bias(1)], axis=1)
    to_heads_copy = Exchange(
        spot, send_ref, refs.head_land, refs.to_heads_sem,
        [(block, 1, slice(0, 3 * head)) for block in range(own_blocks)],
    )
    for block in range(own_blocks):
        rows = slice(block * BLK, (block + 1) * BLK)
        projected = (nn(tokens_ref[rows, :], refs.w_qkv[...]) + projected_bias).astype(LOW)
        turned = projected.astype(WIDE).T
        turned = jnp.concatenate([turned[:width] * score_scale, turned[width:]], axis=0).astype(LOW)
        for h in range(HEADS):
            for kind in range(3):
                at = kind * width + h * head
                send_ref[h, block, kind * head : (kind + 1) * head, :] = turned[at : at + head]
        if block == 0:
            pl.semaphore_wait(pltpu.get_barrier_semaphore(), greeted)
        to_heads_copy.start(block)
    inv_ref = refs.inverse
    for pos in range(blocks):
        row = jnp.int32(0)
        for other in range(1, blocks):
            row = jnp.where(deal_ref[other] == pos, other, row)
        inv_ref[pos] = row
    for block in range(own_blocks):
        to_heads_copy.wait(block)
    all_ref = refs.memory_all
    spread = []
    for step in range(1, ROWS):
        copy = remote(
            memory_ref, all_ref.at[spot.col, spot.row],
            refs.spread_sem.at[0, step], refs.spread_sem.at[1, step], spot.row_peers[step],
        )
        copy.start()
        spread.append(copy)
    all_ref[spot.col, spot.row] = memory_ref[...]

    q_ref, kv_ref = refs.q, refs.kv
    no_head = jnp.zeros((head, BLK), LOW)
    no_tile = jnp.zeros((head, TILE), LOW)
    qt_ref, kt_ref, vt_ref = refs.qt, refs.kt, refs.vt
    exact_ref, lse_ref = refs.exact, refs.lse
    for pos in range(blocks):
        block = refs.head_land[inv_ref[pos]]
        at = slice(pos * BLK, (pos + 1) * BLK)
        qt_ref[:, at] = block[:head]
        kt_ref[:, at] = block[head : 2 * head]
        vt_ref[:, at] = block[2 * head :]
        kv_ref[at, :] = swap(block[head:])

    def tile_spans(tile, chunk_step, state):
        state = chunk_step(tile, state, lambda s, c: hide_later(s))
        first = jnp.where(tile >= prompt_tiles, prompt_tiles, 0)
        state = lax.fori_loop(first, tile, lambda c, s: chunk_step(c, s, lambda x, _: x), state)
        return lax.fori_loop(
            0,
            first,
            lambda c, s: chunk_step(
                c, s, lambda x, cc: hide_prompt(x, offset_ref, open_ref, tile, cc, prompt_blocks)
            ),
            state,
        )

    def forward_tile(tile, carry):
        here = pl.ds(pl.multiple_of(tile * TILE, TILE), TILE)
        queries = jnp.concatenate([qt_ref[:, here], no_tile], axis=0)

        def top_step(chunk, top, hide):
            there = pl.ds(pl.multiple_of(chunk * TILE, TILE), TILE)
            scores = hide(nn(kv_ref[there, :], queries), chunk)
            return jnp.maximum(top, jnp.max(scores.reshape(TILE // 8, 8, TILE), axis=0))

        top = tile_spans(tile, top_step, jnp.full((8, TILE), NEG_FILL, WIDE))
        top = jnp.max(top, axis=0, keepdims=True)

        def chunk_step(chunk, state, hide):
            total, mixed = state
            there = pl.ds(pl.multiple_of(chunk * TILE, TILE), TILE)
            weights = jnp.exp(hide(nn(kv_ref[there, :], queries), chunk) - top)
            total = total + jnp.sum(weights.reshape(TILE // 8, 8, TILE), axis=0)
            return total, mixed + nn(vt_ref[:, there], weights.astype(LOW))

        total, mixed = tile_spans(
            tile, chunk_step, (jnp.zeros((8, TILE), WIDE), jnp.zeros((head, TILE), WIDE))
        )
        total = jnp.sum(total, axis=0, keepdims=True)
        exact = mixed / total
        for sub in range(TILE // BLK):
            exact_ref[tile * (TILE // BLK) + sub] = exact[:, sub * BLK : (sub + 1) * BLK]
        lse_ref[:, here] = top + jnp.log(total)
        return carry

    lax.fori_loop(0, tiles - 2, forward_tile, 0)
    for copy in spread:
        copy.wait()
    spread_side = remote(
        all_ref.at[spot.col], all_ref.at[spot.col],
        refs.spread_sem.at[0, 0], refs.spread_sem.at[1, 0], spot.col_peer,
    )
    spread_side.start()
    lax.fori_loop(tiles - 2, tiles, forward_tile, 0)
    mixed_ref = refs.mixed_send
    for row in range(blocks):
        mixed_ref[row // own_blocks, row % own_blocks] = exact_ref[deal_ref[row]].astype(LOW)
    all_blocks = [(0, own_blocks, slice(0, head))]
    from_heads_copy = Exchange(spot, mixed_ref, refs.mixed_land, refs.from_heads_sem, all_blocks)
    from_heads_copy.start()

    ck_ref, cv_ref, ckt_ref, cvt_ref = refs.ck, refs.cv, refs.ckt, refs.cvt
    loads.w_ckv.wait()
    spread_side.wait()
    for part in range(HEADS):
        rows = slice(part * mem_rows, (part + 1) * mem_rows)
        both = nn(all_ref[part % 2, part // 2], refs.w_ckv[...])
        keys = both[:, :width].astype(LOW)
        values = (both[:, width:] + bias(5)).astype(LOW)
        ck_ref[rows, :] = keys
        cv_ref[rows, :] = values
        ckt_ref[:, rows] = swap(keys)
        cvt_ref[:, rows] = swap(values)

    loads.w_out.wait()
    from_heads_copy.wait()
    attended_t_ref = refs.attended_t
    unit_one_ref, unit_two_ref = refs.unit_one, refs.unit_two
    low_one_ref, low_two_ref = refs.low_one, refs.low_two
    for block in range(own_blocks):
        at = slice(block * BLK, (block + 1) * BLK)
        for h in range(HEADS):
            attended_t_ref[h * head : (h + 1) * head, at] = refs.mixed_land[h * own_blocks + block]
    cq_ref, cqt_ref = refs.cq, refs.cqt
    loads.w_cq.wait()

    def rows_at(block):
        return pl.ds(pl.multiple_of(block * BLK, BLK), BLK)

    def first_norm(block, carry):
        rows = rows_at(block)
        attended = swap(attended_t_ref[:, rows])
        first_sum = tokens_ref[rows, :].astype(WIDE) + nn(attended, refs.w_out[...]) + bias(2)
        unit, scale = norm_parts(first_sum)
        unit_one_ref[rows, :] = unit
        refs.scale_one[rows, :] = scale
        low_one = (unit * gain(0) + bias(3)).astype(LOW)
        low_one_ref[rows, :] = low_one
        cross_query = (nn(low_one, refs.w_cq[...]) + bias(4)).astype(LOW).astype(WIDE)
        cross_query = cross_query * score_scale
        cq_ref[rows, :] = cross_query.astype(LOW)
        cqt_ref[:, rows] = cross_query.T.astype(LOW)
        return carry

    lax.fori_loop(0, own_blocks, first_norm, 0)

    pair_width = 2 * head
    cross_exact_ref, cross_lse_ref = refs.cross_exact, refs.cross_lse
    steps = mem_total // STEP

    def pair_at(pair):
        return pl.ds(pl.multiple_of(pair * pair_width, pair_width), pair_width)

    def step_at(step):
        return pl.ds(pl.multiple_of(step * STEP, STEP), STEP)

    def cross_forward(pair, carry):
        lanes = pair_at(pair)
        for side in range(2):
            at = pl.ds(pl.multiple_of(pair * pair_width + side * head, head), head)
            queries = cqt_ref[at, :]
            none = jnp.zeros_like(queries)
            queries = jnp.concatenate([none, queries] if side else [queries, none], axis=0)

            def first_pass(step, top):
                scores = nn(ck_ref[step_at(step), lanes], queries)
                return jnp.maximum(top, jnp.max(scores.reshape(STEP // 8, 8, row_count), axis=0))

            top = lax.fori_loop(
                0, steps, first_pass, jnp.full((8, row_count), NEG_FILL, WIDE), unroll=True
            )
            top = jnp.max(top, axis=0, keepdims=True)

            def second_pass(step, state):
                total, mixed = state
                weights = jnp.exp(nn(ck_ref[step_at(step), lanes], queries) - top)
                total = total + jnp.sum(weights.reshape(STEP // 8, 8, row_count), axis=0)
                return total, mixed + nn(cvt_ref[at, step_at(step)], weights.astype(LOW))

            total, mixed = lax.fori_loop(
                0, steps, second_pass,
                (jnp.zeros((8, row_count), WIDE), jnp.zeros((head, row_count), WIDE)), unroll=True,
            )
            total = jnp.sum(total, axis=0, keepdims=True)
            across = slice(side * row_count, (side + 1) * row_count)
            cross_lse_ref[pl.ds(pair, 1), across] = top + jnp.log(total)
            cross_exact_ref[at, :] = mixed / total
        return carry

    lax.fori_loop(0, pairs, cross_forward, 0)
    cross_low_ref = refs.cross_low
    total_ref, hidden_ref, slope_ref = g_stream_ref, refs.hidden, refs.slope
    loads.w_cout.wait()

    def second_norm(block, carry):
        rows = rows_at(block)
        cross_low = cross_exact_ref[:, rows].T.astype(LOW)
        cross_low_ref[rows, :] = cross_low
        normed_one = unit_one_ref[rows, :] * gain(0) + bias(3)
        unit, scale = norm_parts(normed_one + nn(cross_low, refs.w_cout[...]) + bias(6))
        unit_two_ref[rows, :] = unit
        refs.scale_two[rows, :] = scale
        normed_two = unit * gain(1) + bias(7)
        low_two_ref[rows, :] = normed_two.astype(LOW)
        total_ref[rows, :] = normed_two + bias(8)
        return carry

    lax.fori_loop(0, own_blocks, second_norm, 0)

    loads.w_up.wait()
    loads.w_down.wait()
    w_up_ref, w_down_ref = refs.w_up, refs.w_down

    def chunk_at(chunk):
        return pl.ds(pl.multiple_of(chunk * width, width), width)

    def up_step(chunk, carry):
        pre = nn(low_two_ref[...], w_up_ref[:, chunk_at(chunk)]) + b_up_ref[:, chunk_at(chunk)]
        normal = 0.5 + 0.5 * lax.erf(pre * (2.0**-0.5))
        hidden = (pre * normal).astype(LOW)
        hidden_ref[chunk] = hidden
        slope = normal + pre * jnp.exp(-0.5 * pre * pre) * ((2.0 * jnp.pi) ** -0.5)
        slope_ref[chunk] = slope.astype(LOW)
        total_ref[...] += nn(hidden, w_down_ref[chunk_at(chunk), :])
        return carry

    lax.fori_loop(0, chunks, up_step, 0)

    low_third_ref = refs.low_third
    no_sums = (zeros_row, zeros_row, zeros_row)

    def third_norm(block, sums):
        rows = rows_at(block)
        unit, scale = norm_parts(total_ref[rows, :])
        output_ref[rows, :] = unit * gain(2) + bias(9)
        upstream = cot_ref[rows, :].astype(WIDE)
        grad = norm_pull(unit, scale, gain(2), upstream)
        low = grad.astype(LOW)
        low_third_ref[rows, :] = low
        total_ref[rows, :] = grad
        return (
            sums[0] + column_sums(upstream * unit),
            sums[1] + column_sums(upstream),
            sums[2] + column_sums(low),
        )

    sums = lax.fori_loop(0, own_blocks, third_norm, no_sums)
    few(6, sums[0])
    few(16, sums[1])
    few(15, sums[2])

    turned_ref = refs.turned
    turned_ref[...] = swap(low_two_ref[...])
    for chunk in range(chunks):
        rows = slice(chunk * width, (chunk + 1) * width)
        grad_hidden = nt(low_third_ref[...], w_down_ref[rows, :])
        grad_pre = (grad_hidden * slope_ref[chunk].astype(WIDE)).astype(LOW)
        few(chunk, column_sums(grad_pre))
        total_ref[...] += nt(grad_pre, w_up_ref[:, rows])
        grad_up = nn(turned_ref[...], grad_pre)
        put_rows(ups[chunk // 2], grad_up, (chunk % 2) * width)
        if chunk % 2 == 1:
            ups[chunk // 2].step()
        if chunk == 2:
            piece.up0.step()
        grad_down = nn(swap(hidden_ref[chunk]), low_third_ref[...])
        split = grad_down.astype(LOW).reshape(2, 2, 4, 2, HALF, width)
        for part in range(4):
            to = downs[part // 2].part
            column = (part % 2) * width
            for half in range(2):
                to[half, chunk, :, :, :, column : column + width] = split[:, :, part, half]
    piece.down0.step()
    piece.down1.step()

    dco_ref, dcot_ref = refs.dco, refs.dcot

    def second_back(block, sums):
        rows = rows_at(block)
        upstream = total_ref[rows, :]
        unit = unit_two_ref[rows, :]
        grad = norm_pull(unit, refs.scale_two[rows, :], gain(1), upstream)
        low = grad.astype(LOW)
        total_ref[rows, :] = grad
        low_third_ref[rows, :] = low
        dco_ref[rows, :] = nt(low, refs.w_cout[...]).astype(LOW)
        dcot_ref[:, rows] = nt(refs.w_cout[...], low).astype(LOW)
        return (
            sums[0] + column_sums(upstream * unit),
            sums[1] + column_sums(upstream),
            sums[2] + column_sums(low),
        )

    sums = lax.fori_loop(0, own_blocks, second_back, no_sums)
    few(5, sums[0])
    few(14, sums[1])
    few(13, sums[2])
    put_rows(piece.cross, nn(swap(cross_low_ref[...]), low_third_ref[...]), 0)
    piece.up1.step()
    piece.down0.step()
    piece.down1.step()

    dcqt_ref = refs.dcqt
    for pair in range(pairs):
        lanes = slice(pair * pair_width, (pair + 1) * pair_width)
        low_half = slice(pair * pair_width, pair * pair_width + head)
        high_half = slice(pair * pair_width + head, (pair + 1) * pair_width)
        queries_t = apart(cqt_ref[low_half, :], cqt_ref[high_half, :])
        upstream_t = apart(dcot_ref[low_half, :], dcot_ref[high_half, :])
        queries = apart_columns(cq_ref[:, lanes])
        upstream = apart_columns(dco_ref[:, lanes])
        dots = cross_exact_ref[lanes, :] * dcot_ref[lanes, :].astype(WIDE)
        delta = jnp.concatenate(
            [column_sums(dots[:head]), column_sums(dots[head:])], axis=1
        )
        lse = cross_lse_ref[pair : pair + 1, :]
        dcqt_ref[lanes, :] = jnp.zeros((pair_width, row_count), WIDE)

        def backward_step(step, carry):
            there = step_at(step)
            weights = jnp.exp(nn(ck_ref[there, lanes], queries_t) - lse)
            grad_weights = nn(cv_ref[there, lanes], upstream_t)
            grad_scores = (weights * (grad_weights - delta)).astype(LOW)
            ck_ref[there, lanes] = nn(grad_scores, queries).astype(LOW)
            cv_ref[there, lanes] = nn(weights.astype(LOW), upstream).astype(LOW)
            dcqt_ref[low_half, :] += nn(ckt_ref[low_half, there], grad_scores[:, :row_count])
            dcqt_ref[high_half, :] += nn(ckt_ref[high_half, there], grad_scores[:, row_count:])
            return carry

        lax.fori_loop(0, steps, backward_step, 0)
    upstream_send = refs.mixed_send

    def first_back(block, sums):
        rows = rows_at(block)
        grad_cq = (dcqt_ref[:, rows].T * score_scale).astype(LOW)
        dco_ref[rows, :] = grad_cq
        upstream = total_ref[rows, :] + nt(grad_cq, refs.w_cq[...])
        unit = unit_one_ref[rows, :]
        grad = norm_pull(unit, refs.scale_one[rows, :], gain(0), upstream)
        low = grad.astype(LOW)
        total_ref[rows, :] = grad
        low_third_ref[rows, :] = low
        grad_attended_t = nt(refs.w_out[...], low).astype(LOW)
        for h in range(HEADS):
            upstream_send[h, block] = grad_attended_t[h * head : (h + 1) * head, :]
        return (
            sums[0] + column_sums(upstream * unit),
            sums[1] + column_sums(upstream),
            sums[2] + column_sums(low),
            sums[3] + column_sums(grad_cq),
        )

    sums = lax.fori_loop(0, own_blocks, first_back, no_sums + (zeros_row,))
    few(4, sums[0])
    few(10, sums[1])
    few(9, sums[2])
    few(11, sums[3])
    up_heads_copy = Exchange(spot, upstream_send, refs.up_land, refs.up_heads_sem, all_blocks)
    up_heads_copy.start()
    turned_ref[...] = swap(low_one_ref[...])
    put_rows(piece.cross, nn(turned_ref[...], dco_ref[...]), width)
    piece.cross.steps(1)
    put_rows(piece.out, nn(attended_t_ref[...], low_third_ref[...]), 0)
    piece.out.steps(1)
    piece.up0.steps(3)
    for part in range(HEADS):
        rows = slice(part * mem_rows, (part + 1) * mem_rows)
        ckt_ref[:, rows] = swap(all_ref[part % 2, part // 2])
        grad = nt(ck_ref[rows, :], refs.w_ckv[:, :width]) + nt(cv_ref[rows, :], refs.w_ckv[:, width:])
        w_up_ref[
            (part // 2) * mem_rows : (part // 2 + 1) * mem_rows,
            (part % 2) * width : (part % 2 + 1) * width,
        ] = grad.astype(LOW)
    g_land = refs.memory_land
    other_side = pl.ds(pl.multiple_of((1 - spot.col) * width, width), width)
    own_side = pl.ds(pl.multiple_of(spot.col * width, width), width)
    memory_copy = remote(
        w_up_ref.at[:, other_side], g_land, refs.memory_sem.at[0, 0], refs.memory_sem.at[1, 0],
        spot.col_peer,
    )
    memory_copy.start()
    piece.cross.steps(2)
    piece.out.steps(2)
    put_rows(piece.ckv, nn(ckt_ref[...], ck_ref[...]), 0)
    put_rows(piece.ckv, nn(ckt_ref[...], cv_ref[...]), width)
    few(12, column_sums(cv_ref[...]))
    piece.ckv.steps(1)
    for pos in range(blocks):
        at = slice(pos * BLK, (pos + 1) * BLK)
        q_ref[at, :] = swap(jnp.concatenate([qt_ref[:, at], no_head], axis=0))
    piece.up1.steps(3)
    piece.down1.steps(3)
    up_heads_copy.wait()
    piece.ckv.steps(2)
    piece.down0.steps(3)

    upq_ref, upt_ref = refs.up, refs.upt
    dkv_ref, dqt_ref = refs.dkv, refs.dqt
    for pos in range(blocks):
        block = refs.up_land[inv_ref[pos]]
        at = slice(pos * BLK, (pos + 1) * BLK)
        upt_ref[:, at] = block
        upq_ref[at, :] = swap(jnp.concatenate([no_head, block], axis=0))
    dkv_ref[...] = jnp.zeros_like(dkv_ref)

    def backward_tile(tile, carry):
        here = pl.ds(pl.multiple_of(tile * TILE, TILE), TILE)
        queries_t = jnp.concatenate([qt_ref[:, here], no_tile], axis=0)
        upstream_t = jnp.concatenate([no_tile, upt_ref[:, here]], axis=0)
        both = jnp.concatenate([q_ref[here, :], upq_ref[here, :]], axis=0)
        lse = lse_ref[:, here]
        exact = jnp.concatenate(
            [exact_ref[tile * (TILE // BLK) + sub] for sub in range(TILE // BLK)], axis=1
        )
        delta = column_sums(exact * upt_ref[:, here].astype(WIDE))

        def chunk_step(chunk, grad_q, hide):
            there = pl.ds(pl.multiple_of(chunk * TILE, TILE), TILE)
            scores = hide(nn(kv_ref[there, :], queries_t), chunk)
            weights = jnp.exp(scores - lse)
            grad_weights = nn(kv_ref[there, :], upstream_t)
            grad_scores = (weights * (grad_weights - delta)).astype(LOW)
            sides = jnp.concatenate([grad_scores, weights.astype(LOW)], axis=1)
            spread_at = pl.ds(chunk * (TILE // BLK), TILE // BLK)
            dkv_ref[spread_at] += nn(sides, both).reshape(TILE // BLK, BLK, 2 * head)
            return grad_q + nn(kt_ref[:, there], grad_scores)

        grad_q = tile_spans(tile, chunk_step, jnp.zeros((head, TILE), WIDE))
        grad_q = (grad_q * score_scale).astype(LOW)
        for sub in range(TILE // BLK):
            dqt_ref[tile * (TILE // BLK) + sub] = grad_q[:, sub * BLK : (sub + 1) * BLK]
        return carry

    lax.fori_loop(0, tiles // 2, backward_tile, 0)
    memory_copy.wait()
    g_land[...] = plus(w_up_ref[:, own_side], g_land[...]).astype(LOW)
    memory_copies = []
    for step in range(1, ROWS):
        copy = remote(
            g_land.at[pl.ds(spot.rows_by_step[step] * mem_rows, mem_rows)], refs.memory_row.at[step - 1],
            refs.memory_sem.at[0, step], refs.memory_sem.at[1, step], spot.row_peers[step],
        )
        copy.start()
        memory_copies.append(copy)
    piece.up0.steps(4)
    piece.up1.steps(4)
    piece.down1.steps(4)
    piece.cross.steps(3)
    lax.fori_loop(tiles // 2, tiles - 2, backward_tile, 0)
    piece.down0.steps(4)
    piece.out.steps(3)
    piece.cross.steps(4)
    lax.fori_loop(tiles - 2, tiles - 1, backward_tile, 0)
    piece.out.steps(4)
    piece.ckv.steps(3)
    piece.up0.steps(5)
    piece.up1.steps(5)
    lax.fori_loop(tiles - 1, tiles, backward_tile, 0)

    piece.ckv.steps(4)
    back_send = refs.head_send
    back_copy = Exchange(
        spot, back_send, refs.head_land, refs.back_sem,
        [(0, own_blocks, slice(kind * head, (kind + 1) * head)) for kind in range(3)],
    )
    for row in range(blocks):
        back_send[row // own_blocks, row % own_blocks, :head] = dqt_ref[deal_ref[row]]
    back_copy.start(0)
    for row in range(blocks):
        back_send[row // own_blocks, row % own_blocks, head:] = dkv_ref[deal_ref[row]].T.astype(LOW)
    back_copy.start(1)
    back_copy.start(2)

    ones = jnp.ones((8, BLK), LOW)
    query_sums = jnp.zeros((8, head), WIDE)
    both_sums = jnp.zeros((1, 2 * head), WIDE)
    for pos in range(blocks):
        query_sums = query_sums + nt(ones, dqt_ref[pos])
        both_sums = both_sums + column_sums(dkv_ref[pos])
    own_lanes = lax.broadcasted_iota(jnp.int32, (1, width), 1) // head == spot.ctx
    few(7, jnp.where(own_lanes, jnp.concatenate([query_sums[:1]] * HEADS, axis=1), 0.0))
    few(8, jnp.where(own_lanes, jnp.concatenate([both_sums[:, head:]] * HEADS, axis=1), 0.0))

    def few_copy(step):
        return remote(
            few_ref.at[step], refs.few_land.at[step],
            refs.few_sem.at[0, step], refs.few_sem.at[1, step], spot.few_peers[step],
        )

    few_copy(0).start()
    finishing = [
        (piece.down1, piece.down0), (piece.cross, piece.out), (piece.ckv,), (), (),
    ]
    for step in range(5):
        for item in finishing[step]:
            item.steps(5)
        few_copy(step).wait()
        total = few_ref[step] + refs.few_land[step]
        if step < 4:
            few_ref[step + 1] = total
            few_copy(step + 1).start()
        else:
            refs.few_total[...] = total
    own_shard = spot.ctx * 2 + spot.wsh
    total = refs.few_total[...]
    part, long_part = width // SHARDS, hidden_width // SHARDS
    picked, long_picked = total[:, :part], total[:1, :long_part]
    for shard in range(1, SHARDS):
        picked = jnp.where(own_shard == shard, total[:, shard * part : (shard + 1) * part], picked)
        row, at = divmod(shard * long_part, width)
        long_picked = jnp.where(
            own_shard == shard, total[row : row + 1, at : at + long_part], long_picked
        )
    o_b_up_ref[...] = long_picked
    o_gains_ref[...] = picked[4:7]
    o_biases_ref[...] = picked[7:17]
    for copy in memory_copies:
        copy.wait()
    total = g_land[pl.ds(spot.row * mem_rows, mem_rows), :].astype(WIDE)
    for step in range(ROWS - 1):
        total = total + refs.memory_row[step].astype(WIDE)
    g_memory_ref[...] = total
    for item in ups + downs + (piece.cross, piece.out, piece.ckv):
        item.steps(6)

    turned_ref[...] = swap(tokens_ref[...])
    kinds = (piece.wq, piece.wk, piece.wv)
    for kind in range(3):
        back_copy.wait(kind)
        for block in range(own_blocks):
            turned = jnp.concatenate(
                [
                    refs.head_land[h * own_blocks + block, kind * head : (kind + 1) * head, :]
                    for h in range(HEADS)
                ],
                axis=0,
            )
            hidden_ref[kind, block * BLK : (block + 1) * BLK, :] = swap(turned)
        put_rows(kinds[kind], nn(turned_ref[...], hidden_ref[kind]), 0)
        kinds[kind].steps(1)
        if kind > 0:
            kinds[kind - 1].steps(2)
    grad_stream = total_ref[...]
    for kind in range(3):
        if kind == 1:
            kinds[2].steps(2)
        lanes = slice(kind * width, (kind + 1) * width)
        grad_stream = grad_stream + nt(hidden_ref[kind], refs.w_qkv[:, lanes])
    g_stream_ref[...] = grad_stream
    for stage in (3, 5, 6):
        for item in kinds:
            item.steps(stage)


def layer_scratch(row_count, width, hidden_width, mem_rows):
    own_blocks = row_count // BLK
    blocks = own_blocks * HEADS
    head = width // HEADS
    tokens = blocks * BLK
    mem_total = mem_rows * HEADS
    dma = pltpu.SemaphoreType.DMA
    scratch = dict(
        w_qkv=((width, 3 * width), LOW), w_ckv=((width, 2 * width), LOW),
        w_out=((width, width), LOW), w_cq=((width, width), LOW),
        w_cout=((width, width), LOW), w_up=((width, hidden_width), LOW),
        w_down=((hidden_width, width), LOW),
        head_send=((HEADS, own_blocks, 3 * head, BLK), LOW),
        head_land=((blocks, 3 * head, BLK), LOW),
        memory_all=((2, ROWS, mem_rows, width), LOW),
        q=((tokens, 2 * head), LOW), kv=((tokens, 2 * head), LOW),
        qt=((head, tokens), LOW), kt=((head, tokens), LOW), vt=((head, tokens), LOW),
        exact=((blocks, head, BLK), WIDE), lse=((1, tokens), WIDE),
        mixed_send=((HEADS, own_blocks, head, BLK), LOW),
        mixed_land=((blocks, head, BLK), LOW),
        ck=((mem_total, width), LOW), cv=((mem_total, width), LOW),
        ckt=((width, mem_total), LOW), cvt=((width, mem_total), LOW),
        attended_t=((width, row_count), LOW),
        unit_one=((row_count, width), WIDE), unit_two=((row_count, width), WIDE),
        scale_one=((row_count, 1), WIDE), scale_two=((row_count, 1), WIDE),
        low_one=((row_count, width), LOW), low_two=((row_count, width), LOW),
        cq=((row_count, width), LOW), cqt=((width, row_count), LOW),
        cross_exact=((width, row_count), WIDE),
        cross_lse=((HEADS // 2, 2 * row_count), WIDE),
        cross_low=((row_count, width), LOW),
        hidden=((hidden_width // width, row_count, width), LOW),
        slope=((hidden_width // width, row_count, width), LOW),
        low_third=((row_count, width), LOW),
        turned=((width, row_count), LOW),
        dco=((row_count, width), LOW), dcot=((width, row_count), LOW),
        dcqt=((width, row_count), WIDE),
        memory_land=((ROWS * mem_rows, width), LOW),
        memory_row=((ROWS - 1, mem_rows, width), LOW),
        up_land=((blocks, head, BLK), LOW),
        up=((tokens, 2 * head), LOW), upt=((head, tokens), LOW),
        dkv=((blocks, BLK, 2 * head), WIDE), dqt=((blocks, head, BLK), LOW),
        few_sum=((5, FEW_ROWS, width), WIDE), few_land=((5, FEW_ROWS, width), WIDE),
        few_total=((FEW_ROWS, width), WIDE),
    )
    out = {name: pltpu.VMEM(shape, kind) for name, (shape, kind) in scratch.items()}
    out.update(
        load_sem=dma((7,)), to_heads_sem=dma((2, HEADS, 3)), from_heads_sem=dma((2, HEADS, 1)),
        up_heads_sem=dma((2, HEADS, 1)), back_sem=dma((2, HEADS, 3)), spread_sem=dma((2, ROWS)),
        inverse=pltpu.SMEM((blocks,), jnp.int32),
        memory_sem=dma((2, ROWS)), few_sem=dma((2, 5)),
    )
    out.update(
        pieces={
            name: dict(
                part=pltpu.VMEM((2, ROWS, 2, 2, HALF, span), LOW),
                core_land=pltpu.VMEM((ROWS, 2, 2, HALF, span), LOW),
                hop_land=pltpu.VMEM(
                    (3, ROWS, HALF, span) if TURNS[name] == 2 else (ROWS, 2, HALF, span), LOW
                ),
                turn_land=pltpu.VMEM((ROWS, HALF, span), LOW),
                row_land=pltpu.VMEM((ROWS - 1, HALF, span), LOW),
                sems=dma((2, 9)),
            )
            for name, span in PIECES.items()
        }
    )
    return out


def layer_call(deal_ids, offsets, opened, tokens, memory, cotangent, weights, b_up, gains, biases, prompt_blocks):
    row_count, width = tokens.shape
    hidden_width = b_up.shape[1]
    mem_rows = memory.shape[0]
    smem = pl.BlockSpec(memory_space=pltpu.SMEM)
    vmem = pl.BlockSpec(memory_space=pltpu.VMEM)
    hbm = pl.BlockSpec(memory_space=pl.ANY)
    scratch = layer_scratch(row_count, width, hidden_width, mem_rows)
    leaves, tree = jax.tree.flatten(scratch, is_leaf=lambda leaf: not isinstance(leaf, dict))
    out_shapes = [
        (row_count, width), (row_count, width), (mem_rows, width),
        (32, 3 * width), (32, width), (32, width), (32, 2 * width), (32, width),
        (32, hidden_width), (hidden_width // SHARDS, width),
        (1, hidden_width // SHARDS), (3, width // SHARDS), (10, width // SHARDS),
    ]

    def body(*args):
        count = len(args) - len(leaves)
        refs = Bag(jax.tree.unflatten(tree, args[count:]))
        layer_kernel(prompt_blocks, *args[:count], refs)

    return pl.pallas_call(
        body,
        out_shape=[jax.ShapeDtypeStruct(shape, WIDE) for shape in out_shapes],
        in_specs=[smem] * 3 + [vmem] * 3 + [hbm] * 7 + [vmem] * 3,
        out_specs=[vmem] * len(out_shapes),
        scratch_shapes=leaves,
        compiler_params=pltpu.CompilerParams(
            collective_id=0, has_side_effects=True, vmem_limit_bytes=BIG_VMEM
        ),
        name="layer",
    )(deal_ids, offsets, opened, tokens, memory, cotangent, *weights, b_up, gains, biases)


def hand_out_kernel(count, *refs):
    for index in range(count):
        refs[count + index][...] = refs[index][...]


def hand_out(arrays):
    count = len(arrays)
    vmem = pl.BlockSpec(memory_space=pltpu.VMEM)
    return pl.pallas_call(
        functools.partial(hand_out_kernel, count),
        out_shape=[jax.ShapeDtypeStruct(a.shape, a.dtype) for a in arrays],
        in_specs=[vmem] * count,
        out_specs=[vmem] * count,
        compiler_params=pltpu.CompilerParams(vmem_limit_bytes=BIG_VMEM),
        name="hand_out",
    )(*arrays)


def layer_shards(
    stream, memory, cotangent, deal_order, offsets, context_mask,
    w_qkv, w_out, w_cq, w_ckv, w_cout, w_up, w_down, b_up, gains, biases,
):
    results = layer_call(
        deal_order[0, 0], offsets[0, 0], context_mask[0, 0],
        stream[0, 0], memory[0, 0], cotangent[0, 0],
        (w_qkv, w_out, w_cq, w_ckv, w_cout, w_up, w_down),
        b_up[None, :], gains, biases, context_mask.shape[3],
    )
    output, grad_stream, grad_memory, *grads = hand_out(results)
    grads[7] = grads[7].reshape(-1)
    return (output[None, None], grad_stream[None, None], grad_memory[None, None], *grads)


def gelu_exact(values):
    return jax.nn.gelu(values, approximate=False)


def norm_rows(values, gain_vec, shift_vec):
    center = values - jnp.mean(values, axis=-1, keepdims=True)
    spread = jnp.mean(center * center, axis=-1, keepdims=True)
    return center * lax.rsqrt(spread + EPS_NORM) * gain_vec + shift_vec


def norm_back(values, gain_vec, shift_vec, upstream):
    _, pullback = jax.vjp(norm_rows, values, gain_vec, shift_vec)
    return pullback(upstream)


def seq_index(positions, prompt_len, cont_len):
    later = jnp.int32(1) + (positions - jnp.int32(prompt_len)) // jnp.int32(cont_len)
    return jnp.where(positions < prompt_len, jnp.zeros_like(later), later)


def visible(query_pos, key_ids, offsets, context_mask, block_len, prompt_blocks, cont_blocks):
    prompt_len = prompt_blocks * block_len
    cont_len = cont_blocks * block_len
    cont_count = offsets.shape[0]
    key_pos = (
        key_ids[:, None] * jnp.int32(block_len) + jnp.arange(block_len, dtype=jnp.int32)[None, :]
    ).reshape(-1)
    query_seq = seq_index(query_pos, prompt_len, cont_len)
    key_seq = seq_index(key_pos, prompt_len, cont_len)
    inside = (query_seq[:, None] == key_seq[None, :]) & (key_pos[None, :] <= query_pos[:, None])
    cont_pick = jnp.clip(query_seq - 1, 0, cont_count - 1)
    prompt_limit = jnp.take(offsets, cont_pick)
    query_block = jnp.clip(
        (query_pos - jnp.int32(prompt_len)) // jnp.int32(block_len), 0, cont_count * cont_blocks - 1
    )
    mask_rows = jnp.take(context_mask, query_block, axis=0)
    key_block = jnp.clip(key_ids, 0, prompt_blocks - 1)
    block_open = jnp.take(mask_rows, key_block, axis=1) > 0
    block_open = jnp.repeat(block_open, block_len, axis=1) | (key_pos[None, :] < block_len)
    from_prompt = (
        (query_seq[:, None] > 0)
        & (key_seq[None, :] == 0)
        & (key_pos[None, :] < prompt_limit[:, None])
        & block_open
    )
    return inside | from_prompt


def dot_first(left, right):
    return lax.dot_general(
        left, right, (((0,), (0,)), ((), ())), preferred_element_type=jnp.float32
    )


def dot_last(left, right):
    return lax.dot_general(
        left, right, (((1,), (1,)), ((), ())), preferred_element_type=jnp.float32
    )


def to_heads(matrix, head_count):
    row_count, model_width = matrix.shape
    return matrix.reshape(row_count, head_count, model_width // head_count).transpose(1, 0, 2)


def from_heads(stacked):
    head_count, row_count, head_width = stacked.shape
    return stacked.transpose(1, 0, 2).reshape(row_count, head_count * head_width)


def pair_heads(key_rows, value_rows, head_count):
    return jnp.concatenate(
        [to_heads(key_rows, head_count), to_heads(value_rows, head_count)], axis=2
    )


def head_scores(queries, key_rows, allowed):
    score_scale = queries.shape[1] ** (-0.5)
    scores = dot_last(queries, key_rows) * score_scale
    if allowed is not None:
        scores = jnp.where(allowed, scores, NEG_FILL)
    return scores


def head_forward(queries, keyval, allowed):
    head_width = queries.shape[1]
    scores = head_scores(queries, keyval[:, :head_width], allowed)
    row_top = jnp.max(scores, axis=1, keepdims=True)
    exp_scores = jnp.exp(scores - row_top)
    row_total = jnp.sum(exp_scores, axis=1, keepdims=True)
    soft_weights = (exp_scores / row_total).astype(jnp.bfloat16)
    mixed_heads = jnp.dot(soft_weights, keyval[:, head_width:], preferred_element_type=jnp.float32)
    return (mixed_heads, row_top + jnp.log(row_total))


def head_backward(queries, keyval, upstream, log_total, allowed):
    head_width = queries.shape[1]
    score_scale = head_width ** (-0.5)
    key_rows = keyval[:, :head_width]
    scores = head_scores(queries, key_rows, allowed)
    soft_weights = jnp.exp(scores - log_total)
    grad_soft = dot_last(upstream, keyval[:, head_width:])
    row_delta = jnp.sum(soft_weights * grad_soft, axis=1, keepdims=True)
    grad_scores = (soft_weights * (grad_soft - row_delta)).astype(jnp.bfloat16)
    grad_query = jnp.dot(grad_scores, key_rows, preferred_element_type=jnp.float32) * score_scale
    grad_keys = dot_first(grad_scores, queries) * score_scale
    grad_values = dot_first(soft_weights.astype(jnp.bfloat16), upstream)
    return (grad_query, jnp.concatenate([grad_keys, grad_values], axis=1))


def shards(
    stream,
    memory,
    cotangent,
    deal_order,
    offsets,
    context_mask,
    w_qkv,
    w_out,
    w_cq,
    w_ckv,
    w_cout,
    w_up,
    w_down,
    b_up,
    gains,
    biases,
):
    tokens = stream[0, 0]
    row_count, model_width = tokens.shape
    head_width = model_width // HEADS
    deal_ids = deal_order[0, 0]
    prompt_blocks = context_mask.shape[3]
    own_blocks = row_count // BLK
    own_ids = lax.dynamic_slice_in_dim(deal_ids, lax.axis_index("ctx") * own_blocks, own_blocks)
    query_pos = (
        own_ids[:, None] * jnp.int32(BLK) + jnp.arange(BLK, dtype=jnp.int32)[None, :]
    ).reshape(-1)
    allowed = visible(
        query_pos, deal_ids, offsets[0, 0], context_mask[0, 0], BLK, prompt_blocks, CBLK
    )
    zeros_row = jnp.zeros((model_width,), jnp.float32)
    projected = (
        jnp.dot(tokens, w_qkv, preferred_element_type=jnp.float32)
        + jnp.concatenate([biases[0], zeros_row, biases[1]])
    ).astype(jnp.bfloat16)
    query_heads = to_heads(projected[:, :model_width], HEADS)
    keyval_own = pair_heads(
        projected[:, model_width : 2 * model_width], projected[:, 2 * model_width :], HEADS
    )
    keyval_all = lax.all_gather(keyval_own, "ctx", axis=1, tiled=True)

    def self_forward(pieces):
        return head_forward(pieces[0], pieces[1], allowed)

    self_out, self_lse = lax.map(self_forward, (query_heads, keyval_all))
    attended = from_heads(self_out).astype(jnp.bfloat16)
    first_sum = (
        tokens.astype(jnp.float32)
        + jnp.dot(attended, w_out, preferred_element_type=jnp.float32)
        + biases[2]
    )
    normed_one = norm_rows(first_sum, gains[0], biases[3])
    normed_low = normed_one.astype(jnp.bfloat16)
    cross_query = (
        jnp.dot(normed_low, w_cq, preferred_element_type=jnp.float32) + biases[4]
    ).astype(jnp.bfloat16)
    cross_bias = jnp.concatenate([zeros_row, biases[5]])
    memory_own = memory[0, 0]
    memory_all = lax.all_gather(memory_own, "ctx", axis=0, tiled=True)
    cross_kv = (jnp.dot(memory_all, w_ckv, preferred_element_type=jnp.float32) + cross_bias).astype(
        jnp.bfloat16
    )
    cross_heads = pair_heads(cross_kv[:, :model_width], cross_kv[:, model_width:], HEADS)
    cross_query_heads = to_heads(cross_query, HEADS)

    def cross_forward(pieces):
        return head_forward(pieces[0], pieces[1], None)

    cross_out, cross_lse = lax.map(cross_forward, (cross_query_heads, cross_heads))
    cross_attended = from_heads(cross_out).astype(jnp.bfloat16)
    second_sum = (
        normed_one + jnp.dot(cross_attended, w_cout, preferred_element_type=jnp.float32) + biases[6]
    )
    normed_two = norm_rows(second_sum, gains[1], biases[7])
    normed_two_low = normed_two.astype(jnp.bfloat16)
    hidden_pre = jnp.dot(normed_two_low, w_up, preferred_element_type=jnp.float32) + b_up
    hidden = gelu_exact(hidden_pre).astype(jnp.bfloat16)
    third_sum = normed_two + jnp.dot(hidden, w_down, preferred_element_type=jnp.float32) + biases[8]
    output = norm_rows(third_sum, gains[2], biases[9])
    grad_third, grad_gain_three, grad_shift_three = norm_back(
        third_sum, gains[2], biases[9], cotangent[0, 0].astype(jnp.float32)
    )
    grad_down_in = grad_third.astype(jnp.bfloat16)
    grad_w_down = dot_first(hidden, grad_down_in)
    grad_b_down = jnp.sum(grad_down_in.astype(jnp.float32), axis=0)
    grad_hidden = dot_last(grad_down_in, w_down)
    _, gelu_pull = jax.vjp(gelu_exact, hidden_pre)
    grad_pre = gelu_pull(grad_hidden)[0].astype(jnp.bfloat16)
    grad_w_up = dot_first(normed_two_low, grad_pre)
    grad_b_up = jnp.sum(grad_pre.astype(jnp.float32), axis=0)
    grad_normed_two = grad_third + dot_last(grad_pre, w_up)
    grad_second, grad_gain_two, grad_shift_two = norm_back(
        second_sum, gains[1], biases[7], grad_normed_two
    )
    grad_cross_in = grad_second.astype(jnp.bfloat16)
    grad_w_cout = dot_first(cross_attended, grad_cross_in)
    grad_b_co = jnp.sum(grad_cross_in.astype(jnp.float32), axis=0)
    grad_cross_heads = to_heads(dot_last(grad_cross_in, w_cout).astype(jnp.bfloat16), HEADS)

    def cross_backward(pieces):
        return head_backward(pieces[0], pieces[1], pieces[2], pieces[3], None)

    grad_cq_heads, grad_ckv_all = lax.map(
        cross_backward, (cross_query_heads, cross_heads, grad_cross_heads, cross_lse)
    )
    grad_ckv_own = lax.psum_scatter(
        grad_ckv_all.astype(jnp.bfloat16), "ctx", scatter_dimension=1, tiled=True
    )
    grad_cv = from_heads(grad_ckv_own[:, :, head_width:])
    grad_ckv = jnp.concatenate([from_heads(grad_ckv_own[:, :, :head_width]), grad_cv], axis=1)
    grad_w_ckv = dot_first(memory_own, grad_ckv)
    grad_b_cv = jnp.sum(grad_cv.astype(jnp.float32), axis=0)
    grad_memory = dot_last(grad_ckv, w_ckv)
    grad_cq = from_heads(grad_cq_heads).astype(jnp.bfloat16)
    grad_w_cq = dot_first(normed_low, grad_cq)
    grad_b_cq = jnp.sum(grad_cq.astype(jnp.float32), axis=0)
    grad_normed_one = grad_second + dot_last(grad_cq, w_cq)
    grad_first, grad_gain_one, grad_shift_one = norm_back(
        first_sum, gains[0], biases[3], grad_normed_one
    )
    grad_att_in = grad_first.astype(jnp.bfloat16)
    grad_w_out = dot_first(attended, grad_att_in)
    grad_b_o = jnp.sum(grad_att_in.astype(jnp.float32), axis=0)
    grad_self_heads = to_heads(dot_last(grad_att_in, w_out).astype(jnp.bfloat16), HEADS)

    def self_backward(pieces):
        return head_backward(pieces[0], pieces[1], pieces[2], pieces[3], allowed)

    grad_q_heads, grad_kv_all = lax.map(
        self_backward, (query_heads, keyval_all, grad_self_heads, self_lse)
    )
    grad_kv_own = lax.psum_scatter(
        grad_kv_all.astype(jnp.bfloat16), "ctx", scatter_dimension=1, tiled=True
    )
    grad_values = from_heads(grad_kv_own[:, :, head_width:])
    grad_queries = from_heads(grad_q_heads).astype(jnp.bfloat16)
    grad_proj = jnp.concatenate(
        [grad_queries, from_heads(grad_kv_own[:, :, :head_width]), grad_values], axis=1
    )
    grad_w_qkv = dot_first(tokens, grad_proj)
    grad_b_q = jnp.sum(grad_queries.astype(jnp.float32), axis=0)
    grad_b_v = jnp.sum(grad_values.astype(jnp.float32), axis=0)
    grad_tokens = grad_first + dot_last(grad_proj, w_qkv)
    gain_grads = jnp.stack([grad_gain_one, grad_gain_two, grad_gain_three])
    shift_grads = jnp.stack(
        [
            grad_b_q,
            grad_b_v,
            grad_b_o,
            grad_shift_one,
            grad_b_cq,
            grad_b_cv,
            grad_b_co,
            grad_shift_two,
            grad_b_down,
            grad_shift_three,
        ]
    )
    (
        part_qkv,
        part_out,
        part_cq,
        part_ckv,
        part_cout,
        part_up,
        part_down,
        part_b_up,
        part_gains,
        part_biases,
    ) = (
        lax.psum_scatter(grad_w_qkv, ("ctx", "wsh"), scatter_dimension=0, tiled=True),
        lax.psum_scatter(grad_w_out, ("ctx", "wsh"), scatter_dimension=0, tiled=True),
        lax.psum_scatter(grad_w_cq, ("ctx", "wsh"), scatter_dimension=0, tiled=True),
        lax.psum_scatter(grad_w_ckv, ("ctx", "wsh"), scatter_dimension=0, tiled=True),
        lax.psum_scatter(grad_w_cout, ("ctx", "wsh"), scatter_dimension=0, tiled=True),
        lax.psum_scatter(grad_w_up, ("ctx", "wsh"), scatter_dimension=0, tiled=True),
        lax.psum_scatter(grad_w_down, ("ctx", "wsh"), scatter_dimension=0, tiled=True),
        lax.psum_scatter(grad_b_up, ("ctx", "wsh"), scatter_dimension=0, tiled=True),
        lax.psum_scatter(gain_grads, ("ctx", "wsh"), scatter_dimension=1, tiled=True),
        lax.psum_scatter(shift_grads, ("ctx", "wsh"), scatter_dimension=1, tiled=True),
    )
    (
        total_qkv,
        total_out,
        total_cq,
        total_ckv,
        total_cout,
        total_up,
        total_down,
        total_b_up,
        total_gains,
        total_biases,
    ) = (
        lax.psum(part_qkv.astype(jnp.bfloat16), "grp").astype(jnp.float32),
        lax.psum(part_out.astype(jnp.bfloat16), "grp").astype(jnp.float32),
        lax.psum(part_cq.astype(jnp.bfloat16), "grp").astype(jnp.float32),
        lax.psum(part_ckv.astype(jnp.bfloat16), "grp").astype(jnp.float32),
        lax.psum(part_cout.astype(jnp.bfloat16), "grp").astype(jnp.float32),
        lax.psum(part_up.astype(jnp.bfloat16), "grp").astype(jnp.float32),
        lax.psum(part_down.astype(jnp.bfloat16), "grp").astype(jnp.float32),
        lax.psum(part_b_up.astype(jnp.bfloat16), "grp").astype(jnp.float32),
        lax.psum(part_gains.astype(jnp.bfloat16), "grp").astype(jnp.float32),
        lax.psum(part_biases.astype(jnp.bfloat16), "grp").astype(jnp.float32),
    )
    return (
        output[None, None],
        grad_tokens[None, None],
        grad_memory[None, None],
        total_qkv,
        total_out,
        total_cq,
        total_ckv,
        total_cout,
        total_up,
        total_down,
        total_b_up,
        total_gains,
        total_biases,
    )


def solution(mesh):
    in_specs = (
        P("grp", "wsh", "ctx", None),
        P("grp", "wsh", "ctx", None),
        P("grp", "wsh", "ctx", None),
        P("grp", "wsh", None),
        P("grp", "wsh", None),
        P("grp", "wsh", None, None),
        P(),
        P(),
        P(),
        P(),
        P(),
        P(),
        P(),
        P(),
        P(),
        P(),
    )
    out_specs = (
        P("grp", "wsh", "ctx", None),
        P("grp", "wsh", "ctx", None),
        P("grp", "wsh", "ctx", None),
        P(("ctx", "wsh"), None),
        P(("ctx", "wsh"), None),
        P(("ctx", "wsh"), None),
        P(("ctx", "wsh"), None),
        P(("ctx", "wsh"), None),
        P(("ctx", "wsh"), None),
        P(("ctx", "wsh"), None),
        P(("ctx", "wsh")),
        P(None, ("ctx", "wsh")),
        P(None, ("ctx", "wsh")),
    )
    body = layer_shards if mesh.shape["ctx"] == HEADS else shards
    return jax.shard_map(body, mesh=mesh, in_specs=in_specs, out_specs=out_specs, check_vma=False)
```

```python
import functools

import jax
import jax.numpy as jnp
from jax import lax
from jax.experimental import pallas as pl
from jax.experimental.pallas import tpu as pltpu
from jax.sharding import PartitionSpec as P

HEADS = 8
BLK = 128
CBLK = 16


NEG_FILL = -1000000000.0
EPS_NORM = 1e-05


MESH_ID = pl.DeviceIdType.MESH
TILE = 512
STEP = 256
KEYS = 1024
BIG_VMEM = 62 << 20
LOW = jnp.bfloat16
WIDE = jnp.float32
SHARDS = 16
HALF = 16
ROWS = 4
PIECES = dict(
    up0=1024, up1=1024, down0=1024, down1=1024, cross=1024, out=512, ckv=1024, wq=512, wk=512, wv=512
)
TURNS = dict(up0=0, up1=1, down0=0, down1=1, cross=0, out=0, ckv=0, wq=2, wk=2, wv=2)
FEW_ROWS = 24


def nn(left, right):
    return lax.dot_general(
        left, right, (((1,), (0,)), ((), ())), preferred_element_type=WIDE
    )


def nt(left, right):
    return lax.dot_general(
        left, right, (((1,), (1,)), ((), ())), preferred_element_type=WIDE
    )


def swap(block):
    return block.astype(WIDE).T.astype(block.dtype)


def plus(left, right):
    return left.astype(WIDE) + right.astype(WIDE)


def column_sums(values):
    return jnp.sum(values.astype(WIDE), axis=0, keepdims=True)


def norm_parts(values):
    center = values - jnp.mean(values, axis=-1, keepdims=True)
    spread = jnp.mean(center * center, axis=-1, keepdims=True)
    scale = lax.rsqrt(spread + EPS_NORM)
    return center * scale, scale


def norm_pull(unit, scale, gain, upstream):
    inner = upstream * gain
    first = jnp.mean(inner, axis=-1, keepdims=True)
    second = jnp.mean(inner * unit, axis=-1, keepdims=True)
    return scale * (inner - first - unit * second)


def hide_later(scores, lead):
    rows = lax.broadcasted_iota(jnp.int32, scores.shape, 0)
    cols = lax.broadcasted_iota(jnp.int32, scores.shape, 1)
    return jnp.where(rows - cols <= lead, scores, NEG_FILL)


def hide_prompt(scores, offset_ref, open_ref, tile, chunk, prompt_blocks):
    span, key_span = TILE // BLK, scores.shape[0] // BLK
    rows = lax.broadcasted_iota(jnp.int32, (BLK, BLK), 0)
    columns = []
    for q_sub in range(span):
        pieces = []
        for k_sub in range(key_span):
            key_block = chunk * key_span + k_sub
            opened = open_ref[tile * span + q_sub - prompt_blocks, key_block]
            opened = jnp.where(key_block == 0, 1, opened)
            limit = jnp.where(opened > 0, offset_ref[0], 0) - key_block * BLK
            part = scores[k_sub * BLK : (k_sub + 1) * BLK, q_sub * BLK : (q_sub + 1) * BLK]
            pieces.append(jnp.where(rows < limit, part, NEG_FILL))
        columns.append(jnp.concatenate(pieces, axis=0))
    return jnp.concatenate(columns, axis=1)


def apart(upper, lower):
    none = jnp.zeros_like(upper)
    return jnp.concatenate(
        [jnp.concatenate([upper, none], axis=1), jnp.concatenate([none, lower], axis=1)], axis=0
    )


def apart_columns(pair):
    lanes = lax.broadcasted_iota(jnp.int32, pair.shape, 1)
    wide = pair.astype(WIDE)
    left = jnp.where(lanes < pair.shape[1] // 2, wide, 0.0).astype(pair.dtype)
    right = jnp.where(lanes < pair.shape[1] // 2, 0.0, wide).astype(pair.dtype)
    return jnp.concatenate([left, right], axis=0)


def remote(src_ref, dst_ref, send_sem, recv_sem, target):
    return pltpu.make_async_remote_copy(
        src_ref=src_ref,
        dst_ref=dst_ref,
        send_sem=send_sem,
        recv_sem=recv_sem,
        device_id=target,
        device_id_type=MESH_ID,
    )


class Bag:
    def __init__(self, items):
        self.__dict__.update(items)


class Spot:
    def __init__(self):
        ctx = lax.axis_index("ctx")
        self.grp, self.ctx, self.wsh = lax.axis_index("grp"), ctx, lax.axis_index("wsh")
        self.row, self.col = ctx // 2, lax.rem(ctx, 2)
        self.core_peer = (1 - self.grp, ctx, self.wsh)
        self.wsh_peer = (self.grp, ctx, 1 - self.wsh)
        self.col_peer = self.at_row_col(self.row, 1 - self.col)
        self.cross_peer = (self.grp, self.row * 2 + 1 - self.col, 1 - self.wsh)
        self.rows_by_step = [lax.rem(self.row + step, ROWS) for step in range(ROWS)]
        self.row_peers = [self.at_row_col(row, self.col) for row in self.rows_by_step]
        self.far_peers = [(1 - self.grp, peer[1], self.wsh) for peer in self.row_peers]
        self.ways = [
            (self.wsh_peer, self.col, 1 - self.wsh),
            (self.col_peer, 1 - self.col, self.wsh),
            (self.cross_peer, 1 - self.col, 1 - self.wsh),
        ]
        self.ctx_by_step = [lax.rem(ctx + step, HEADS) for step in range(HEADS)]
        self.ctx_peers = [(self.grp, peer, self.wsh) for peer in self.ctx_by_step]

    def at_row_col(self, row, col):
        return (self.grp, row * 2 + col, self.wsh)

    def greet(self):
        barrier = pltpu.get_barrier_semaphore()
        targets = [self.core_peer, self.wsh_peer, self.cross_peer]
        targets += self.ctx_peers[1:] + self.far_peers[1:]
        for target in targets:
            pl.semaphore_signal(barrier, inc=1, device_id=target, device_id_type=MESH_ID)
        return len(targets)


class Exchange:
    def __init__(self, spot, source, sems, parts):
        self.spot, self.source, self.sems, self.parts = spot, source, sems, parts
        self.copies = [[] for _ in parts]

    def start(self, part=0):
        spot, own_blocks = self.spot, self.source.shape[1]
        first, count, rows, target, target_rows = self.parts[part]
        here = (pl.ds(spot.ctx * own_blocks + first, count), target_rows)
        there = (pl.ds(first, count), rows)
        for step in range(1, HEADS):
            copy = remote(
                self.source.at[(spot.ctx_by_step[step],) + there], target.at[here],
                self.sems.at[0, step, part], self.sems.at[1, step, part], spot.ctx_peers[step],
            )
            copy.start()
            self.copies[part].append(copy)
        target[here] = self.source[(spot.ctx,) + there]

    def wait(self, part=0):
        for copy in self.copies[part]:
            copy.wait()


class Piece:
    def __init__(self, spot, turn, refs, outs):
        self.spot, self.turn, self.sems, self.outs = spot, turn, refs.sems, outs
        self.part, self.core_land, self.hop_land = refs.part, refs.core_land, refs.hop_land
        self.turn_land, self.row_land = refs.turn_land, refs.row_land
        self.turn_sum = self.core_land.at[:, 0]
        self.copies = []
        self.stage = 0

    def copy(self, index, source, target_ref, target):
        copy = remote(source, target_ref, self.sems.at[0, index], self.sems.at[1, index], target)
        copy.start()
        self.copies.append(copy)

    def finish(self):
        for copy in self.copies:
            copy.wait()
        self.copies = []

    def send_rows(self):
        spot = self.spot
        for step in range(1, ROWS):
            self.copy(
                2 + step, self.turn_land.at[spot.rows_by_step[step]],
                self.row_land.at[step - 1], spot.row_peers[step],
            )

    def steps(self, stage):
        while self.stage < stage:
            self.step()

    def step(self):
        spot, part = self.spot, self.part
        own = spot.grp
        if self.stage == 0:
            self.copy(0, part.at[1 - own], self.core_land, spot.core_peer)
        elif self.stage == 1:
            self.finish()
            part[own] = plus(part[own], self.core_land[...]).astype(LOW)
            if self.turn == 2:
                for way, (target, to_col, to_wsh) in enumerate(spot.ways):
                    self.copy(
                        1 + way, part.at[own, :, to_col, to_wsh], self.hop_land.at[way],
                        target,
                    )
            elif self.turn == 0:
                self.copy(1, part.at[own, :, :, 1 - spot.wsh], self.hop_land, spot.wsh_peer)
            else:
                self.copy(1, part.at[own, :, 1 - spot.col], self.hop_land, spot.col_peer)
        elif self.stage == 2:
            self.finish()
            if self.turn == 2:
                total = part[own, :, spot.col, spot.wsh].astype(WIDE)
                for way in range(3):
                    total = total + self.hop_land[way].astype(WIDE)
                self.turn_land[...] = total.astype(LOW)
                self.row_land[own, spot.row] = self.turn_land[spot.row]
                for step in range(ROWS):
                    for side, peers in enumerate((spot.row_peers, spot.far_peers)):
                        if step + side > 0:
                            self.copy(
                                4 + 2 * step + side, self.turn_land.at[spot.rows_by_step[step]],
                                self.row_land.at[own, spot.row], peers[step],
                            )
                self.stage = 4
                return
            if self.turn == 0:
                mine = part[own, :, :, spot.wsh]
                away, target = 1 - spot.col, spot.col_peer
            else:
                mine = part[own, :, spot.col]
                away, target = 1 - spot.wsh, spot.wsh_peer
            self.turn_sum[...] = plus(mine, self.hop_land[...]).astype(LOW)
            self.copy(2, self.turn_sum.at[:, away], self.turn_land, target)
        elif self.stage == 3:
            self.finish()
            keep = spot.col if self.turn == 0 else spot.wsh
            self.turn_land[...] = plus(self.turn_sum[:, keep], self.turn_land[...]).astype(LOW)
            self.send_rows()
        elif self.stage == 4:
            self.finish()
            if self.turn == 2:
                (out_ref, _, column, width), = self.outs
                for half in range(2):
                    total = self.row_land[half, 0].astype(WIDE)
                    for row in range(1, ROWS):
                        total = total + self.row_land[half, row].astype(WIDE)
                    out_ref[half * HALF : (half + 1) * HALF, column : column + width] = total
                self.stage = 6
                return
            total = self.turn_land[spot.row].astype(WIDE)
            for step in range(ROWS - 1):
                total = total + self.row_land[step].astype(WIDE)
            at = 0
            for index, (out_ref, row, column, width) in enumerate(self.outs):
                here = (
                    pl.ds(pl.multiple_of(row + own * HALF, HALF), HALF),
                    slice(column, column + width),
                )
                out_ref[here] = total[:, at : at + width]
                at += width
                self.copy(7 + index, out_ref.at[here], out_ref.at[here], spot.core_peer)
        elif self.stage == 5:
            self.finish()
        self.stage += 1


def layer_kernel(
    prompt_blocks,
    deal_ref, offset_ref, open_ref, tokens_ref, memory_ref, cot_ref,
    w_qkv_hbm, w_out_hbm, w_cq_hbm, w_ckv_hbm, w_cout_hbm, w_up_hbm, w_down_hbm,
    b_up_ref, gains_ref, biases_ref,
    output_ref, g_stream_ref, g_memory_ref, o_qkv_ref, o_out_ref, o_cq_ref, o_ckv_ref, o_cout_ref,
    o_up_ref, o_down_ref, o_b_up_ref, o_gains_ref, o_biases_ref,
    refs,
):
    spot = Spot()
    greeted = spot.greet()
    row_count, width = tokens_ref.shape
    own_blocks = row_count // BLK
    head = width // HEADS
    blocks = own_blocks * HEADS
    mem_rows = memory_ref.shape[0]
    mem_total = mem_rows * HEADS
    hidden_width = b_up_ref.shape[1]
    chunks = hidden_width // width
    pairs = HEADS // 2
    score_scale = head ** (-0.5)
    prompt_tiles = prompt_blocks * BLK // TILE
    tiles = blocks * BLK // TILE

    sources = dict(
        w_qkv=w_qkv_hbm, w_ckv=w_ckv_hbm, w_out=w_out_hbm, w_cq=w_cq_hbm, w_cout=w_cout_hbm,
        w_up=w_up_hbm, w_down=w_down_hbm,
    )
    loads = Bag(
        {
            name: pltpu.make_async_copy(source, getattr(refs, name), refs.load_sem.at[index])
            for index, (name, source) in enumerate(sources.items())
        }
    )
    for name in sources:
        getattr(loads, name).start()

    outs = dict(
        up0=[(o_up_ref, 0, 0, 1024)],
        up1=[(o_up_ref, 0, 1024, 1024)],
        down0=[(o_down_ref, 0, 0, 512), (o_down_ref, 32, 0, 512)],
        down1=[(o_down_ref, 64, 0, 512), (o_down_ref, 96, 0, 512)],
        cross=[(o_cout_ref, 0, 0, 512), (o_cq_ref, 0, 0, 512)],
        out=[(o_out_ref, 0, 0, 512)],
        ckv=[(o_ckv_ref, 0, 0, 1024)],
        wq=[(o_qkv_ref, 0, 0, 512)],
        wk=[(o_qkv_ref, 0, 512, 512)],
        wv=[(o_qkv_ref, 0, 1024, 512)],
    )
    piece = Bag(
        {
            name: Piece(spot, TURNS[name], Bag(refs.pieces[name]), outs[name])
            for name in PIECES
        }
    )
    ups, downs = (piece.up0, piece.up1), (piece.down0, piece.down1)

    def put_rows(to, values, column):
        span = values.shape[1]
        split = values.astype(LOW).reshape(ROWS, 2, 2, 2, HALF, span)
        for half in range(2):
            to.part[half, :, :, :, :, column : column + span] = split[:, :, :, half]

    few_ref = refs.few_sum
    few_ref[...] = jnp.zeros_like(few_ref)

    def few(row, values):
        few_ref[row : row + 1, :] = values

    def gain(row):
        return gains_ref[row : row + 1, :]

    def bias(row):
        return biases_ref[row : row + 1, :]

    send_ref = refs.head_send
    loads.w_qkv.wait()
    zeros_row = jnp.zeros((1, width), WIDE)
    pair_rows, last_rows = slice(0, 2 * head), slice(2 * head, 3 * head)
    pair_land, last_land = refs.pair_land, refs.last_land
    to_heads_copy = Exchange(
        spot, send_ref, refs.to_heads_sem,
        [(block, 1, pair_rows, pair_land, pair_rows) for block in range(own_blocks)]
        + [(0, own_blocks, last_rows, last_land, slice(0, head))],
    )
    pair_bias = jnp.concatenate([bias(0), zeros_row], axis=1)
    for block in range(own_blocks):
        rows = slice(block * BLK, (block + 1) * BLK)
        projected = (nn(tokens_ref[rows, :], refs.w_qkv[:, : 2 * width]) + pair_bias).astype(LOW)
        turned = projected.astype(WIDE).T
        turned = jnp.concatenate([turned[:width] * score_scale, turned[width:]], axis=0).astype(LOW)
        for h in range(HEADS):
            for kind in range(2):
                at = kind * width + h * head
                send_ref[h, block, kind * head : (kind + 1) * head, :] = turned[at : at + head]
        if block == 0:
            pl.semaphore_wait(pltpu.get_barrier_semaphore(), greeted)
        to_heads_copy.start(block)
    for block in range(own_blocks):
        rows = slice(block * BLK, (block + 1) * BLK)
        turned = swap((nn(tokens_ref[rows, :], refs.w_qkv[:, 2 * width :]) + bias(1)).astype(LOW))
        for h in range(HEADS):
            send_ref[h, block, last_rows, :] = turned[h * head : (h + 1) * head]
    to_heads_copy.start(own_blocks)
    all_ref = refs.memory_all
    all_ref[spot.col, spot.row] = memory_ref[...]

    def pass_on(step):
        row = lax.rem(spot.row + ROWS - step, ROWS)
        copy = remote(
            all_ref.at[spot.col, row], all_ref.at[spot.col, row],
            refs.spread_sem.at[0, ROWS + step], refs.spread_sem.at[1, ROWS + step], spot.col_peer,
        )
        copy.start()
        return copy

    passed = [pass_on(0)]
    inv_ref = refs.inverse
    for pos in range(blocks):
        row = jnp.int32(0)
        for other in range(1, blocks):
            row = jnp.where(deal_ref[other] == pos, other, row)
        inv_ref[pos] = row
    for block in range(own_blocks):
        to_heads_copy.wait(block)

    q_ref, kv_ref = refs.q, refs.kv
    no_head = jnp.zeros((head, BLK), LOW)
    no_tile = jnp.zeros((head, TILE), LOW)
    qt_ref, kt_ref, vt_ref = refs.qt, refs.kt, refs.vt
    exact_ref, lse_ref = refs.exact, refs.lse
    for pos in range(blocks):
        block = pair_land[inv_ref[pos]]
        at = slice(pos * BLK, (pos + 1) * BLK)
        qt_ref[:, at] = block[:head]
        kt_ref[:, at] = block[head:]
        kv_ref[at, :] = swap(jnp.concatenate([block[head:], no_head], axis=0))

    def key_spans(tile, step, state):
        first = tile * TILE
        base = 0 if first < prompt_blocks * BLK else prompt_blocks * BLK
        chunk = first // KEYS
        state = step(chunk, state, lambda s, c: hide_later(s, first - chunk * KEYS))
        for chunk in range(base // KEYS, first // KEYS):
            state = step(chunk, state, lambda s, c: s)
        for chunk in range(base // KEYS):
            state = step(
                chunk,
                state,
                lambda s, c: hide_prompt(s, offset_ref, open_ref, tile, c, prompt_blocks),
            )
        return state

    tile_count = blocks * BLK // TILE
    for tile in range(tile_count):
        here = slice(tile * TILE, (tile + 1) * TILE)
        queries = jnp.concatenate([qt_ref[:, here], no_tile], axis=0)

        def top_step(chunk, top, hide):
            scores = nn(kv_ref[chunk * KEYS : (chunk + 1) * KEYS, :], queries)
            scores = hide(scores, chunk).reshape(KEYS // 8, 8, TILE)
            return jnp.maximum(top, jnp.max(scores, axis=0))

        top = key_spans(tile, top_step, jnp.full((8, TILE), NEG_FILL, WIDE))
        lse_ref[:, here] = jnp.max(top, axis=0, keepdims=True)
    to_heads_copy.wait(own_blocks)
    spread = []
    for step in range(1, ROWS):
        copy = remote(
            memory_ref, all_ref.at[spot.col, spot.row],
            refs.spread_sem.at[0, step], refs.spread_sem.at[1, step], spot.row_peers[step],
        )
        copy.start()
        spread.append(copy)
    for pos in range(blocks):
        vt_ref[:, pos * BLK : (pos + 1) * BLK] = last_land[inv_ref[pos]]

    def tile_spans(tile, chunk_step, state):
        state = chunk_step(tile, state, lambda s, c: hide_later(s, 0))
        first = jnp.where(tile >= prompt_tiles, prompt_tiles, 0)
        state = lax.fori_loop(first, tile, lambda c, s: chunk_step(c, s, lambda x, _: x), state)
        return lax.fori_loop(
            0,
            first,
            lambda c, s: chunk_step(
                c, s, lambda x, cc: hide_prompt(x, offset_ref, open_ref, tile, cc, prompt_blocks)
            ),
            state,
        )

    for tile in range(tile_count):
        here = slice(tile * TILE, (tile + 1) * TILE)
        queries = jnp.concatenate([qt_ref[:, here], no_tile], axis=0)
        top = lse_ref[:, here]

        def mix_step(chunk, state, hide):
            total, mixed = state
            there = slice(chunk * KEYS, (chunk + 1) * KEYS)
            weights = jnp.exp(hide(nn(kv_ref[there, :], queries), chunk) - top)
            total = total + jnp.sum(weights.reshape(KEYS // 8, 8, TILE), axis=0)
            return total, mixed + nn(vt_ref[:, there], weights.astype(LOW))

        total, mixed = key_spans(
            tile, mix_step, (jnp.zeros((8, TILE), WIDE), jnp.zeros((head, TILE), WIDE))
        )
        total = jnp.sum(total, axis=0, keepdims=True)
        exact = mixed / total
        for sub in range(TILE // BLK):
            exact_ref[tile * (TILE // BLK) + sub] = exact[:, sub * BLK : (sub + 1) * BLK]
        lse_ref[:, here] = top + jnp.log(total)
        if tile == tile_count - 2:
            spread[0].wait()
            passed.append(pass_on(1))
    for step in range(2, ROWS):
        spread[step - 1].wait()
        passed.append(pass_on(step))
    mixed_ref = refs.mixed_send
    for row in range(blocks):
        mixed_ref[row // own_blocks, row % own_blocks] = exact_ref[deal_ref[row]].astype(LOW)
    all_rows = slice(0, head)
    from_heads_copy = Exchange(
        spot, mixed_ref, refs.from_heads_sem,
        [(0, own_blocks, all_rows, refs.mixed_land, all_rows)],
    )
    from_heads_copy.start()

    for pos in range(blocks):
        at = slice(pos * BLK, (pos + 1) * BLK)
        kv_ref[at, :] = swap(jnp.concatenate([kt_ref[:, at], vt_ref[:, at]], axis=0))

    ck_ref, cv_ref, ckt_ref, cvt_ref = refs.ck, refs.cv, refs.ckt, refs.cvt
    loads.w_ckv.wait()

    def encode(col, row):
        rows = pl.ds(pl.multiple_of((row * 2 + col) * mem_rows, mem_rows), mem_rows)
        both = nn(all_ref[col, row], refs.w_ckv[...])
        keys = both[:, :width].astype(LOW)
        values = (both[:, width:] + bias(5)).astype(LOW)
        ck_ref[rows, :] = keys
        cv_ref[rows, :] = values
        ckt_ref[:, rows] = swap(keys)
        cvt_ref[:, rows] = swap(values)

    for row in range(ROWS):
        encode(spot.col, row)
    for copy in passed:
        copy.wait()
    for row in range(ROWS):
        encode(1 - spot.col, row)

    loads.w_out.wait()
    from_heads_copy.wait()
    attended_t_ref = refs.attended_t
    unit_one_ref, unit_two_ref = refs.unit_one, refs.unit_two
    low_one_ref, low_two_ref = refs.low_one, refs.low_two
    for block in range(own_blocks):
        at = slice(block * BLK, (block + 1) * BLK)
        for h in range(HEADS):
            attended_t_ref[h * head : (h + 1) * head, at] = refs.mixed_land[h * own_blocks + block]
    cq_ref, cqt_ref = refs.cq, refs.cqt
    loads.w_cq.wait()

    def rows_at(block):
        return pl.ds(pl.multiple_of(block * BLK, BLK), BLK)

    def first_norm(block, carry):
        rows = rows_at(block)
        attended = swap(attended_t_ref[:, rows])
        first_sum = tokens_ref[rows, :].astype(WIDE) + nn(attended, refs.w_out[...]) + bias(2)
        unit, scale = norm_parts(first_sum)
        unit_one_ref[rows, :] = unit
        refs.scale_one[rows, :] = scale
        low_one = (unit * gain(0) + bias(3)).astype(LOW)
        low_one_ref[rows, :] = low_one
        cross_query = (nn(low_one, refs.w_cq[...]) + bias(4)).astype(LOW).astype(WIDE)
        cross_query = cross_query * score_scale
        cq_ref[rows, :] = cross_query.astype(LOW)
        cqt_ref[:, rows] = cross_query.T.astype(LOW)
        return carry

    lax.fori_loop(0, own_blocks, first_norm, 0)

    pair_width = 2 * head
    cross_exact_ref, cross_lse_ref = refs.cross_exact, refs.cross_lse
    steps = mem_total // STEP

    def pair_at(pair):
        return pl.ds(pl.multiple_of(pair * pair_width, pair_width), pair_width)

    def step_at(step):
        return pl.ds(pl.multiple_of(step * STEP, STEP), STEP)

    def cross_forward(pair, carry):
        lanes = pair_at(pair)
        for side in range(2):
            at = pl.ds(pl.multiple_of(pair * pair_width + side * head, head), head)
            queries = cqt_ref[at, :]
            none = jnp.zeros_like(queries)
            queries = jnp.concatenate([none, queries] if side else [queries, none], axis=0)

            def first_pass(step, top):
                scores = nn(ck_ref[step_at(step), lanes], queries)
                return jnp.maximum(top, jnp.max(scores.reshape(STEP // 8, 8, row_count), axis=0))

            top = lax.fori_loop(
                0, steps, first_pass, jnp.full((8, row_count), NEG_FILL, WIDE), unroll=True
            )
            top = jnp.max(top, axis=0, keepdims=True)

            def second_pass(step, state):
                total, mixed = state
                weights = jnp.exp(nn(ck_ref[step_at(step), lanes], queries) - top)
                total = total + jnp.sum(weights.reshape(STEP // 8, 8, row_count), axis=0)
                return total, mixed + nn(cvt_ref[at, step_at(step)], weights.astype(LOW))

            total, mixed = lax.fori_loop(
                0, steps, second_pass,
                (jnp.zeros((8, row_count), WIDE), jnp.zeros((head, row_count), WIDE)), unroll=True,
            )
            total = jnp.sum(total, axis=0, keepdims=True)
            across = slice(side * row_count, (side + 1) * row_count)
            cross_lse_ref[pl.ds(pair, 1), across] = top + jnp.log(total)
            cross_exact_ref[at, :] = mixed / total
        return carry

    lax.fori_loop(0, pairs, cross_forward, 0)
    cross_low_ref = refs.cross_low
    total_ref, hidden_ref, slope_ref = g_stream_ref, refs.hidden, refs.slope
    loads.w_cout.wait()

    def second_norm(block, carry):
        rows = rows_at(block)
        cross_low = cross_exact_ref[:, rows].T.astype(LOW)
        cross_low_ref[rows, :] = cross_low
        normed_one = unit_one_ref[rows, :] * gain(0) + bias(3)
        unit, scale = norm_parts(normed_one + nn(cross_low, refs.w_cout[...]) + bias(6))
        unit_two_ref[rows, :] = unit
        refs.scale_two[rows, :] = scale
        normed_two = unit * gain(1) + bias(7)
        low_two_ref[rows, :] = normed_two.astype(LOW)
        total_ref[rows, :] = normed_two + bias(8)
        return carry

    lax.fori_loop(0, own_blocks, second_norm, 0)

    loads.w_up.wait()
    loads.w_down.wait()
    w_up_ref, w_down_ref = refs.w_up, refs.w_down

    def chunk_at(chunk):
        return pl.ds(pl.multiple_of(chunk * width, width), width)

    def up_step(chunk, carry):
        pre = nn(low_two_ref[...], w_up_ref[:, chunk_at(chunk)]) + b_up_ref[:, chunk_at(chunk)]
        normal = 0.5 + 0.5 * lax.erf(pre * (2.0**-0.5))
        hidden = (pre * normal).astype(LOW)
        hidden_ref[chunk] = hidden
        slope = normal + pre * jnp.exp(-0.5 * pre * pre) * ((2.0 * jnp.pi) ** -0.5)
        slope_ref[chunk] = slope.astype(LOW)
        total_ref[...] += nn(hidden, w_down_ref[chunk_at(chunk), :])
        return carry

    lax.fori_loop(0, chunks, up_step, 0)

    low_third_ref = refs.low_third
    no_sums = (zeros_row, zeros_row, zeros_row)

    def third_norm(block, sums):
        rows = rows_at(block)
        unit, scale = norm_parts(total_ref[rows, :])
        output_ref[rows, :] = unit * gain(2) + bias(9)
        upstream = cot_ref[rows, :].astype(WIDE)
        grad = norm_pull(unit, scale, gain(2), upstream)
        low = grad.astype(LOW)
        low_third_ref[rows, :] = low
        total_ref[rows, :] = grad
        return (
            sums[0] + column_sums(upstream * unit),
            sums[1] + column_sums(upstream),
            sums[2] + column_sums(low),
        )

    sums = lax.fori_loop(0, own_blocks, third_norm, no_sums)
    few(6, sums[0])
    few(16, sums[1])
    few(15, sums[2])

    turned_ref = refs.turned
    turned_ref[...] = swap(low_two_ref[...])
    for chunk in range(chunks):
        rows = slice(chunk * width, (chunk + 1) * width)
        grad_hidden = nt(low_third_ref[...], w_down_ref[rows, :])
        grad_pre = (grad_hidden * slope_ref[chunk].astype(WIDE)).astype(LOW)
        few(chunk, column_sums(grad_pre))
        total_ref[...] += nt(grad_pre, w_up_ref[:, rows])
        grad_up = nn(turned_ref[...], grad_pre)
        put_rows(ups[chunk // 2], grad_up, (chunk % 2) * width)
        if chunk % 2 == 1:
            ups[chunk // 2].step()
        if chunk == 2:
            piece.up0.step()
        grad_down = nn(swap(hidden_ref[chunk]), low_third_ref[...])
        split = grad_down.astype(LOW).reshape(2, 2, 4, 2, HALF, width)
        for part in range(4):
            to = downs[part // 2].part
            column = (part % 2) * width
            for half in range(2):
                to[half, chunk, :, :, :, column : column + width] = split[:, :, part, half]
    piece.down0.step()
    piece.down1.step()

    dco_ref, dcot_ref = refs.dco, refs.dcot

    def second_back(block, sums):
        rows = rows_at(block)
        upstream = total_ref[rows, :]
        unit = unit_two_ref[rows, :]
        grad = norm_pull(unit, refs.scale_two[rows, :], gain(1), upstream)
        low = grad.astype(LOW)
        total_ref[rows, :] = grad
        low_third_ref[rows, :] = low
        dco_ref[rows, :] = nt(low, refs.w_cout[...]).astype(LOW)
        dcot_ref[:, rows] = nt(refs.w_cout[...], low).astype(LOW)
        return (
            sums[0] + column_sums(upstream * unit),
            sums[1] + column_sums(upstream),
            sums[2] + column_sums(low),
        )

    sums = lax.fori_loop(0, own_blocks, second_back, no_sums)
    few(5, sums[0])
    few(14, sums[1])
    few(13, sums[2])
    put_rows(piece.cross, nn(swap(cross_low_ref[...]), low_third_ref[...]), 0)
    piece.up1.step()
    piece.down0.step()
    piece.down1.step()

    dcqt_ref = refs.dcqt
    for pair in range(pairs):
        lanes = slice(pair * pair_width, (pair + 1) * pair_width)
        low_half = slice(pair * pair_width, pair * pair_width + head)
        high_half = slice(pair * pair_width + head, (pair + 1) * pair_width)
        queries_t = apart(cqt_ref[low_half, :], cqt_ref[high_half, :])
        upstream_t = apart(dcot_ref[low_half, :], dcot_ref[high_half, :])
        queries = apart_columns(cq_ref[:, lanes])
        upstream = apart_columns(dco_ref[:, lanes])
        dots = cross_exact_ref[lanes, :] * dcot_ref[lanes, :].astype(WIDE)
        delta = jnp.concatenate(
            [column_sums(dots[:head]), column_sums(dots[head:])], axis=1
        )
        lse = cross_lse_ref[pair : pair + 1, :]
        dcqt_ref[lanes, :] = jnp.zeros((pair_width, row_count), WIDE)

        def backward_step(step, carry):
            there = step_at(step)
            weights = jnp.exp(nn(ck_ref[there, lanes], queries_t) - lse)
            grad_weights = nn(cv_ref[there, lanes], upstream_t)
            grad_scores = (weights * (grad_weights - delta)).astype(LOW)
            ck_ref[there, lanes] = nn(grad_scores, queries).astype(LOW)
            cv_ref[there, lanes] = nn(weights.astype(LOW), upstream).astype(LOW)
            dcqt_ref[low_half, :] += nn(ckt_ref[low_half, there], grad_scores[:, :row_count])
            dcqt_ref[high_half, :] += nn(ckt_ref[high_half, there], grad_scores[:, row_count:])
            return carry

        lax.fori_loop(0, steps, backward_step, 0)
    upstream_send = refs.mixed_send

    def first_back(block, sums):
        rows = rows_at(block)
        grad_cq = (dcqt_ref[:, rows].T * score_scale).astype(LOW)
        dco_ref[rows, :] = grad_cq
        upstream = total_ref[rows, :] + nt(grad_cq, refs.w_cq[...])
        unit = unit_one_ref[rows, :]
        grad = norm_pull(unit, refs.scale_one[rows, :], gain(0), upstream)
        low = grad.astype(LOW)
        total_ref[rows, :] = grad
        low_third_ref[rows, :] = low
        grad_attended_t = nt(refs.w_out[...], low).astype(LOW)
        for h in range(HEADS):
            upstream_send[h, block] = grad_attended_t[h * head : (h + 1) * head, :]
        return (
            sums[0] + column_sums(upstream * unit),
            sums[1] + column_sums(upstream),
            sums[2] + column_sums(low),
            sums[3] + column_sums(grad_cq),
        )

    sums = lax.fori_loop(0, own_blocks, first_back, no_sums + (zeros_row,))
    few(4, sums[0])
    few(10, sums[1])
    few(9, sums[2])
    few(11, sums[3])
    up_heads_copy = Exchange(
        spot, upstream_send, refs.up_heads_sem,
        [(0, own_blocks, all_rows, refs.up_land, all_rows)],
    )
    up_heads_copy.start()
    turned_ref[...] = swap(low_one_ref[...])
    put_rows(piece.cross, nn(turned_ref[...], dco_ref[...]), width)
    piece.cross.steps(1)
    put_rows(piece.out, nn(attended_t_ref[...], low_third_ref[...]), 0)
    piece.out.steps(1)
    for part in range(HEADS):
        rows = slice(part * mem_rows, (part + 1) * mem_rows)
        ckt_ref[:, rows] = swap(all_ref[part % 2, part // 2])
        grad = nt(ck_ref[rows, :], refs.w_ckv[:, :width]) + nt(cv_ref[rows, :], refs.w_ckv[:, width:])
        w_up_ref[
            (part // 2) * mem_rows : (part // 2 + 1) * mem_rows,
            (part % 2) * width : (part % 2 + 1) * width,
        ] = grad.astype(LOW)
    g_land = refs.memory_land
    other_side = pl.ds(pl.multiple_of((1 - spot.col) * width, width), width)
    own_side = pl.ds(pl.multiple_of(spot.col * width, width), width)
    memory_copy = remote(
        w_up_ref.at[:, other_side], g_land, refs.memory_sem.at[0, 0], refs.memory_sem.at[1, 0],
        spot.col_peer,
    )
    put_rows(piece.ckv, nn(ckt_ref[...], ck_ref[...]), 0)
    put_rows(piece.ckv, nn(ckt_ref[...], cv_ref[...]), width)
    few(12, column_sums(cv_ref[...]))
    piece.ckv.steps(1)
    for pos in range(blocks):
        at = slice(pos * BLK, (pos + 1) * BLK)
        q_ref[at, :] = swap(jnp.concatenate([qt_ref[:, at], no_head], axis=0))
    up_heads_copy.wait()
    for item in ups + downs:
        item.steps(3)
    memory_copy.start()
    for item in (piece.cross, piece.out, piece.ckv):
        item.steps(2)

    upq_ref, upt_ref = refs.up, refs.upt
    dkv_ref, dqt_ref = refs.dkv, refs.dqt
    for pos in range(blocks):
        block = refs.up_land[inv_ref[pos]]
        at = slice(pos * BLK, (pos + 1) * BLK)
        upt_ref[:, at] = block
        upq_ref[at, :] = swap(jnp.concatenate([no_head, block], axis=0))
    dkv_ref[...] = jnp.zeros_like(dkv_ref)

    def backward_tile(tile, carry):
        here = pl.ds(pl.multiple_of(tile * TILE, TILE), TILE)
        queries_t = jnp.concatenate([qt_ref[:, here], no_tile], axis=0)
        upstream_t = jnp.concatenate([no_tile, upt_ref[:, here]], axis=0)
        both = jnp.concatenate([q_ref[here, :], upq_ref[here, :]], axis=0)
        lse = lse_ref[:, here]
        exact = jnp.concatenate(
            [exact_ref[tile * (TILE // BLK) + sub] for sub in range(TILE // BLK)], axis=1
        )
        delta = column_sums(exact * upt_ref[:, here].astype(WIDE))

        def chunk_step(chunk, grad_q, hide):
            there = pl.ds(pl.multiple_of(chunk * TILE, TILE), TILE)
            scores = hide(nn(kv_ref[there, :], queries_t), chunk)
            weights = jnp.exp(scores - lse)
            grad_weights = nn(kv_ref[there, :], upstream_t)
            grad_scores = (weights * (grad_weights - delta)).astype(LOW)
            sides = jnp.concatenate([grad_scores, weights.astype(LOW)], axis=1)
            spread_at = pl.ds(chunk * (TILE // BLK), TILE // BLK)
            dkv_ref[spread_at] += nn(sides, both).reshape(TILE // BLK, BLK, 2 * head)
            return grad_q + nn(kt_ref[:, there], grad_scores)

        grad_q = tile_spans(tile, chunk_step, jnp.zeros((head, TILE), WIDE))
        grad_q = (grad_q * score_scale).astype(LOW)
        for sub in range(TILE // BLK):
            dqt_ref[tile * (TILE // BLK) + sub] = grad_q[:, sub * BLK : (sub + 1) * BLK]
        return carry

    lax.fori_loop(0, tiles // 2, backward_tile, 0)
    piece.up0.steps(4)
    piece.up1.steps(4)
    lax.fori_loop(tiles // 2, tiles - 2, backward_tile, 0)
    piece.down0.steps(4)
    piece.down1.steps(4)
    lax.fori_loop(tiles - 2, tiles, backward_tile, 0)

    back_send = refs.head_send
    back_copy = Exchange(
        spot, back_send, refs.back_sem,
        [
            (0, own_blocks, slice(0, head), pair_land, slice(0, head)),
            (0, own_blocks, slice(head, 2 * head), pair_land, slice(head, 2 * head)),
            (0, own_blocks, last_rows, last_land, slice(0, head)),
        ],
    )
    for row in range(blocks):
        back_send[row // own_blocks, row % own_blocks, :head] = dqt_ref[deal_ref[row]]
    back_copy.start(0)
    for row in range(blocks):
        back_send[row // own_blocks, row % own_blocks, head:] = dkv_ref[deal_ref[row]].T.astype(LOW)
    back_copy.start(1)
    back_copy.start(2)

    ones = jnp.ones((8, BLK), LOW)
    query_sums = jnp.zeros((8, head), WIDE)
    both_sums = jnp.zeros((1, 2 * head), WIDE)
    for pos in range(blocks):
        query_sums = query_sums + nt(ones, dqt_ref[pos])
        both_sums = both_sums + column_sums(dkv_ref[pos])
    own_lanes = lax.broadcasted_iota(jnp.int32, (1, width), 1) // head == spot.ctx
    few(7, jnp.where(own_lanes, jnp.concatenate([query_sums[:1]] * HEADS, axis=1), 0.0))
    few(8, jnp.where(own_lanes, jnp.concatenate([both_sums[:, head:]] * HEADS, axis=1), 0.0))

    few_core, few_plane, few_rows = refs.few_core, refs.few_plane, refs.few_rows
    few_sem = refs.few_sem
    core_copy = remote(few_ref, few_core, few_sem.at[0, 0], few_sem.at[1, 0], spot.core_peer)
    core_copy.start()
    for item in ups + downs:
        item.steps(5)
    core_copy.wait()
    own_place = spot.col * 2 + spot.wsh
    few_plane[own_place] = few_ref[...] + few_core[...]
    plane_copies = []
    for way, (target, _, _) in enumerate(spot.ways):
        copy = remote(
            few_plane.at[own_place], few_plane.at[own_place],
            few_sem.at[0, 1 + way], few_sem.at[1, 1 + way], target,
        )
        copy.start()
        plane_copies.append(copy)
    piece.cross.steps(3)
    piece.out.steps(3)
    for copy in plane_copies:
        copy.wait()
    few_rows[spot.row] = few_plane[0] + few_plane[1] + few_plane[2] + few_plane[3]
    row_copies = []
    for step in range(1, ROWS):
        copy = remote(
            few_rows.at[spot.row], few_rows.at[spot.row],
            few_sem.at[0, 3 + step], few_sem.at[1, 3 + step], spot.row_peers[step],
        )
        copy.start()
        row_copies.append(copy)
    piece.ckv.steps(3)
    memory_copy.wait()
    g_land[...] = plus(w_up_ref[:, own_side], g_land[...]).astype(LOW)
    for item in ups + downs:
        item.steps(6)

    turned_ref[...] = swap(tokens_ref[...])
    kinds = (piece.wq, piece.wk, piece.wv)
    for kind in range(3):
        back_copy.wait(kind)
        for block in range(own_blocks):
            turned = jnp.concatenate(
                [
                    (pair_land, pair_land, last_land)[kind][
                        h * own_blocks + block, kind % 2 * head : (kind % 2 + 1) * head, :
                    ]
                    for h in range(HEADS)
                ],
                axis=0,
            )
            hidden_ref[kind, block * BLK : (block + 1) * BLK, :] = swap(turned)
        put_rows(kinds[kind], nn(turned_ref[...], hidden_ref[kind]), 0)
        kinds[kind].steps(1)
        if kind > 0:
            kinds[kind - 1].steps(2)
    for item in (piece.cross, piece.out, piece.ckv):
        item.steps(4)
    memory_copies = []
    for step in range(1, ROWS):
        copy = remote(
            g_land.at[pl.ds(spot.rows_by_step[step] * mem_rows, mem_rows)], refs.memory_row.at[step - 1],
            refs.memory_sem.at[0, step], refs.memory_sem.at[1, step], spot.row_peers[step],
        )
        copy.start()
        memory_copies.append(copy)
    grad_stream = total_ref[...]
    for kind in range(3):
        if kind == 1:
            kinds[2].steps(2)
        lanes = slice(kind * width, (kind + 1) * width)
        grad_stream = grad_stream + nt(hidden_ref[kind], refs.w_qkv[:, lanes])
    g_stream_ref[...] = grad_stream
    for item in kinds:
        item.steps(3)
    for copy in row_copies:
        copy.wait()
    total = few_rows[0] + few_rows[1] + few_rows[2] + few_rows[3]
    own_shard = spot.ctx * 2 + spot.wsh
    part, long_part = width // SHARDS, hidden_width // SHARDS
    picked, long_picked = total[:, :part], total[:1, :long_part]
    for shard in range(1, SHARDS):
        picked = jnp.where(own_shard == shard, total[:, shard * part : (shard + 1) * part], picked)
        row, at = divmod(shard * long_part, width)
        long_picked = jnp.where(
            own_shard == shard, total[row : row + 1, at : at + long_part], long_picked
        )
    o_b_up_ref[...] = long_picked
    o_gains_ref[...] = picked[4:7]
    o_biases_ref[...] = picked[7:17]
    for item in (piece.cross, piece.out, piece.ckv):
        item.steps(5)
    for copy in memory_copies:
        copy.wait()
    total = g_land[pl.ds(spot.row * mem_rows, mem_rows), :].astype(WIDE)
    for step in range(ROWS - 1):
        total = total + refs.memory_row[step].astype(WIDE)
    g_memory_ref[...] = total
    for item in kinds + (piece.cross, piece.out, piece.ckv):
        item.steps(6)


def layer_scratch(row_count, width, hidden_width, mem_rows):
    own_blocks = row_count // BLK
    blocks = own_blocks * HEADS
    head = width // HEADS
    tokens = blocks * BLK
    mem_total = mem_rows * HEADS
    dma = pltpu.SemaphoreType.DMA
    scratch = dict(
        w_qkv=((width, 3 * width), LOW), w_ckv=((width, 2 * width), LOW),
        w_out=((width, width), LOW), w_cq=((width, width), LOW),
        w_cout=((width, width), LOW), w_up=((width, hidden_width), LOW),
        w_down=((hidden_width, width), LOW),
        head_send=((HEADS, own_blocks, 3 * head, BLK), LOW),
        pair_land=((blocks, 2 * head, BLK), LOW), last_land=((blocks, head, BLK), LOW),
        memory_all=((2, ROWS, mem_rows, width), LOW),
        q=((tokens, 2 * head), LOW), kv=((tokens, 2 * head), LOW),
        qt=((head, tokens), LOW), kt=((head, tokens), LOW), vt=((head, tokens), LOW),
        exact=((blocks, head, BLK), WIDE), lse=((1, tokens), WIDE),
        mixed_send=((HEADS, own_blocks, head, BLK), LOW),
        mixed_land=((blocks, head, BLK), LOW),
        ck=((mem_total, width), LOW), cv=((mem_total, width), LOW),
        ckt=((width, mem_total), LOW), cvt=((width, mem_total), LOW),
        attended_t=((width, row_count), LOW),
        unit_one=((row_count, width), WIDE), unit_two=((row_count, width), WIDE),
        scale_one=((row_count, 1), WIDE), scale_two=((row_count, 1), WIDE),
        low_one=((row_count, width), LOW), low_two=((row_count, width), LOW),
        cq=((row_count, width), LOW), cqt=((width, row_count), LOW),
        cross_exact=((width, row_count), WIDE),
        cross_lse=((HEADS // 2, 2 * row_count), WIDE),
        cross_low=((row_count, width), LOW),
        hidden=((hidden_width // width, row_count, width), LOW),
        slope=((hidden_width // width, row_count, width), LOW),
        low_third=((row_count, width), LOW),
        turned=((width, row_count), LOW),
        dco=((row_count, width), LOW), dcot=((width, row_count), LOW),
        dcqt=((width, row_count), WIDE),
        memory_land=((ROWS * mem_rows, width), LOW),
        memory_row=((ROWS - 1, mem_rows, width), LOW),
        up_land=((blocks, head, BLK), LOW),
        up=((tokens, 2 * head), LOW), upt=((head, tokens), LOW),
        dkv=((blocks, BLK, 2 * head), WIDE), dqt=((blocks, head, BLK), LOW),
        few_sum=((FEW_ROWS, width), WIDE), few_core=((FEW_ROWS, width), WIDE),
        few_plane=((4, FEW_ROWS, width), WIDE), few_rows=((ROWS, FEW_ROWS, width), WIDE),
    )
    out = {name: pltpu.VMEM(shape, kind) for name, (shape, kind) in scratch.items()}
    out.update(
        load_sem=dma((7,)), to_heads_sem=dma((2, HEADS, 4)), from_heads_sem=dma((2, HEADS, 1)),
        up_heads_sem=dma((2, HEADS, 1)), back_sem=dma((2, HEADS, 3)), spread_sem=dma((2, 2 * ROWS)),
        inverse=pltpu.SMEM((blocks,), jnp.int32),
        memory_sem=dma((2, ROWS)), few_sem=dma((2, 7)),
    )
    out.update(
        pieces={
            name: dict(
                part=pltpu.VMEM((2, ROWS, 2, 2, HALF, span), LOW),
                core_land=pltpu.VMEM((ROWS, 2, 2, HALF, span), LOW),
                hop_land=pltpu.VMEM(
                    (3, ROWS, HALF, span) if TURNS[name] == 2 else (ROWS, 2, HALF, span), LOW
                ),
                turn_land=pltpu.VMEM((ROWS, HALF, span), LOW),
                row_land=pltpu.VMEM(
                    (2, ROWS, HALF, span) if TURNS[name] == 2 else (ROWS - 1, HALF, span), LOW
                ),
                sems=dma((2, 12)),
            )
            for name, span in PIECES.items()
        }
    )
    return out


def layer_call(deal_ids, offsets, opened, tokens, memory, cotangent, weights, b_up, gains, biases, prompt_blocks):
    row_count, width = tokens.shape
    hidden_width = b_up.shape[1]
    mem_rows = memory.shape[0]
    smem = pl.BlockSpec(memory_space=pltpu.SMEM)
    vmem = pl.BlockSpec(memory_space=pltpu.VMEM)
    hbm = pl.BlockSpec(memory_space=pl.ANY)
    scratch = layer_scratch(row_count, width, hidden_width, mem_rows)
    leaves, tree = jax.tree.flatten(scratch, is_leaf=lambda leaf: not isinstance(leaf, dict))
    out_shapes = [
        (row_count, width), (row_count, width), (mem_rows, width),
        (32, 3 * width), (32, width), (32, width), (32, 2 * width), (32, width),
        (32, hidden_width), (hidden_width // SHARDS, width),
        (1, hidden_width // SHARDS), (3, width // SHARDS), (10, width // SHARDS),
    ]

    def body(*args):
        count = len(args) - len(leaves)
        refs = Bag(jax.tree.unflatten(tree, args[count:]))
        layer_kernel(prompt_blocks, *args[:count], refs)

    return pl.pallas_call(
        body,
        out_shape=[jax.ShapeDtypeStruct(shape, WIDE) for shape in out_shapes],
        in_specs=[smem] * 3 + [vmem] * 3 + [hbm] * 7 + [vmem] * 3,
        out_specs=[vmem] * len(out_shapes),
        scratch_shapes=leaves,
        compiler_params=pltpu.CompilerParams(
            collective_id=0, has_side_effects=True, vmem_limit_bytes=BIG_VMEM
        ),
        name="layer",
    )(deal_ids, offsets, opened, tokens, memory, cotangent, *weights, b_up, gains, biases)


def hand_out_kernel(count, *refs):
    for index in range(count):
        refs[count + index][...] = refs[index][...]


def hand_out(arrays):
    count = len(arrays)
    vmem = pl.BlockSpec(memory_space=pltpu.VMEM)
    return pl.pallas_call(
        functools.partial(hand_out_kernel, count),
        out_shape=[jax.ShapeDtypeStruct(a.shape, a.dtype) for a in arrays],
        in_specs=[vmem] * count,
        out_specs=[vmem] * count,
        compiler_params=pltpu.CompilerParams(vmem_limit_bytes=BIG_VMEM),
        name="hand_out",
    )(*arrays)


def layer_shards(
    stream, memory, cotangent, deal_order, offsets, context_mask,
    w_qkv, w_out, w_cq, w_ckv, w_cout, w_up, w_down, b_up, gains, biases,
):
    results = layer_call(
        deal_order[0, 0], offsets[0, 0], context_mask[0, 0],
        stream[0, 0], memory[0, 0], cotangent[0, 0],
        (w_qkv, w_out, w_cq, w_ckv, w_cout, w_up, w_down),
        b_up[None, :], gains, biases, context_mask.shape[3],
    )
    output, grad_stream, grad_memory, *grads = hand_out(results)
    grads[7] = grads[7].reshape(-1)
    return (output[None, None], grad_stream[None, None], grad_memory[None, None], *grads)


def gelu_exact(values):
    return jax.nn.gelu(values, approximate=False)


def norm_rows(values, gain_vec, shift_vec):
    center = values - jnp.mean(values, axis=-1, keepdims=True)
    spread = jnp.mean(center * center, axis=-1, keepdims=True)
    return center * lax.rsqrt(spread + EPS_NORM) * gain_vec + shift_vec


def norm_back(values, gain_vec, shift_vec, upstream):
    _, pullback = jax.vjp(norm_rows, values, gain_vec, shift_vec)
    return pullback(upstream)


def seq_index(positions, prompt_len, cont_len):
    later = jnp.int32(1) + (positions - jnp.int32(prompt_len)) // jnp.int32(cont_len)
    return jnp.where(positions < prompt_len, jnp.zeros_like(later), later)


def visible(query_pos, key_ids, offsets, context_mask, block_len, prompt_blocks, cont_blocks):
    prompt_len = prompt_blocks * block_len
    cont_len = cont_blocks * block_len
    cont_count = offsets.shape[0]
    key_pos = (
        key_ids[:, None] * jnp.int32(block_len) + jnp.arange(block_len, dtype=jnp.int32)[None, :]
    ).reshape(-1)
    query_seq = seq_index(query_pos, prompt_len, cont_len)
    key_seq = seq_index(key_pos, prompt_len, cont_len)
    inside = (query_seq[:, None] == key_seq[None, :]) & (key_pos[None, :] <= query_pos[:, None])
    cont_pick = jnp.clip(query_seq - 1, 0, cont_count - 1)
    prompt_limit = jnp.take(offsets, cont_pick)
    query_block = jnp.clip(
        (query_pos - jnp.int32(prompt_len)) // jnp.int32(block_len), 0, cont_count * cont_blocks - 1
    )
    mask_rows = jnp.take(context_mask, query_block, axis=0)
    key_block = jnp.clip(key_ids, 0, prompt_blocks - 1)
    block_open = jnp.take(mask_rows, key_block, axis=1) > 0
    block_open = jnp.repeat(block_open, block_len, axis=1) | (key_pos[None, :] < block_len)
    from_prompt = (
        (query_seq[:, None] > 0)
        & (key_seq[None, :] == 0)
        & (key_pos[None, :] < prompt_limit[:, None])
        & block_open
    )
    return inside | from_prompt


def dot_first(left, right):
    return lax.dot_general(
        left, right, (((0,), (0,)), ((), ())), preferred_element_type=jnp.float32
    )


def dot_last(left, right):
    return lax.dot_general(
        left, right, (((1,), (1,)), ((), ())), preferred_element_type=jnp.float32
    )


def to_heads(matrix, head_count):
    row_count, model_width = matrix.shape
    return matrix.reshape(row_count, head_count, model_width // head_count).transpose(1, 0, 2)


def from_heads(stacked):
    head_count, row_count, head_width = stacked.shape
    return stacked.transpose(1, 0, 2).reshape(row_count, head_count * head_width)


def pair_heads(key_rows, value_rows, head_count):
    return jnp.concatenate(
        [to_heads(key_rows, head_count), to_heads(value_rows, head_count)], axis=2
    )


def head_scores(queries, key_rows, allowed):
    score_scale = queries.shape[1] ** (-0.5)
    scores = dot_last(queries, key_rows) * score_scale
    if allowed is not None:
        scores = jnp.where(allowed, scores, NEG_FILL)
    return scores


def head_forward(queries, keyval, allowed):
    head_width = queries.shape[1]
    scores = head_scores(queries, keyval[:, :head_width], allowed)
    row_top = jnp.max(scores, axis=1, keepdims=True)
    exp_scores = jnp.exp(scores - row_top)
    row_total = jnp.sum(exp_scores, axis=1, keepdims=True)
    soft_weights = (exp_scores / row_total).astype(jnp.bfloat16)
    mixed_heads = jnp.dot(soft_weights, keyval[:, head_width:], preferred_element_type=jnp.float32)
    return (mixed_heads, row_top + jnp.log(row_total))


def head_backward(queries, keyval, upstream, log_total, allowed):
    head_width = queries.shape[1]
    score_scale = head_width ** (-0.5)
    key_rows = keyval[:, :head_width]
    scores = head_scores(queries, key_rows, allowed)
    soft_weights = jnp.exp(scores - log_total)
    grad_soft = dot_last(upstream, keyval[:, head_width:])
    row_delta = jnp.sum(soft_weights * grad_soft, axis=1, keepdims=True)
    grad_scores = (soft_weights * (grad_soft - row_delta)).astype(jnp.bfloat16)
    grad_query = jnp.dot(grad_scores, key_rows, preferred_element_type=jnp.float32) * score_scale
    grad_keys = dot_first(grad_scores, queries) * score_scale
    grad_values = dot_first(soft_weights.astype(jnp.bfloat16), upstream)
    return (grad_query, jnp.concatenate([grad_keys, grad_values], axis=1))


def shards(
    stream,
    memory,
    cotangent,
    deal_order,
    offsets,
    context_mask,
    w_qkv,
    w_out,
    w_cq,
    w_ckv,
    w_cout,
    w_up,
    w_down,
    b_up,
    gains,
    biases,
):
    tokens = stream[0, 0]
    row_count, model_width = tokens.shape
    head_width = model_width // HEADS
    deal_ids = deal_order[0, 0]
    prompt_blocks = context_mask.shape[3]
    own_blocks = row_count // BLK
    own_ids = lax.dynamic_slice_in_dim(deal_ids, lax.axis_index("ctx") * own_blocks, own_blocks)
    query_pos = (
        own_ids[:, None] * jnp.int32(BLK) + jnp.arange(BLK, dtype=jnp.int32)[None, :]
    ).reshape(-1)
    allowed = visible(
        query_pos, deal_ids, offsets[0, 0], context_mask[0, 0], BLK, prompt_blocks, CBLK
    )
    zeros_row = jnp.zeros((model_width,), jnp.float32)
    projected = (
        jnp.dot(tokens, w_qkv, preferred_element_type=jnp.float32)
        + jnp.concatenate([biases[0], zeros_row, biases[1]])
    ).astype(jnp.bfloat16)
    query_heads = to_heads(projected[:, :model_width], HEADS)
    keyval_own = pair_heads(
        projected[:, model_width : 2 * model_width], projected[:, 2 * model_width :], HEADS
    )
    keyval_all = lax.all_gather(keyval_own, "ctx", axis=1, tiled=True)

    def self_forward(pieces):
        return head_forward(pieces[0], pieces[1], allowed)

    self_out, self_lse = lax.map(self_forward, (query_heads, keyval_all))
    attended = from_heads(self_out).astype(jnp.bfloat16)
    first_sum = (
        tokens.astype(jnp.float32)
        + jnp.dot(attended, w_out, preferred_element_type=jnp.float32)
        + biases[2]
    )
    normed_one = norm_rows(first_sum, gains[0], biases[3])
    normed_low = normed_one.astype(jnp.bfloat16)
    cross_query = (
        jnp.dot(normed_low, w_cq, preferred_element_type=jnp.float32) + biases[4]
    ).astype(jnp.bfloat16)
    cross_bias = jnp.concatenate([zeros_row, biases[5]])
    memory_own = memory[0, 0]
    memory_all = lax.all_gather(memory_own, "ctx", axis=0, tiled=True)
    cross_kv = (jnp.dot(memory_all, w_ckv, preferred_element_type=jnp.float32) + cross_bias).astype(
        jnp.bfloat16
    )
    cross_heads = pair_heads(cross_kv[:, :model_width], cross_kv[:, model_width:], HEADS)
    cross_query_heads = to_heads(cross_query, HEADS)

    def cross_forward(pieces):
        return head_forward(pieces[0], pieces[1], None)

    cross_out, cross_lse = lax.map(cross_forward, (cross_query_heads, cross_heads))
    cross_attended = from_heads(cross_out).astype(jnp.bfloat16)
    second_sum = (
        normed_one + jnp.dot(cross_attended, w_cout, preferred_element_type=jnp.float32) + biases[6]
    )
    normed_two = norm_rows(second_sum, gains[1], biases[7])
    normed_two_low = normed_two.astype(jnp.bfloat16)
    hidden_pre = jnp.dot(normed_two_low, w_up, preferred_element_type=jnp.float32) + b_up
    hidden = gelu_exact(hidden_pre).astype(jnp.bfloat16)
    third_sum = normed_two + jnp.dot(hidden, w_down, preferred_element_type=jnp.float32) + biases[8]
    output = norm_rows(third_sum, gains[2], biases[9])
    grad_third, grad_gain_three, grad_shift_three = norm_back(
        third_sum, gains[2], biases[9], cotangent[0, 0].astype(jnp.float32)
    )
    grad_down_in = grad_third.astype(jnp.bfloat16)
    grad_w_down = dot_first(hidden, grad_down_in)
    grad_b_down = jnp.sum(grad_down_in.astype(jnp.float32), axis=0)
    grad_hidden = dot_last(grad_down_in, w_down)
    _, gelu_pull = jax.vjp(gelu_exact, hidden_pre)
    grad_pre = gelu_pull(grad_hidden)[0].astype(jnp.bfloat16)
    grad_w_up = dot_first(normed_two_low, grad_pre)
    grad_b_up = jnp.sum(grad_pre.astype(jnp.float32), axis=0)
    grad_normed_two = grad_third + dot_last(grad_pre, w_up)
    grad_second, grad_gain_two, grad_shift_two = norm_back(
        second_sum, gains[1], biases[7], grad_normed_two
    )
    grad_cross_in = grad_second.astype(jnp.bfloat16)
    grad_w_cout = dot_first(cross_attended, grad_cross_in)
    grad_b_co = jnp.sum(grad_cross_in.astype(jnp.float32), axis=0)
    grad_cross_heads = to_heads(dot_last(grad_cross_in, w_cout).astype(jnp.bfloat16), HEADS)

    def cross_backward(pieces):
        return head_backward(pieces[0], pieces[1], pieces[2], pieces[3], None)

    grad_cq_heads, grad_ckv_all = lax.map(
        cross_backward, (cross_query_heads, cross_heads, grad_cross_heads, cross_lse)
    )
    grad_ckv_own = lax.psum_scatter(
        grad_ckv_all.astype(jnp.bfloat16), "ctx", scatter_dimension=1, tiled=True
    )
    grad_cv = from_heads(grad_ckv_own[:, :, head_width:])
    grad_ckv = jnp.concatenate([from_heads(grad_ckv_own[:, :, :head_width]), grad_cv], axis=1)
    grad_w_ckv = dot_first(memory_own, grad_ckv)
    grad_b_cv = jnp.sum(grad_cv.astype(jnp.float32), axis=0)
    grad_memory = dot_last(grad_ckv, w_ckv)
    grad_cq = from_heads(grad_cq_heads).astype(jnp.bfloat16)
    grad_w_cq = dot_first(normed_low, grad_cq)
    grad_b_cq = jnp.sum(grad_cq.astype(jnp.float32), axis=0)
    grad_normed_one = grad_second + dot_last(grad_cq, w_cq)
    grad_first, grad_gain_one, grad_shift_one = norm_back(
        first_sum, gains[0], biases[3], grad_normed_one
    )
    grad_att_in = grad_first.astype(jnp.bfloat16)
    grad_w_out = dot_first(attended, grad_att_in)
    grad_b_o = jnp.sum(grad_att_in.astype(jnp.float32), axis=0)
    grad_self_heads = to_heads(dot_last(grad_att_in, w_out).astype(jnp.bfloat16), HEADS)

    def self_backward(pieces):
        return head_backward(pieces[0], pieces[1], pieces[2], pieces[3], allowed)

    grad_q_heads, grad_kv_all = lax.map(
        self_backward, (query_heads, keyval_all, grad_self_heads, self_lse)
    )
    grad_kv_own = lax.psum_scatter(
        grad_kv_all.astype(jnp.bfloat16), "ctx", scatter_dimension=1, tiled=True
    )
    grad_values = from_heads(grad_kv_own[:, :, head_width:])
    grad_queries = from_heads(grad_q_heads).astype(jnp.bfloat16)
    grad_proj = jnp.concatenate(
        [grad_queries, from_heads(grad_kv_own[:, :, :head_width]), grad_values], axis=1
    )
    grad_w_qkv = dot_first(tokens, grad_proj)
    grad_b_q = jnp.sum(grad_queries.astype(jnp.float32), axis=0)
    grad_b_v = jnp.sum(grad_values.astype(jnp.float32), axis=0)
    grad_tokens = grad_first + dot_last(grad_proj, w_qkv)
    gain_grads = jnp.stack([grad_gain_one, grad_gain_two, grad_gain_three])
    shift_grads = jnp.stack(
        [
            grad_b_q,
            grad_b_v,
            grad_b_o,
            grad_shift_one,
            grad_b_cq,
            grad_b_cv,
            grad_b_co,
            grad_shift_two,
            grad_b_down,
            grad_shift_three,
        ]
    )
    (
        part_qkv,
        part_out,
        part_cq,
        part_ckv,
        part_cout,
        part_up,
        part_down,
        part_b_up,
        part_gains,
        part_biases,
    ) = (
        lax.psum_scatter(grad_w_qkv, ("ctx", "wsh"), scatter_dimension=0, tiled=True),
        lax.psum_scatter(grad_w_out, ("ctx", "wsh"), scatter_dimension=0, tiled=True),
        lax.psum_scatter(grad_w_cq, ("ctx", "wsh"), scatter_dimension=0, tiled=True),
        lax.psum_scatter(grad_w_ckv, ("ctx", "wsh"), scatter_dimension=0, tiled=True),
        lax.psum_scatter(grad_w_cout, ("ctx", "wsh"), scatter_dimension=0, tiled=True),
        lax.psum_scatter(grad_w_up, ("ctx", "wsh"), scatter_dimension=0, tiled=True),
        lax.psum_scatter(grad_w_down, ("ctx", "wsh"), scatter_dimension=0, tiled=True),
        lax.psum_scatter(grad_b_up, ("ctx", "wsh"), scatter_dimension=0, tiled=True),
        lax.psum_scatter(gain_grads, ("ctx", "wsh"), scatter_dimension=1, tiled=True),
        lax.psum_scatter(shift_grads, ("ctx", "wsh"), scatter_dimension=1, tiled=True),
    )
    (
        total_qkv,
        total_out,
        total_cq,
        total_ckv,
        total_cout,
        total_up,
        total_down,
        total_b_up,
        total_gains,
        total_biases,
    ) = (
        lax.psum(part_qkv.astype(jnp.bfloat16), "grp").astype(jnp.float32),
        lax.psum(part_out.astype(jnp.bfloat16), "grp").astype(jnp.float32),
        lax.psum(part_cq.astype(jnp.bfloat16), "grp").astype(jnp.float32),
        lax.psum(part_ckv.astype(jnp.bfloat16), "grp").astype(jnp.float32),
        lax.psum(part_cout.astype(jnp.bfloat16), "grp").astype(jnp.float32),
        lax.psum(part_up.astype(jnp.bfloat16), "grp").astype(jnp.float32),
        lax.psum(part_down.astype(jnp.bfloat16), "grp").astype(jnp.float32),
        lax.psum(part_b_up.astype(jnp.bfloat16), "grp").astype(jnp.float32),
        lax.psum(part_gains.astype(jnp.bfloat16), "grp").astype(jnp.float32),
        lax.psum(part_biases.astype(jnp.bfloat16), "grp").astype(jnp.float32),
    )
    return (
        output[None, None],
        grad_tokens[None, None],
        grad_memory[None, None],
        total_qkv,
        total_out,
        total_cq,
        total_ckv,
        total_cout,
        total_up,
        total_down,
        total_b_up,
        total_gains,
        total_biases,
    )


def solution(mesh):
    in_specs = (
        P("grp", "wsh", "ctx", None),
        P("grp", "wsh", "ctx", None),
        P("grp", "wsh", "ctx", None),
        P("grp", "wsh", None),
        P("grp", "wsh", None),
        P("grp", "wsh", None, None),
        P(),
        P(),
        P(),
        P(),
        P(),
        P(),
        P(),
        P(),
        P(),
        P(),
    )
    out_specs = (
        P("grp", "wsh", "ctx", None),
        P("grp", "wsh", "ctx", None),
        P("grp", "wsh", "ctx", None),
        P(("ctx", "wsh"), None),
        P(("ctx", "wsh"), None),
        P(("ctx", "wsh"), None),
        P(("ctx", "wsh"), None),
        P(("ctx", "wsh"), None),
        P(("ctx", "wsh"), None),
        P(("ctx", "wsh"), None),
        P(("ctx", "wsh")),
        P(None, ("ctx", "wsh")),
        P(None, ("ctx", "wsh")),
    )
    body = layer_shards if mesh.shape["ctx"] == HEADS else shards
    return jax.shard_map(body, mesh=mesh, in_specs=in_specs, out_specs=out_specs, check_vma=False)
```

```python
import functools

import jax
import jax.numpy as jnp
from jax import lax
from jax.experimental import pallas as pl
from jax.experimental.pallas import tpu as pltpu
from jax.sharding import PartitionSpec as P

HEADS = 8
BLK = 128
CBLK = 16


NEG_FILL = -1000000000.0
EPS_NORM = 1e-05


MESH_ID = pl.DeviceIdType.MESH
TILE = 512
STEP = 256
KEYS = 1024
BIG_VMEM = 62 << 20
LOW = jnp.bfloat16
WIDE = jnp.float32
SHARDS = 16
HALF = 16
ROWS = 4
PIECES = dict(
    up0=1024, up1=1024, down0=1024, down1=1024, cross=1024, out=512, ckv=1024, wq=512, wk=512, wv=512
)
TURNS = dict(up0=0, up1=1, down0=0, down1=1, cross=0, out=0, ckv=0, wq=2, wk=2, wv=2)
FEW_ROWS = 24


def nn(left, right):
    return lax.dot_general(
        left, right, (((1,), (0,)), ((), ())), preferred_element_type=WIDE
    )


def nt(left, right):
    return lax.dot_general(
        left, right, (((1,), (1,)), ((), ())), preferred_element_type=WIDE
    )


def swap(block):
    return block.astype(WIDE).T.astype(block.dtype)


def plus(left, right):
    return left.astype(WIDE) + right.astype(WIDE)


def column_sums(values):
    return jnp.sum(values.astype(WIDE), axis=0, keepdims=True)


def norm_parts(values):
    center = values - jnp.mean(values, axis=-1, keepdims=True)
    spread = jnp.mean(center * center, axis=-1, keepdims=True)
    scale = lax.rsqrt(spread + EPS_NORM)
    return center * scale, scale


def norm_pull(unit, scale, gain, upstream):
    inner = upstream * gain
    first = jnp.mean(inner, axis=-1, keepdims=True)
    second = jnp.mean(inner * unit, axis=-1, keepdims=True)
    return scale * (inner - first - unit * second)


def hide_later(scores, lead):
    rows = lax.broadcasted_iota(jnp.int32, scores.shape, 0)
    cols = lax.broadcasted_iota(jnp.int32, scores.shape, 1)
    return jnp.where(rows - cols <= lead, scores, NEG_FILL)


def hide_prompt(scores, offset_ref, open_ref, tile, chunk, prompt_blocks):
    span, key_span = TILE // BLK, scores.shape[0] // BLK
    rows = lax.broadcasted_iota(jnp.int32, (BLK, BLK), 0)
    columns = []
    for q_sub in range(span):
        pieces = []
        for k_sub in range(key_span):
            key_block = chunk * key_span + k_sub
            opened = open_ref[tile * span + q_sub - prompt_blocks, key_block]
            opened = jnp.where(key_block == 0, 1, opened)
            limit = jnp.where(opened > 0, offset_ref[0], 0) - key_block * BLK
            part = scores[k_sub * BLK : (k_sub + 1) * BLK, q_sub * BLK : (q_sub + 1) * BLK]
            pieces.append(jnp.where(rows < limit, part, NEG_FILL))
        columns.append(jnp.concatenate(pieces, axis=0))
    return jnp.concatenate(columns, axis=1)


def apart(upper, lower):
    none = jnp.zeros_like(upper)
    return jnp.concatenate(
        [jnp.concatenate([upper, none], axis=1), jnp.concatenate([none, lower], axis=1)], axis=0
    )


def apart_columns(pair):
    lanes = lax.broadcasted_iota(jnp.int32, pair.shape, 1)
    wide = pair.astype(WIDE)
    left = jnp.where(lanes < pair.shape[1] // 2, wide, 0.0).astype(pair.dtype)
    right = jnp.where(lanes < pair.shape[1] // 2, 0.0, wide).astype(pair.dtype)
    return jnp.concatenate([left, right], axis=0)


def remote(src_ref, dst_ref, send_sem, recv_sem, target):
    return pltpu.make_async_remote_copy(
        src_ref=src_ref,
        dst_ref=dst_ref,
        send_sem=send_sem,
        recv_sem=recv_sem,
        device_id=target,
        device_id_type=MESH_ID,
    )


class Bag:
    def __init__(self, items):
        self.__dict__.update(items)


class Spot:
    def __init__(self):
        ctx = lax.axis_index("ctx")
        self.grp, self.ctx, self.wsh = lax.axis_index("grp"), ctx, lax.axis_index("wsh")
        self.row, self.col = ctx // 2, lax.rem(ctx, 2)
        self.core_peer = (1 - self.grp, ctx, self.wsh)
        self.wsh_peer = (self.grp, ctx, 1 - self.wsh)
        self.col_peer = self.at_row_col(self.row, 1 - self.col)
        self.cross_peer = (self.grp, self.row * 2 + 1 - self.col, 1 - self.wsh)
        self.rows_by_step = [lax.rem(self.row + step, ROWS) for step in range(ROWS)]
        self.row_peers = [self.at_row_col(row, self.col) for row in self.rows_by_step]
        self.far_peers = [(1 - self.grp, peer[1], self.wsh) for peer in self.row_peers]
        self.ways = [
            (self.wsh_peer, self.col, 1 - self.wsh),
            (self.col_peer, 1 - self.col, self.wsh),
            (self.cross_peer, 1 - self.col, 1 - self.wsh),
        ]
        self.ctx_by_step = [lax.rem(ctx + step, HEADS) for step in range(HEADS)]
        self.ctx_peers = [(self.grp, peer, self.wsh) for peer in self.ctx_by_step]

    def at_row_col(self, row, col):
        return (self.grp, row * 2 + col, self.wsh)

    def greet(self):
        barrier = pltpu.get_barrier_semaphore()
        targets = [self.core_peer, self.wsh_peer, self.cross_peer]
        targets += self.ctx_peers[1:] + self.far_peers[1:]
        for target in targets:
            pl.semaphore_signal(barrier, inc=1, device_id=target, device_id_type=MESH_ID)
        return len(targets)


class Exchange:
    def __init__(self, spot, source, sems, parts):
        self.spot, self.source, self.sems, self.parts = spot, source, sems, parts
        self.copies = [[] for _ in parts]

    def start(self, part=0):
        spot, own_blocks = self.spot, self.source.shape[1]
        first, count, rows, target, target_rows = self.parts[part]
        here = (pl.ds(spot.ctx * own_blocks + first, count), target_rows)
        there = (pl.ds(first, count), rows)
        for step in range(1, HEADS):
            copy = remote(
                self.source.at[(spot.ctx_by_step[step],) + there], target.at[here],
                self.sems.at[0, step, part], self.sems.at[1, step, part], spot.ctx_peers[step],
            )
            copy.start()
            self.copies[part].append(copy)
        target[here] = self.source[(spot.ctx,) + there]

    def wait(self, part=0):
        for copy in self.copies[part]:
            copy.wait()


class Piece:
    def __init__(self, spot, turn, refs, outs):
        self.spot, self.turn, self.sems, self.outs = spot, turn, refs.sems, outs
        self.part, self.core_land, self.hop_land = refs.part, refs.core_land, refs.hop_land
        self.turn_land, self.row_land = refs.turn_land, refs.row_land
        self.turn_sum = self.core_land.at[:, 0]
        self.copies = []
        self.stage = 0

    def copy(self, index, source, target_ref, target):
        copy = remote(source, target_ref, self.sems.at[0, index], self.sems.at[1, index], target)
        copy.start()
        self.copies.append(copy)

    def finish(self):
        for copy in self.copies:
            copy.wait()
        self.copies = []

    def send_rows(self):
        spot = self.spot
        for step in range(1, ROWS):
            self.copy(
                2 + step, self.turn_land.at[spot.rows_by_step[step]],
                self.row_land.at[step - 1], spot.row_peers[step],
            )

    def steps(self, stage):
        while self.stage < stage:
            self.step()

    def step(self):
        spot, part = self.spot, self.part
        own = spot.grp
        if self.stage == 0:
            self.copy(0, part.at[1 - own], self.core_land, spot.core_peer)
        elif self.stage == 1:
            self.finish()
            part[own] = plus(part[own], self.core_land[...]).astype(LOW)
            if self.turn == 2:
                for way, (target, to_col, to_wsh) in enumerate(spot.ways):
                    self.copy(
                        1 + way, part.at[own, :, to_col, to_wsh], self.hop_land.at[way],
                        target,
                    )
            elif self.turn == 0:
                self.copy(1, part.at[own, :, :, 1 - spot.wsh], self.hop_land, spot.wsh_peer)
            else:
                self.copy(1, part.at[own, :, 1 - spot.col], self.hop_land, spot.col_peer)
        elif self.stage == 2:
            self.finish()
            if self.turn == 2:
                total = part[own, :, spot.col, spot.wsh].astype(WIDE)
                for way in range(3):
                    total = total + self.hop_land[way].astype(WIDE)
                self.turn_land[...] = total.astype(LOW)
                self.row_land[own, spot.row] = self.turn_land[spot.row]
                for step in range(ROWS):
                    for side, peers in enumerate((spot.row_peers, spot.far_peers)):
                        if step + side > 0:
                            self.copy(
                                4 + 2 * step + side, self.turn_land.at[spot.rows_by_step[step]],
                                self.row_land.at[own, spot.row], peers[step],
                            )
                self.stage = 4
                return
            if self.turn == 0:
                mine = part[own, :, :, spot.wsh]
                away, target = 1 - spot.col, spot.col_peer
            else:
                mine = part[own, :, spot.col]
                away, target = 1 - spot.wsh, spot.wsh_peer
            self.turn_sum[...] = plus(mine, self.hop_land[...]).astype(LOW)
            self.copy(2, self.turn_sum.at[:, away], self.turn_land, target)
        elif self.stage == 3:
            self.finish()
            keep = spot.col if self.turn == 0 else spot.wsh
            self.turn_land[...] = plus(self.turn_sum[:, keep], self.turn_land[...]).astype(LOW)
            self.send_rows()
        elif self.stage == 4:
            self.finish()
            if self.turn == 2:
                (out_ref, _, column, width), = self.outs
                for half in range(2):
                    total = self.row_land[half, 0].astype(WIDE)
                    for row in range(1, ROWS):
                        total = total + self.row_land[half, row].astype(WIDE)
                    out_ref[half * HALF : (half + 1) * HALF, column : column + width] = total
                self.stage = 6
                return
            total = self.turn_land[spot.row].astype(WIDE)
            for step in range(ROWS - 1):
                total = total + self.row_land[step].astype(WIDE)
            at = 0
            for index, (out_ref, row, column, width) in enumerate(self.outs):
                here = (
                    pl.ds(pl.multiple_of(row + own * HALF, HALF), HALF),
                    slice(column, column + width),
                )
                out_ref[here] = total[:, at : at + width]
                at += width
                self.copy(7 + index, out_ref.at[here], out_ref.at[here], spot.core_peer)
        elif self.stage == 5:
            self.finish()
        self.stage += 1


def layer_kernel(
    prompt_blocks,
    deal_ref, offset_ref, open_ref, tokens_ref, memory_ref, cot_ref,
    w_qkv_hbm, w_out_hbm, w_cq_hbm, w_ckv_hbm, w_cout_hbm, w_up_hbm, w_down_hbm,
    b_up_ref, gains_ref, biases_ref,
    output_ref, g_stream_ref, g_memory_ref, o_qkv_ref, o_out_ref, o_cq_ref, o_ckv_ref, o_cout_ref,
    o_up_ref, o_down_ref, o_b_up_ref, o_gains_ref, o_biases_ref,
    refs,
):
    spot = Spot()
    greeted = spot.greet()
    row_count, width = tokens_ref.shape
    own_blocks = row_count // BLK
    head = width // HEADS
    blocks = own_blocks * HEADS
    mem_rows = memory_ref.shape[0]
    mem_total = mem_rows * HEADS
    hidden_width = b_up_ref.shape[1]
    chunks = hidden_width // width
    pairs = HEADS // 2
    score_scale = head ** (-0.5)
    prompt_tiles = prompt_blocks * BLK // TILE
    tiles = blocks * BLK // TILE

    sources = dict(
        w_qkv=w_qkv_hbm, w_ckv=w_ckv_hbm, w_out=w_out_hbm, w_cq=w_cq_hbm, w_cout=w_cout_hbm,
        w_up=w_up_hbm, w_down=w_down_hbm,
    )
    loads = Bag(
        {
            name: pltpu.make_async_copy(source, getattr(refs, name), refs.load_sem.at[index])
            for index, (name, source) in enumerate(sources.items())
        }
    )
    for name in sources:
        getattr(loads, name).start()

    outs = dict(
        up0=[(o_up_ref, 0, 0, 1024)],
        up1=[(o_up_ref, 0, 1024, 1024)],
        down0=[(o_down_ref, 0, 0, 512), (o_down_ref, 32, 0, 512)],
        down1=[(o_down_ref, 64, 0, 512), (o_down_ref, 96, 0, 512)],
        cross=[(o_cout_ref, 0, 0, 512), (o_cq_ref, 0, 0, 512)],
        out=[(o_out_ref, 0, 0, 512)],
        ckv=[(o_ckv_ref, 0, 0, 1024)],
        wq=[(o_qkv_ref, 0, 0, 512)],
        wk=[(o_qkv_ref, 0, 512, 512)],
        wv=[(o_qkv_ref, 0, 1024, 512)],
    )
    piece = Bag(
        {
            name: Piece(spot, TURNS[name], Bag(refs.pieces[name]), outs[name])
            for name in PIECES
        }
    )
    ups, downs = (piece.up0, piece.up1), (piece.down0, piece.down1)

    def put_rows(to, values, column):
        span = values.shape[1]
        split = values.astype(LOW).reshape(ROWS, 2, 2, 2, HALF, span)
        for half in range(2):
            to.part[half, :, :, :, :, column : column + span] = split[:, :, :, half]

    few_ref = refs.few_sum
    few_ref[...] = jnp.zeros_like(few_ref)

    def few(row, values):
        few_ref[row : row + 1, :] = values

    def gain(row):
        return gains_ref[row : row + 1, :]

    def bias(row):
        return biases_ref[row : row + 1, :]

    send_ref = refs.head_send
    loads.w_qkv.wait()
    zeros_row = jnp.zeros((1, width), WIDE)
    pair_rows, last_rows = slice(0, 2 * head), slice(2 * head, 3 * head)
    pair_land, last_land = refs.pair_land, refs.last_land
    to_heads_copy = Exchange(
        spot, send_ref, refs.to_heads_sem,
        [(block, 1, pair_rows, pair_land, pair_rows) for block in range(own_blocks)]
        + [(0, own_blocks, last_rows, last_land, slice(0, head))],
    )
    pair_bias = jnp.concatenate([bias(0), zeros_row], axis=1)
    for block in range(own_blocks):
        rows = slice(block * BLK, (block + 1) * BLK)
        projected = (nn(tokens_ref[rows, :], refs.w_qkv[:, : 2 * width]) + pair_bias).astype(LOW)
        turned = projected.astype(WIDE).T
        turned = jnp.concatenate([turned[:width] * score_scale, turned[width:]], axis=0).astype(LOW)
        for h in range(HEADS):
            for kind in range(2):
                at = kind * width + h * head
                send_ref[h, block, kind * head : (kind + 1) * head, :] = turned[at : at + head]
        if block == 0:
            pl.semaphore_wait(pltpu.get_barrier_semaphore(), greeted)
        to_heads_copy.start(block)
    for block in range(own_blocks):
        rows = slice(block * BLK, (block + 1) * BLK)
        turned = swap((nn(tokens_ref[rows, :], refs.w_qkv[:, 2 * width :]) + bias(1)).astype(LOW))
        for h in range(HEADS):
            send_ref[h, block, last_rows, :] = turned[h * head : (h + 1) * head]
    to_heads_copy.start(own_blocks)
    all_ref = refs.memory_all
    all_ref[spot.col, spot.row] = memory_ref[...]

    def pass_on(step):
        row = lax.rem(spot.row + ROWS - step, ROWS)
        copy = remote(
            all_ref.at[spot.col, row], all_ref.at[spot.col, row],
            refs.spread_sem.at[0, ROWS + step], refs.spread_sem.at[1, ROWS + step], spot.col_peer,
        )
        copy.start()
        return copy

    passed = [pass_on(0)]
    inv_ref = refs.inverse
    for pos in range(blocks):
        row = jnp.int32(0)
        for other in range(1, blocks):
            row = jnp.where(deal_ref[other] == pos, other, row)
        inv_ref[pos] = row
    for block in range(own_blocks):
        to_heads_copy.wait(block)

    q_ref, kv_ref = refs.q, refs.kv
    no_head = jnp.zeros((head, BLK), LOW)
    no_tile = jnp.zeros((head, TILE), LOW)
    qt_ref, kt_ref, vt_ref = refs.qt, refs.kt, refs.vt
    exact_ref, lse_ref = refs.exact, refs.lse
    for pos in range(blocks):
        block = pair_land[inv_ref[pos]]
        at = slice(pos * BLK, (pos + 1) * BLK)
        qt_ref[:, at] = block[:head]
        kt_ref[:, at] = block[head:]
        kv_ref[at, :] = swap(jnp.concatenate([block[head:], no_head], axis=0))

    prompt_chunks = prompt_blocks * BLK // KEYS
    group = KEYS // TILE

    def key_spans(chunk, tile, step, state):
        base = 0 if chunk < prompt_chunks else prompt_chunks
        lead = tile * TILE - chunk * KEYS
        state = step(chunk, state, lambda s, c: hide_later(s, lead))
        for other in range(base, chunk):
            state = step(other, state, lambda s, c: s)
        for other in range(base):
            state = step(
                other,
                state,
                lambda s, c: hide_prompt(s, offset_ref, open_ref, tile, c, prompt_blocks),
            )
        return state

    def top_tile(chunk, tile):
        here = pl.ds(pl.multiple_of(tile * TILE, TILE), TILE)
        queries = jnp.concatenate([qt_ref[:, here], no_tile], axis=0)

        def top_step(other, top, hide):
            scores = nn(kv_ref[other * KEYS : (other + 1) * KEYS, :], queries)
            scores = hide(scores, other).reshape(KEYS // 8, 8, TILE)
            return jnp.maximum(top, jnp.max(scores, axis=0))

        top = key_spans(chunk, tile, top_step, jnp.full((8, TILE), NEG_FILL, WIDE))
        lse_ref[:, here] = jnp.max(top, axis=0, keepdims=True)

    def each_tile(chunk, step):
        def body(tile, carry):
            step(chunk, tile)
            return carry

        lax.fori_loop(chunk * group, (chunk + 1) * group, body, 0)

    for chunk in range(tiles // group):
        each_tile(chunk, top_tile)
    to_heads_copy.wait(own_blocks)
    spread = []
    for step in range(1, ROWS):
        copy = remote(
            memory_ref, all_ref.at[spot.col, spot.row],
            refs.spread_sem.at[0, step], refs.spread_sem.at[1, step], spot.row_peers[step],
        )
        copy.start()
        spread.append(copy)
    for pos in range(blocks):
        vt_ref[:, pos * BLK : (pos + 1) * BLK] = last_land[inv_ref[pos]]

    def tile_spans(tile, chunk_step, state):
        state = chunk_step(tile, state, lambda s, c: hide_later(s, 0))
        first = jnp.where(tile >= prompt_tiles, prompt_tiles, 0)
        state = lax.fori_loop(first, tile, lambda c, s: chunk_step(c, s, lambda x, _: x), state)
        return lax.fori_loop(
            0,
            first,
            lambda c, s: chunk_step(
                c, s, lambda x, cc: hide_prompt(x, offset_ref, open_ref, tile, cc, prompt_blocks)
            ),
            state,
        )

    def mix_tile(chunk, tile):
        here = pl.ds(pl.multiple_of(tile * TILE, TILE), TILE)
        queries = jnp.concatenate([qt_ref[:, here], no_tile], axis=0)
        top = lse_ref[:, here]

        def mix_step(other, state, hide):
            total, mixed = state
            there = slice(other * KEYS, (other + 1) * KEYS)
            weights = jnp.exp(hide(nn(kv_ref[there, :], queries), other) - top)
            total = total + jnp.sum(weights.reshape(KEYS // 8, 8, TILE), axis=0)
            return total, mixed + nn(vt_ref[:, there], weights.astype(LOW))

        total, mixed = key_spans(
            chunk, tile, mix_step, (jnp.zeros((8, TILE), WIDE), jnp.zeros((head, TILE), WIDE))
        )
        total = jnp.sum(total, axis=0, keepdims=True)
        exact = mixed / total
        for sub in range(TILE // BLK):
            exact_ref[tile * (TILE // BLK) + sub] = exact[:, sub * BLK : (sub + 1) * BLK]
        lse_ref[:, here] = top + jnp.log(total)

    for chunk in range(tiles // group):
        if chunk == tiles // group - 1:
            spread[0].wait()
            passed.append(pass_on(1))
        each_tile(chunk, mix_tile)
    for step in range(2, ROWS):
        spread[step - 1].wait()
        passed.append(pass_on(step))
    mixed_ref = refs.mixed_send
    for row in range(blocks):
        mixed_ref[row // own_blocks, row % own_blocks] = exact_ref[deal_ref[row]].astype(LOW)
    all_rows = slice(0, head)
    from_heads_copy = Exchange(
        spot, mixed_ref, refs.from_heads_sem,
        [(0, own_blocks, all_rows, refs.mixed_land, all_rows)],
    )
    from_heads_copy.start()

    for pos in range(blocks):
        at = slice(pos * BLK, (pos + 1) * BLK)
        kv_ref[at, :] = swap(jnp.concatenate([kt_ref[:, at], vt_ref[:, at]], axis=0))

    ck_ref, cv_ref, ckt_ref, cvt_ref = refs.ck, refs.cv, refs.ckt, refs.cvt
    loads.w_ckv.wait()

    def encode(col, row):
        rows = pl.ds(pl.multiple_of((row * 2 + col) * mem_rows, mem_rows), mem_rows)
        both = nn(all_ref[col, row], refs.w_ckv[...])
        keys = both[:, :width].astype(LOW)
        values = (both[:, width:] + bias(5)).astype(LOW)
        ck_ref[rows, :] = keys
        cv_ref[rows, :] = values
        ckt_ref[:, rows] = swap(keys)
        cvt_ref[:, rows] = swap(values)

    for row in range(ROWS):
        encode(spot.col, row)
    for copy in passed:
        copy.wait()
    for row in range(ROWS):
        encode(1 - spot.col, row)

    loads.w_out.wait()
    from_heads_copy.wait()
    attended_t_ref = refs.attended_t
    unit_one_ref, unit_two_ref = refs.unit_one, refs.unit_two
    low_one_ref, low_two_ref = refs.low_one, refs.low_two
    for block in range(own_blocks):
        at = slice(block * BLK, (block + 1) * BLK)
        for h in range(HEADS):
            attended_t_ref[h * head : (h + 1) * head, at] = refs.mixed_land[h * own_blocks + block]
    cq_ref, cqt_ref = refs.cq, refs.cqt
    loads.w_cq.wait()

    def rows_at(block):
        return pl.ds(pl.multiple_of(block * BLK, BLK), BLK)

    def first_norm(block, carry):
        rows = rows_at(block)
        attended = swap(attended_t_ref[:, rows])
        first_sum = tokens_ref[rows, :].astype(WIDE) + nn(attended, refs.w_out[...]) + bias(2)
        unit, scale = norm_parts(first_sum)
        unit_one_ref[rows, :] = unit
        refs.scale_one[rows, :] = scale
        low_one = (unit * gain(0) + bias(3)).astype(LOW)
        low_one_ref[rows, :] = low_one
        cross_query = (nn(low_one, refs.w_cq[...]) + bias(4)).astype(LOW).astype(WIDE)
        cross_query = cross_query * score_scale
        cq_ref[rows, :] = cross_query.astype(LOW)
        cqt_ref[:, rows] = cross_query.T.astype(LOW)
        return carry

    lax.fori_loop(0, own_blocks, first_norm, 0)

    pair_width = 2 * head
    cross_exact_ref, cross_lse_ref = refs.cross_exact, refs.cross_lse
    steps = mem_total // STEP

    def pair_at(pair):
        return pl.ds(pl.multiple_of(pair * pair_width, pair_width), pair_width)

    def step_at(step):
        return pl.ds(pl.multiple_of(step * STEP, STEP), STEP)

    def cross_forward(h, carry):
        lanes = pair_at(h // 2)
        at = pl.ds(pl.multiple_of(h * head, head), head)
        own_rows = lax.broadcasted_iota(jnp.int32, (pair_width, row_count), 0) // head
        queries = jnp.where(own_rows == lax.rem(h, 2), cqt_ref[lanes, :].astype(WIDE), 0.0)
        queries = queries.astype(LOW)

        def first_pass(step, top):
            scores = nn(ck_ref[step_at(step), lanes], queries)
            return jnp.maximum(top, jnp.max(scores.reshape(STEP // 8, 8, row_count), axis=0))

        top = lax.fori_loop(
            0, steps, first_pass, jnp.full((8, row_count), NEG_FILL, WIDE), unroll=True
        )
        top = jnp.max(top, axis=0, keepdims=True)

        def second_pass(step, state):
            total, mixed = state
            weights = jnp.exp(nn(ck_ref[step_at(step), lanes], queries) - top)
            total = total + jnp.sum(weights.reshape(STEP // 8, 8, row_count), axis=0)
            return total, mixed + nn(cvt_ref[at, step_at(step)], weights.astype(LOW))

        total, mixed = lax.fori_loop(
            0, steps, second_pass,
            (jnp.zeros((8, row_count), WIDE), jnp.zeros((head, row_count), WIDE)), unroll=True,
        )
        total = jnp.sum(total, axis=0, keepdims=True)
        cross_lse_ref[h] = top + jnp.log(total)
        cross_exact_ref[at, :] = mixed / total
        return carry

    lax.fori_loop(0, HEADS, cross_forward, 0)
    cross_low_ref = refs.cross_low
    total_ref, hidden_ref, slope_ref = g_stream_ref, refs.hidden, refs.slope
    loads.w_cout.wait()

    def second_norm(block, carry):
        rows = rows_at(block)
        cross_low = cross_exact_ref[:, rows].T.astype(LOW)
        cross_low_ref[rows, :] = cross_low
        normed_one = unit_one_ref[rows, :] * gain(0) + bias(3)
        unit, scale = norm_parts(normed_one + nn(cross_low, refs.w_cout[...]) + bias(6))
        unit_two_ref[rows, :] = unit
        refs.scale_two[rows, :] = scale
        normed_two = unit * gain(1) + bias(7)
        low_two_ref[rows, :] = normed_two.astype(LOW)
        total_ref[rows, :] = normed_two + bias(8)
        return carry

    lax.fori_loop(0, own_blocks, second_norm, 0)

    loads.w_up.wait()
    loads.w_down.wait()
    w_up_ref, w_down_ref = refs.w_up, refs.w_down

    def chunk_at(chunk):
        return pl.ds(pl.multiple_of(chunk * width, width), width)

    def up_step(chunk, carry):
        pre = nn(low_two_ref[...], w_up_ref[:, chunk_at(chunk)]) + b_up_ref[:, chunk_at(chunk)]
        normal = 0.5 + 0.5 * lax.erf(pre * (2.0**-0.5))
        hidden = (pre * normal).astype(LOW)
        hidden_ref[chunk] = hidden
        slope = normal + pre * jnp.exp(-0.5 * pre * pre) * ((2.0 * jnp.pi) ** -0.5)
        slope_ref[chunk] = slope.astype(LOW)
        total_ref[...] += nn(hidden, w_down_ref[chunk_at(chunk), :])
        return carry

    lax.fori_loop(0, chunks, up_step, 0)

    low_third_ref = refs.low_third
    no_sums = (zeros_row, zeros_row, zeros_row)

    def third_norm(block, sums):
        rows = rows_at(block)
        unit, scale = norm_parts(total_ref[rows, :])
        output_ref[rows, :] = unit * gain(2) + bias(9)
        upstream = cot_ref[rows, :].astype(WIDE)
        grad = norm_pull(unit, scale, gain(2), upstream)
        low = grad.astype(LOW)
        low_third_ref[rows, :] = low
        total_ref[rows, :] = grad
        return (
            sums[0] + column_sums(upstream * unit),
            sums[1] + column_sums(upstream),
            sums[2] + column_sums(low),
        )

    sums = lax.fori_loop(0, own_blocks, third_norm, no_sums)
    few(6, sums[0])
    few(16, sums[1])
    few(15, sums[2])

    turned_ref = refs.turned
    turned_ref[...] = swap(low_two_ref[...])
    for chunk in range(chunks):
        rows = slice(chunk * width, (chunk + 1) * width)
        grad_hidden = nt(low_third_ref[...], w_down_ref[rows, :])
        grad_pre = (grad_hidden * slope_ref[chunk].astype(WIDE)).astype(LOW)
        few(chunk, column_sums(grad_pre))
        total_ref[...] += nt(grad_pre, w_up_ref[:, rows])
        grad_up = nn(turned_ref[...], grad_pre)
        put_rows(ups[chunk // 2], grad_up, (chunk % 2) * width)
        if chunk % 2 == 1:
            ups[chunk // 2].step()
        if chunk == 2:
            piece.up0.step()
        grad_down = nn(swap(hidden_ref[chunk]), low_third_ref[...])
        split = grad_down.astype(LOW).reshape(2, 2, 4, 2, HALF, width)
        for part in range(4):
            to = downs[part // 2].part
            column = (part % 2) * width
            for half in range(2):
                to[half, chunk, :, :, :, column : column + width] = split[:, :, part, half]
    piece.down0.step()
    piece.down1.step()

    dco_ref, dcot_ref = refs.dco, refs.dcot

    def second_back(block, sums):
        rows = rows_at(block)
        upstream = total_ref[rows, :]
        unit = unit_two_ref[rows, :]
        grad = norm_pull(unit, refs.scale_two[rows, :], gain(1), upstream)
        low = grad.astype(LOW)
        total_ref[rows, :] = grad
        low_third_ref[rows, :] = low
        dco_ref[rows, :] = nt(low, refs.w_cout[...]).astype(LOW)
        dcot_ref[:, rows] = nt(refs.w_cout[...], low).astype(LOW)
        return (
            sums[0] + column_sums(upstream * unit),
            sums[1] + column_sums(upstream),
            sums[2] + column_sums(low),
        )

    sums = lax.fori_loop(0, own_blocks, second_back, no_sums)
    few(5, sums[0])
    few(14, sums[1])
    few(13, sums[2])
    put_rows(piece.cross, nn(swap(cross_low_ref[...]), low_third_ref[...]), 0)
    piece.up1.step()
    piece.down0.step()
    piece.down1.step()

    dcqt_ref = refs.dcqt
    def cross_backward(pair, carry):
        lanes = pair_at(pair)
        low_half = pl.ds(pl.multiple_of(pair * pair_width, head), head)
        high_half = pl.ds(pl.multiple_of(pair * pair_width + head, head), head)
        queries_t = apart(cqt_ref[low_half, :], cqt_ref[high_half, :])
        upstream_t = apart(dcot_ref[low_half, :], dcot_ref[high_half, :])
        queries = apart_columns(cq_ref[:, lanes])
        upstream = apart_columns(dco_ref[:, lanes])
        dots = cross_exact_ref[lanes, :] * dcot_ref[lanes, :].astype(WIDE)
        delta = jnp.concatenate(
            [column_sums(dots[:head]), column_sums(dots[head:])], axis=1
        )
        lse = jnp.concatenate([cross_lse_ref[2 * pair], cross_lse_ref[2 * pair + 1]], axis=1)
        dcqt_ref[lanes, :] = jnp.zeros((pair_width, row_count), WIDE)

        def backward_step(step, carry):
            there = step_at(step)
            weights = jnp.exp(nn(ck_ref[there, lanes], queries_t) - lse)
            grad_weights = nn(cv_ref[there, lanes], upstream_t)
            grad_scores = (weights * (grad_weights - delta)).astype(LOW)
            ck_ref[there, lanes] = nn(grad_scores, queries).astype(LOW)
            cv_ref[there, lanes] = nn(weights.astype(LOW), upstream).astype(LOW)
            dcqt_ref[low_half, :] += nn(ckt_ref[low_half, there], grad_scores[:, :row_count])
            dcqt_ref[high_half, :] += nn(ckt_ref[high_half, there], grad_scores[:, row_count:])
            return carry

        lax.fori_loop(0, steps, backward_step, 0)
        return carry

    lax.fori_loop(0, pairs, cross_backward, 0)
    upstream_send = refs.mixed_send

    def first_back(block, sums):
        rows = rows_at(block)
        grad_cq = (dcqt_ref[:, rows].T * score_scale).astype(LOW)
        dco_ref[rows, :] = grad_cq
        upstream = total_ref[rows, :] + nt(grad_cq, refs.w_cq[...])
        unit = unit_one_ref[rows, :]
        grad = norm_pull(unit, refs.scale_one[rows, :], gain(0), upstream)
        low = grad.astype(LOW)
        total_ref[rows, :] = grad
        low_third_ref[rows, :] = low
        grad_attended_t = nt(refs.w_out[...], low).astype(LOW)
        for h in range(HEADS):
            upstream_send[h, block] = grad_attended_t[h * head : (h + 1) * head, :]
        return (
            sums[0] + column_sums(upstream * unit),
            sums[1] + column_sums(upstream),
            sums[2] + column_sums(low),
            sums[3] + column_sums(grad_cq),
        )

    sums = lax.fori_loop(0, own_blocks, first_back, no_sums + (zeros_row,))
    few(4, sums[0])
    few(10, sums[1])
    few(9, sums[2])
    few(11, sums[3])
    up_heads_copy = Exchange(
        spot, upstream_send, refs.up_heads_sem,
        [(0, own_blocks, all_rows, refs.up_land, all_rows)],
    )
    up_heads_copy.start()
    turned_ref[...] = swap(low_one_ref[...])
    put_rows(piece.cross, nn(turned_ref[...], dco_ref[...]), width)
    piece.cross.steps(1)
    put_rows(piece.out, nn(attended_t_ref[...], low_third_ref[...]), 0)
    piece.out.steps(1)
    for part in range(HEADS):
        rows = slice(part * mem_rows, (part + 1) * mem_rows)
        ckt_ref[:, rows] = swap(all_ref[part % 2, part // 2])
        grad = nt(ck_ref[rows, :], refs.w_ckv[:, :width]) + nt(cv_ref[rows, :], refs.w_ckv[:, width:])
        w_up_ref[
            (part // 2) * mem_rows : (part // 2 + 1) * mem_rows,
            (part % 2) * width : (part % 2 + 1) * width,
        ] = grad.astype(LOW)
    g_land = refs.memory_land
    other_side = pl.ds(pl.multiple_of((1 - spot.col) * width, width), width)
    own_side = pl.ds(pl.multiple_of(spot.col * width, width), width)
    memory_copy = remote(
        w_up_ref.at[:, other_side], g_land, refs.memory_sem.at[0, 0], refs.memory_sem.at[1, 0],
        spot.col_peer,
    )
    put_rows(piece.ckv, nn(ckt_ref[...], ck_ref[...]), 0)
    put_rows(piece.ckv, nn(ckt_ref[...], cv_ref[...]), width)
    few(12, column_sums(cv_ref[...]))
    piece.ckv.steps(1)
    for pos in range(blocks):
        at = slice(pos * BLK, (pos + 1) * BLK)
        q_ref[at, :] = swap(jnp.concatenate([qt_ref[:, at], no_head], axis=0))
    up_heads_copy.wait()
    for item in ups + downs:
        item.steps(3)
    memory_copy.start()
    for item in (piece.cross, piece.out, piece.ckv):
        item.steps(2)

    upq_ref, upt_ref = refs.up, refs.upt
    dkv_ref, dqt_ref = refs.dkv, refs.dqt
    for pos in range(blocks):
        block = refs.up_land[inv_ref[pos]]
        at = slice(pos * BLK, (pos + 1) * BLK)
        upt_ref[:, at] = block
        upq_ref[at, :] = swap(jnp.concatenate([no_head, block], axis=0))
    dkv_ref[...] = jnp.zeros_like(dkv_ref)

    def backward_tile(tile, carry):
        here = pl.ds(pl.multiple_of(tile * TILE, TILE), TILE)
        queries_t = jnp.concatenate([qt_ref[:, here], no_tile], axis=0)
        upstream_t = jnp.concatenate([no_tile, upt_ref[:, here]], axis=0)
        both = jnp.concatenate([q_ref[here, :], upq_ref[here, :]], axis=0)
        lse = lse_ref[:, here]
        exact = jnp.concatenate(
            [exact_ref[tile * (TILE // BLK) + sub] for sub in range(TILE // BLK)], axis=1
        )
        delta = column_sums(exact * upt_ref[:, here].astype(WIDE))

        def chunk_step(chunk, grad_q, hide):
            there = pl.ds(pl.multiple_of(chunk * TILE, TILE), TILE)
            scores = hide(nn(kv_ref[there, :], queries_t), chunk)
            weights = jnp.exp(scores - lse)
            grad_weights = nn(kv_ref[there, :], upstream_t)
            grad_scores = (weights * (grad_weights - delta)).astype(LOW)
            sides = jnp.concatenate([grad_scores, weights.astype(LOW)], axis=1)
            spread_at = pl.ds(chunk * (TILE // BLK), TILE // BLK)
            dkv_ref[spread_at] += nn(sides, both).reshape(TILE // BLK, BLK, 2 * head)
            return grad_q + nn(kt_ref[:, there], grad_scores)

        grad_q = tile_spans(tile, chunk_step, jnp.zeros((head, TILE), WIDE))
        grad_q = (grad_q * score_scale).astype(LOW)
        for sub in range(TILE // BLK):
            dqt_ref[tile * (TILE // BLK) + sub] = grad_q[:, sub * BLK : (sub + 1) * BLK]
        return carry

    lax.fori_loop(0, tiles // 2, backward_tile, 0)
    for item in ups + downs:
        item.steps(4)
    lax.fori_loop(tiles // 2, tiles, backward_tile, 0)

    back_send = refs.head_send
    back_copy = Exchange(
        spot, back_send, refs.back_sem,
        [
            (0, own_blocks, slice(0, head), pair_land, slice(0, head)),
            (0, own_blocks, slice(head, 2 * head), pair_land, slice(head, 2 * head)),
            (0, own_blocks, last_rows, last_land, slice(0, head)),
        ],
    )
    for row in range(blocks):
        back_send[row // own_blocks, row % own_blocks, :head] = dqt_ref[deal_ref[row]]
    back_copy.start(0)
    for row in range(blocks):
        back_send[row // own_blocks, row % own_blocks, head:] = dkv_ref[deal_ref[row]].T.astype(LOW)
    back_copy.start(1)
    back_copy.start(2)

    ones = jnp.ones((8, BLK), LOW)
    query_sums = jnp.zeros((8, head), WIDE)
    both_sums = jnp.zeros((1, 2 * head), WIDE)
    for pos in range(blocks):
        query_sums = query_sums + nt(ones, dqt_ref[pos])
        both_sums = both_sums + column_sums(dkv_ref[pos])
    own_lanes = lax.broadcasted_iota(jnp.int32, (1, width), 1) // head == spot.ctx
    few(7, jnp.where(own_lanes, jnp.concatenate([query_sums[:1]] * HEADS, axis=1), 0.0))
    few(8, jnp.where(own_lanes, jnp.concatenate([both_sums[:, head:]] * HEADS, axis=1), 0.0))

    few_core, few_plane, few_rows = refs.few_core, refs.few_plane, refs.few_rows
    few_sem = refs.few_sem
    core_copy = remote(few_ref, few_core, few_sem.at[0, 0], few_sem.at[1, 0], spot.core_peer)
    core_copy.start()
    for item in ups + downs:
        item.steps(5)
    core_copy.wait()
    own_place = spot.col * 2 + spot.wsh
    few_plane[own_place] = few_ref[...] + few_core[...]
    plane_copies = []
    for way, (target, _, _) in enumerate(spot.ways):
        copy = remote(
            few_plane.at[own_place], few_plane.at[own_place],
            few_sem.at[0, 1 + way], few_sem.at[1, 1 + way], target,
        )
        copy.start()
        plane_copies.append(copy)
    piece.cross.steps(3)
    piece.out.steps(3)
    for copy in plane_copies:
        copy.wait()
    few_rows[spot.row] = few_plane[0] + few_plane[1] + few_plane[2] + few_plane[3]
    row_copies = []
    for step in range(1, ROWS):
        copy = remote(
            few_rows.at[spot.row], few_rows.at[spot.row],
            few_sem.at[0, 3 + step], few_sem.at[1, 3 + step], spot.row_peers[step],
        )
        copy.start()
        row_copies.append(copy)
    piece.ckv.steps(3)
    memory_copy.wait()
    g_land[...] = plus(w_up_ref[:, own_side], g_land[...]).astype(LOW)
    for item in ups + downs:
        item.steps(6)

    turned_ref[...] = swap(tokens_ref[...])
    kinds = (piece.wq, piece.wk, piece.wv)
    for kind in range(3):
        back_copy.wait(kind)
        for block in range(own_blocks):
            turned = jnp.concatenate(
                [
                    (pair_land, pair_land, last_land)[kind][
                        h * own_blocks + block, kind % 2 * head : (kind % 2 + 1) * head, :
                    ]
                    for h in range(HEADS)
                ],
                axis=0,
            )
            hidden_ref[kind, block * BLK : (block + 1) * BLK, :] = swap(turned)
        put_rows(kinds[kind], nn(turned_ref[...], hidden_ref[kind]), 0)
        kinds[kind].steps(1)
        if kind > 0:
            kinds[kind - 1].steps(2)
    for item in (piece.cross, piece.out, piece.ckv):
        item.steps(4)
    memory_copies = []
    for step in range(1, ROWS):
        copy = remote(
            g_land.at[pl.ds(spot.rows_by_step[step] * mem_rows, mem_rows)], refs.memory_row.at[step - 1],
            refs.memory_sem.at[0, step], refs.memory_sem.at[1, step], spot.row_peers[step],
        )
        copy.start()
        memory_copies.append(copy)
    grad_stream = total_ref[...]
    for kind in range(3):
        if kind == 1:
            kinds[2].steps(2)
        lanes = slice(kind * width, (kind + 1) * width)
        grad_stream = grad_stream + nt(hidden_ref[kind], refs.w_qkv[:, lanes])
    g_stream_ref[...] = grad_stream
    for item in kinds:
        item.steps(3)
    for copy in row_copies:
        copy.wait()
    total = few_rows[0] + few_rows[1] + few_rows[2] + few_rows[3]
    own_shard = spot.ctx * 2 + spot.wsh
    part, long_part = width // SHARDS, hidden_width // SHARDS
    picked, long_picked = total[:, :part], total[:1, :long_part]
    for shard in range(1, SHARDS):
        picked = jnp.where(own_shard == shard, total[:, shard * part : (shard + 1) * part], picked)
        row, at = divmod(shard * long_part, width)
        long_picked = jnp.where(
            own_shard == shard, total[row : row + 1, at : at + long_part], long_picked
        )
    o_b_up_ref[...] = long_picked
    o_gains_ref[...] = picked[4:7]
    o_biases_ref[...] = picked[7:17]
    for item in (piece.cross, piece.out, piece.ckv):
        item.steps(5)
    for copy in memory_copies:
        copy.wait()
    total = g_land[pl.ds(spot.row * mem_rows, mem_rows), :].astype(WIDE)
    for step in range(ROWS - 1):
        total = total + refs.memory_row[step].astype(WIDE)
    g_memory_ref[...] = total
    for item in kinds + (piece.cross, piece.out, piece.ckv):
        item.steps(6)


def layer_scratch(row_count, width, hidden_width, mem_rows):
    own_blocks = row_count // BLK
    blocks = own_blocks * HEADS
    head = width // HEADS
    tokens = blocks * BLK
    mem_total = mem_rows * HEADS
    dma = pltpu.SemaphoreType.DMA
    scratch = dict(
        w_qkv=((width, 3 * width), LOW), w_ckv=((width, 2 * width), LOW),
        w_out=((width, width), LOW), w_cq=((width, width), LOW),
        w_cout=((width, width), LOW), w_up=((width, hidden_width), LOW),
        w_down=((hidden_width, width), LOW),
        head_send=((HEADS, own_blocks, 3 * head, BLK), LOW),
        pair_land=((blocks, 2 * head, BLK), LOW), last_land=((blocks, head, BLK), LOW),
        memory_all=((2, ROWS, mem_rows, width), LOW),
        q=((tokens, 2 * head), LOW), kv=((tokens, 2 * head), LOW),
        qt=((head, tokens), LOW), kt=((head, tokens), LOW), vt=((head, tokens), LOW),
        exact=((blocks, head, BLK), WIDE), lse=((1, tokens), WIDE),
        mixed_send=((HEADS, own_blocks, head, BLK), LOW),
        mixed_land=((blocks, head, BLK), LOW),
        ck=((mem_total, width), LOW), cv=((mem_total, width), LOW),
        ckt=((width, mem_total), LOW), cvt=((width, mem_total), LOW),
        attended_t=((width, row_count), LOW),
        unit_one=((row_count, width), WIDE), unit_two=((row_count, width), WIDE),
        scale_one=((row_count, 1), WIDE), scale_two=((row_count, 1), WIDE),
        low_one=((row_count, width), LOW), low_two=((row_count, width), LOW),
        cq=((row_count, width), LOW), cqt=((width, row_count), LOW),
        cross_exact=((width, row_count), WIDE),
        cross_lse=((HEADS, 1, row_count), WIDE),
        cross_low=((row_count, width), LOW),
        hidden=((hidden_width // width, row_count, width), LOW),
        slope=((hidden_width // width, row_count, width), LOW),
        low_third=((row_count, width), LOW),
        turned=((width, row_count), LOW),
        dco=((row_count, width), LOW), dcot=((width, row_count), LOW),
        dcqt=((width, row_count), WIDE),
        memory_land=((ROWS * mem_rows, width), LOW),
        memory_row=((ROWS - 1, mem_rows, width), LOW),
        up_land=((blocks, head, BLK), LOW),
        up=((tokens, 2 * head), LOW), upt=((head, tokens), LOW),
        dkv=((blocks, BLK, 2 * head), WIDE), dqt=((blocks, head, BLK), LOW),
        few_sum=((FEW_ROWS, width), WIDE), few_core=((FEW_ROWS, width), WIDE),
        few_plane=((4, FEW_ROWS, width), WIDE), few_rows=((ROWS, FEW_ROWS, width), WIDE),
    )
    out = {name: pltpu.VMEM(shape, kind) for name, (shape, kind) in scratch.items()}
    out.update(
        load_sem=dma((7,)), to_heads_sem=dma((2, HEADS, 4)), from_heads_sem=dma((2, HEADS, 1)),
        up_heads_sem=dma((2, HEADS, 1)), back_sem=dma((2, HEADS, 3)), spread_sem=dma((2, 2 * ROWS)),
        inverse=pltpu.SMEM((blocks,), jnp.int32),
        memory_sem=dma((2, ROWS)), few_sem=dma((2, 7)),
    )
    out.update(
        pieces={
            name: dict(
                part=pltpu.VMEM((2, ROWS, 2, 2, HALF, span), LOW),
                core_land=pltpu.VMEM((ROWS, 2, 2, HALF, span), LOW),
                hop_land=pltpu.VMEM(
                    (3, ROWS, HALF, span) if TURNS[name] == 2 else (ROWS, 2, HALF, span), LOW
                ),
                turn_land=pltpu.VMEM((ROWS, HALF, span), LOW),
                row_land=pltpu.VMEM(
                    (2, ROWS, HALF, span) if TURNS[name] == 2 else (ROWS - 1, HALF, span), LOW
                ),
                sems=dma((2, 12)),
            )
            for name, span in PIECES.items()
        }
    )
    return out


def layer_call(deal_ids, offsets, opened, tokens, memory, cotangent, weights, b_up, gains, biases, prompt_blocks):
    row_count, width = tokens.shape
    hidden_width = b_up.shape[1]
    mem_rows = memory.shape[0]
    smem = pl.BlockSpec(memory_space=pltpu.SMEM)
    vmem = pl.BlockSpec(memory_space=pltpu.VMEM)
    hbm = pl.BlockSpec(memory_space=pl.ANY)
    scratch = layer_scratch(row_count, width, hidden_width, mem_rows)
    leaves, tree = jax.tree.flatten(scratch, is_leaf=lambda leaf: not isinstance(leaf, dict))
    out_shapes = [
        (row_count, width), (row_count, width), (mem_rows, width),
        (32, 3 * width), (32, width), (32, width), (32, 2 * width), (32, width),
        (32, hidden_width), (hidden_width // SHARDS, width),
        (1, hidden_width // SHARDS), (3, width // SHARDS), (10, width // SHARDS),
    ]

    def body(*args):
        count = len(args) - len(leaves)
        refs = Bag(jax.tree.unflatten(tree, args[count:]))
        layer_kernel(prompt_blocks, *args[:count], refs)

    return pl.pallas_call(
        body,
        out_shape=[jax.ShapeDtypeStruct(shape, WIDE) for shape in out_shapes],
        in_specs=[smem] * 3 + [vmem] * 3 + [hbm] * 7 + [vmem] * 3,
        out_specs=[vmem] * len(out_shapes),
        scratch_shapes=leaves,
        compiler_params=pltpu.CompilerParams(
            collective_id=0, has_side_effects=True, vmem_limit_bytes=BIG_VMEM
        ),
        name="layer",
    )(deal_ids, offsets, opened, tokens, memory, cotangent, *weights, b_up, gains, biases)


def hand_out_kernel(count, *refs):
    for index in range(count):
        refs[count + index][...] = refs[index][...]


def hand_out(arrays):
    count = len(arrays)
    vmem = pl.BlockSpec(memory_space=pltpu.VMEM)
    return pl.pallas_call(
        functools.partial(hand_out_kernel, count),
        out_shape=[jax.ShapeDtypeStruct(a.shape, a.dtype) for a in arrays],
        in_specs=[vmem] * count,
        out_specs=[vmem] * count,
        compiler_params=pltpu.CompilerParams(vmem_limit_bytes=BIG_VMEM),
        name="hand_out",
    )(*arrays)


def layer_shards(
    stream, memory, cotangent, deal_order, offsets, context_mask,
    w_qkv, w_out, w_cq, w_ckv, w_cout, w_up, w_down, b_up, gains, biases,
):
    results = layer_call(
        deal_order[0, 0], offsets[0, 0], context_mask[0, 0],
        stream[0, 0], memory[0, 0], cotangent[0, 0],
        (w_qkv, w_out, w_cq, w_ckv, w_cout, w_up, w_down),
        b_up[None, :], gains, biases, context_mask.shape[3],
    )
    output, grad_stream, grad_memory, *grads = hand_out(results)
    grads[7] = grads[7].reshape(-1)
    return (output[None, None], grad_stream[None, None], grad_memory[None, None], *grads)


def gelu_exact(values):
    return jax.nn.gelu(values, approximate=False)


def norm_rows(values, gain_vec, shift_vec):
    center = values - jnp.mean(values, axis=-1, keepdims=True)
    spread = jnp.mean(center * center, axis=-1, keepdims=True)
    return center * lax.rsqrt(spread + EPS_NORM) * gain_vec + shift_vec


def norm_back(values, gain_vec, shift_vec, upstream):
    _, pullback = jax.vjp(norm_rows, values, gain_vec, shift_vec)
    return pullback(upstream)


def seq_index(positions, prompt_len, cont_len):
    later = jnp.int32(1) + (positions - jnp.int32(prompt_len)) // jnp.int32(cont_len)
    return jnp.where(positions < prompt_len, jnp.zeros_like(later), later)


def visible(query_pos, key_ids, offsets, context_mask, block_len, prompt_blocks, cont_blocks):
    prompt_len = prompt_blocks * block_len
    cont_len = cont_blocks * block_len
    cont_count = offsets.shape[0]
    key_pos = (
        key_ids[:, None] * jnp.int32(block_len) + jnp.arange(block_len, dtype=jnp.int32)[None, :]
    ).reshape(-1)
    query_seq = seq_index(query_pos, prompt_len, cont_len)
    key_seq = seq_index(key_pos, prompt_len, cont_len)
    inside = (query_seq[:, None] == key_seq[None, :]) & (key_pos[None, :] <= query_pos[:, None])
    cont_pick = jnp.clip(query_seq - 1, 0, cont_count - 1)
    prompt_limit = jnp.take(offsets, cont_pick)
    query_block = jnp.clip(
        (query_pos - jnp.int32(prompt_len)) // jnp.int32(block_len), 0, cont_count * cont_blocks - 1
    )
    mask_rows = jnp.take(context_mask, query_block, axis=0)
    key_block = jnp.clip(key_ids, 0, prompt_blocks - 1)
    block_open = jnp.take(mask_rows, key_block, axis=1) > 0
    block_open = jnp.repeat(block_open, block_len, axis=1) | (key_pos[None, :] < block_len)
    from_prompt = (
        (query_seq[:, None] > 0)
        & (key_seq[None, :] == 0)
        & (key_pos[None, :] < prompt_limit[:, None])
        & block_open
    )
    return inside | from_prompt


def dot_first(left, right):
    return lax.dot_general(
        left, right, (((0,), (0,)), ((), ())), preferred_element_type=jnp.float32
    )


def dot_last(left, right):
    return lax.dot_general(
        left, right, (((1,), (1,)), ((), ())), preferred_element_type=jnp.float32
    )


def to_heads(matrix, head_count):
    row_count, model_width = matrix.shape
    return matrix.reshape(row_count, head_count, model_width // head_count).transpose(1, 0, 2)


def from_heads(stacked):
    head_count, row_count, head_width = stacked.shape
    return stacked.transpose(1, 0, 2).reshape(row_count, head_count * head_width)


def pair_heads(key_rows, value_rows, head_count):
    return jnp.concatenate(
        [to_heads(key_rows, head_count), to_heads(value_rows, head_count)], axis=2
    )


def head_scores(queries, key_rows, allowed):
    score_scale = queries.shape[1] ** (-0.5)
    scores = dot_last(queries, key_rows) * score_scale
    if allowed is not None:
        scores = jnp.where(allowed, scores, NEG_FILL)
    return scores


def head_forward(queries, keyval, allowed):
    head_width = queries.shape[1]
    scores = head_scores(queries, keyval[:, :head_width], allowed)
    row_top = jnp.max(scores, axis=1, keepdims=True)
    exp_scores = jnp.exp(scores - row_top)
    row_total = jnp.sum(exp_scores, axis=1, keepdims=True)
    soft_weights = (exp_scores / row_total).astype(jnp.bfloat16)
    mixed_heads = jnp.dot(soft_weights, keyval[:, head_width:], preferred_element_type=jnp.float32)
    return (mixed_heads, row_top + jnp.log(row_total))


def head_backward(queries, keyval, upstream, log_total, allowed):
    head_width = queries.shape[1]
    score_scale = head_width ** (-0.5)
    key_rows = keyval[:, :head_width]
    scores = head_scores(queries, key_rows, allowed)
    soft_weights = jnp.exp(scores - log_total)
    grad_soft = dot_last(upstream, keyval[:, head_width:])
    row_delta = jnp.sum(soft_weights * grad_soft, axis=1, keepdims=True)
    grad_scores = (soft_weights * (grad_soft - row_delta)).astype(jnp.bfloat16)
    grad_query = jnp.dot(grad_scores, key_rows, preferred_element_type=jnp.float32) * score_scale
    grad_keys = dot_first(grad_scores, queries) * score_scale
    grad_values = dot_first(soft_weights.astype(jnp.bfloat16), upstream)
    return (grad_query, jnp.concatenate([grad_keys, grad_values], axis=1))


def shards(
    stream,
    memory,
    cotangent,
    deal_order,
    offsets,
    context_mask,
    w_qkv,
    w_out,
    w_cq,
    w_ckv,
    w_cout,
    w_up,
    w_down,
    b_up,
    gains,
    biases,
):
    tokens = stream[0, 0]
    row_count, model_width = tokens.shape
    head_width = model_width // HEADS
    deal_ids = deal_order[0, 0]
    prompt_blocks = context_mask.shape[3]
    own_blocks = row_count // BLK
    own_ids = lax.dynamic_slice_in_dim(deal_ids, lax.axis_index("ctx") * own_blocks, own_blocks)
    query_pos = (
        own_ids[:, None] * jnp.int32(BLK) + jnp.arange(BLK, dtype=jnp.int32)[None, :]
    ).reshape(-1)
    allowed = visible(
        query_pos, deal_ids, offsets[0, 0], context_mask[0, 0], BLK, prompt_blocks, CBLK
    )
    zeros_row = jnp.zeros((model_width,), jnp.float32)
    projected = (
        jnp.dot(tokens, w_qkv, preferred_element_type=jnp.float32)
        + jnp.concatenate([biases[0], zeros_row, biases[1]])
    ).astype(jnp.bfloat16)
    query_heads = to_heads(projected[:, :model_width], HEADS)
    keyval_own = pair_heads(
        projected[:, model_width : 2 * model_width], projected[:, 2 * model_width :], HEADS
    )
    keyval_all = lax.all_gather(keyval_own, "ctx", axis=1, tiled=True)

    def self_forward(pieces):
        return head_forward(pieces[0], pieces[1], allowed)

    self_out, self_lse = lax.map(self_forward, (query_heads, keyval_all))
    attended = from_heads(self_out).astype(jnp.bfloat16)
    first_sum = (
        tokens.astype(jnp.float32)
        + jnp.dot(attended, w_out, preferred_element_type=jnp.float32)
        + biases[2]
    )
    normed_one = norm_rows(first_sum, gains[0], biases[3])
    normed_low = normed_one.astype(jnp.bfloat16)
    cross_query = (
        jnp.dot(normed_low, w_cq, preferred_element_type=jnp.float32) + biases[4]
    ).astype(jnp.bfloat16)
    cross_bias = jnp.concatenate([zeros_row, biases[5]])
    memory_own = memory[0, 0]
    memory_all = lax.all_gather(memory_own, "ctx", axis=0, tiled=True)
    cross_kv = (jnp.dot(memory_all, w_ckv, preferred_element_type=jnp.float32) + cross_bias).astype(
        jnp.bfloat16
    )
    cross_heads = pair_heads(cross_kv[:, :model_width], cross_kv[:, model_width:], HEADS)
    cross_query_heads = to_heads(cross_query, HEADS)

    def cross_forward(pieces):
        return head_forward(pieces[0], pieces[1], None)

    cross_out, cross_lse = lax.map(cross_forward, (cross_query_heads, cross_heads))
    cross_attended = from_heads(cross_out).astype(jnp.bfloat16)
    second_sum = (
        normed_one + jnp.dot(cross_attended, w_cout, preferred_element_type=jnp.float32) + biases[6]
    )
    normed_two = norm_rows(second_sum, gains[1], biases[7])
    normed_two_low = normed_two.astype(jnp.bfloat16)
    hidden_pre = jnp.dot(normed_two_low, w_up, preferred_element_type=jnp.float32) + b_up
    hidden = gelu_exact(hidden_pre).astype(jnp.bfloat16)
    third_sum = normed_two + jnp.dot(hidden, w_down, preferred_element_type=jnp.float32) + biases[8]
    output = norm_rows(third_sum, gains[2], biases[9])
    grad_third, grad_gain_three, grad_shift_three = norm_back(
        third_sum, gains[2], biases[9], cotangent[0, 0].astype(jnp.float32)
    )
    grad_down_in = grad_third.astype(jnp.bfloat16)
    grad_w_down = dot_first(hidden, grad_down_in)
    grad_b_down = jnp.sum(grad_down_in.astype(jnp.float32), axis=0)
    grad_hidden = dot_last(grad_down_in, w_down)
    _, gelu_pull = jax.vjp(gelu_exact, hidden_pre)
    grad_pre = gelu_pull(grad_hidden)[0].astype(jnp.bfloat16)
    grad_w_up = dot_first(normed_two_low, grad_pre)
    grad_b_up = jnp.sum(grad_pre.astype(jnp.float32), axis=0)
    grad_normed_two = grad_third + dot_last(grad_pre, w_up)
    grad_second, grad_gain_two, grad_shift_two = norm_back(
        second_sum, gains[1], biases[7], grad_normed_two
    )
    grad_cross_in = grad_second.astype(jnp.bfloat16)
    grad_w_cout = dot_first(cross_attended, grad_cross_in)
    grad_b_co = jnp.sum(grad_cross_in.astype(jnp.float32), axis=0)
    grad_cross_heads = to_heads(dot_last(grad_cross_in, w_cout).astype(jnp.bfloat16), HEADS)

    def cross_backward(pieces):
        return head_backward(pieces[0], pieces[1], pieces[2], pieces[3], None)

    grad_cq_heads, grad_ckv_all = lax.map(
        cross_backward, (cross_query_heads, cross_heads, grad_cross_heads, cross_lse)
    )
    grad_ckv_own = lax.psum_scatter(
        grad_ckv_all.astype(jnp.bfloat16), "ctx", scatter_dimension=1, tiled=True
    )
    grad_cv = from_heads(grad_ckv_own[:, :, head_width:])
    grad_ckv = jnp.concatenate([from_heads(grad_ckv_own[:, :, :head_width]), grad_cv], axis=1)
    grad_w_ckv = dot_first(memory_own, grad_ckv)
    grad_b_cv = jnp.sum(grad_cv.astype(jnp.float32), axis=0)
    grad_memory = dot_last(grad_ckv, w_ckv)
    grad_cq = from_heads(grad_cq_heads).astype(jnp.bfloat16)
    grad_w_cq = dot_first(normed_low, grad_cq)
    grad_b_cq = jnp.sum(grad_cq.astype(jnp.float32), axis=0)
    grad_normed_one = grad_second + dot_last(grad_cq, w_cq)
    grad_first, grad_gain_one, grad_shift_one = norm_back(
        first_sum, gains[0], biases[3], grad_normed_one
    )
    grad_att_in = grad_first.astype(jnp.bfloat16)
    grad_w_out = dot_first(attended, grad_att_in)
    grad_b_o = jnp.sum(grad_att_in.astype(jnp.float32), axis=0)
    grad_self_heads = to_heads(dot_last(grad_att_in, w_out).astype(jnp.bfloat16), HEADS)

    def self_backward(pieces):
        return head_backward(pieces[0], pieces[1], pieces[2], pieces[3], allowed)

    grad_q_heads, grad_kv_all = lax.map(
        self_backward, (query_heads, keyval_all, grad_self_heads, self_lse)
    )
    grad_kv_own = lax.psum_scatter(
        grad_kv_all.astype(jnp.bfloat16), "ctx", scatter_dimension=1, tiled=True
    )
    grad_values = from_heads(grad_kv_own[:, :, head_width:])
    grad_queries = from_heads(grad_q_heads).astype(jnp.bfloat16)
    grad_proj = jnp.concatenate(
        [grad_queries, from_heads(grad_kv_own[:, :, :head_width]), grad_values], axis=1
    )
    grad_w_qkv = dot_first(tokens, grad_proj)
    grad_b_q = jnp.sum(grad_queries.astype(jnp.float32), axis=0)
    grad_b_v = jnp.sum(grad_values.astype(jnp.float32), axis=0)
    grad_tokens = grad_first + dot_last(grad_proj, w_qkv)
    gain_grads = jnp.stack([grad_gain_one, grad_gain_two, grad_gain_three])
    shift_grads = jnp.stack(
        [
            grad_b_q,
            grad_b_v,
            grad_b_o,
            grad_shift_one,
            grad_b_cq,
            grad_b_cv,
            grad_b_co,
            grad_shift_two,
            grad_b_down,
            grad_shift_three,
        ]
    )
    (
        part_qkv,
        part_out,
        part_cq,
        part_ckv,
        part_cout,
        part_up,
        part_down,
        part_b_up,
        part_gains,
        part_biases,
    ) = (
        lax.psum_scatter(grad_w_qkv, ("ctx", "wsh"), scatter_dimension=0, tiled=True),
        lax.psum_scatter(grad_w_out, ("ctx", "wsh"), scatter_dimension=0, tiled=True),
        lax.psum_scatter(grad_w_cq, ("ctx", "wsh"), scatter_dimension=0, tiled=True),
        lax.psum_scatter(grad_w_ckv, ("ctx", "wsh"), scatter_dimension=0, tiled=True),
        lax.psum_scatter(grad_w_cout, ("ctx", "wsh"), scatter_dimension=0, tiled=True),
        lax.psum_scatter(grad_w_up, ("ctx", "wsh"), scatter_dimension=0, tiled=True),
        lax.psum_scatter(grad_w_down, ("ctx", "wsh"), scatter_dimension=0, tiled=True),
        lax.psum_scatter(grad_b_up, ("ctx", "wsh"), scatter_dimension=0, tiled=True),
        lax.psum_scatter(gain_grads, ("ctx", "wsh"), scatter_dimension=1, tiled=True),
        lax.psum_scatter(shift_grads, ("ctx", "wsh"), scatter_dimension=1, tiled=True),
    )
    (
        total_qkv,
        total_out,
        total_cq,
        total_ckv,
        total_cout,
        total_up,
        total_down,
        total_b_up,
        total_gains,
        total_biases,
    ) = (
        lax.psum(part_qkv.astype(jnp.bfloat16), "grp").astype(jnp.float32),
        lax.psum(part_out.astype(jnp.bfloat16), "grp").astype(jnp.float32),
        lax.psum(part_cq.astype(jnp.bfloat16), "grp").astype(jnp.float32),
        lax.psum(part_ckv.astype(jnp.bfloat16), "grp").astype(jnp.float32),
        lax.psum(part_cout.astype(jnp.bfloat16), "grp").astype(jnp.float32),
        lax.psum(part_up.astype(jnp.bfloat16), "grp").astype(jnp.float32),
        lax.psum(part_down.astype(jnp.bfloat16), "grp").astype(jnp.float32),
        lax.psum(part_b_up.astype(jnp.bfloat16), "grp").astype(jnp.float32),
        lax.psum(part_gains.astype(jnp.bfloat16), "grp").astype(jnp.float32),
        lax.psum(part_biases.astype(jnp.bfloat16), "grp").astype(jnp.float32),
    )
    return (
        output[None, None],
        grad_tokens[None, None],
        grad_memory[None, None],
        total_qkv,
        total_out,
        total_cq,
        total_ckv,
        total_cout,
        total_up,
        total_down,
        total_b_up,
        total_gains,
        total_biases,
    )


def solution(mesh):
    in_specs = (
        P("grp", "wsh", "ctx", None),
        P("grp", "wsh", "ctx", None),
        P("grp", "wsh", "ctx", None),
        P("grp", "wsh", None),
        P("grp", "wsh", None),
        P("grp", "wsh", None, None),
        P(),
        P(),
        P(),
        P(),
        P(),
        P(),
        P(),
        P(),
        P(),
        P(),
    )
    out_specs = (
        P("grp", "wsh", "ctx", None),
        P("grp", "wsh", "ctx", None),
        P("grp", "wsh", "ctx", None),
        P(("ctx", "wsh"), None),
        P(("ctx", "wsh"), None),
        P(("ctx", "wsh"), None),
        P(("ctx", "wsh"), None),
        P(("ctx", "wsh"), None),
        P(("ctx", "wsh"), None),
        P(("ctx", "wsh"), None),
        P(("ctx", "wsh")),
        P(None, ("ctx", "wsh")),
        P(None, ("ctx", "wsh")),
    )
    body = layer_shards if mesh.shape["ctx"] == HEADS else shards
    return jax.shard_map(body, mesh=mesh, in_specs=in_specs, out_specs=out_specs, check_vma=False)
```

```python
import functools

import jax
import jax.numpy as jnp
from jax import lax
from jax.experimental import pallas as pl
from jax.experimental.pallas import tpu as pltpu
from jax.sharding import PartitionSpec as P

HEADS = 8
BLK = 128
CBLK = 16


NEG_FILL = -1000000000.0
EPS_NORM = 1e-05


MESH_ID = pl.DeviceIdType.MESH
TILE = 512
STEP = 512
KEYS = 1024
BIG_VMEM = 62 << 20
LOW = jnp.bfloat16
WIDE = jnp.float32
SHARDS = 16
HALF = 16
ROWS = 4
PIECES = dict(
    up0=1024, up1=1024, down0=1024, down1=1024, cross=1024, out=512, ckv=1024, wq=512, wk=512, wv=512
)
TURNS = dict(up0=0, up1=1, down0=0, down1=1, cross=0, out=0, ckv=0, wq=2, wk=2, wv=2)
FEW_ROWS = 24


def nn(left, right):
    return lax.dot_general(
        left, right, (((1,), (0,)), ((), ())), preferred_element_type=WIDE
    )


def nt(left, right):
    return lax.dot_general(
        left, right, (((1,), (1,)), ((), ())), preferred_element_type=WIDE
    )


def swap(block):
    return block.astype(WIDE).T.astype(block.dtype)


def plus(left, right):
    return left.astype(WIDE) + right.astype(WIDE)


def column_sums(values):
    return jnp.sum(values.astype(WIDE), axis=0, keepdims=True)


def norm_parts(values):
    center = values - jnp.mean(values, axis=-1, keepdims=True)
    spread = jnp.mean(center * center, axis=-1, keepdims=True)
    scale = lax.rsqrt(spread + EPS_NORM)
    return center * scale, scale


def norm_pull(unit, scale, gain, upstream):
    inner = upstream * gain
    first = jnp.mean(inner, axis=-1, keepdims=True)
    second = jnp.mean(inner * unit, axis=-1, keepdims=True)
    return scale * (inner - first - unit * second)


def hide_later(scores, lead):
    rows = lax.broadcasted_iota(jnp.int32, scores.shape, 0)
    cols = lax.broadcasted_iota(jnp.int32, scores.shape, 1)
    return jnp.where(rows - cols <= lead, scores, NEG_FILL)


def hide_prompt(scores, offset_ref, open_ref, tile, chunk, prompt_blocks):
    span, key_span = TILE // BLK, scores.shape[0] // BLK
    rows = lax.broadcasted_iota(jnp.int32, (BLK, BLK), 0)
    columns = []
    for q_sub in range(span):
        pieces = []
        for k_sub in range(key_span):
            key_block = chunk * key_span + k_sub
            opened = open_ref[tile * span + q_sub - prompt_blocks, key_block]
            opened = jnp.where(key_block == 0, 1, opened)
            limit = jnp.where(opened > 0, offset_ref[0], 0) - key_block * BLK
            part = scores[k_sub * BLK : (k_sub + 1) * BLK, q_sub * BLK : (q_sub + 1) * BLK]
            pieces.append(jnp.where(rows < limit, part, NEG_FILL))
        columns.append(jnp.concatenate(pieces, axis=0))
    return jnp.concatenate(columns, axis=1)


def apart(upper, lower):
    none = jnp.zeros_like(upper)
    return jnp.concatenate(
        [jnp.concatenate([upper, none], axis=1), jnp.concatenate([none, lower], axis=1)], axis=0
    )


def apart_columns(pair):
    lanes = lax.broadcasted_iota(jnp.int32, pair.shape, 1)
    wide = pair.astype(WIDE)
    left = jnp.where(lanes < pair.shape[1] // 2, wide, 0.0).astype(pair.dtype)
    right = jnp.where(lanes < pair.shape[1] // 2, 0.0, wide).astype(pair.dtype)
    return jnp.concatenate([left, right], axis=0)


def remote(src_ref, dst_ref, send_sem, recv_sem, target):
    return pltpu.make_async_remote_copy(
        src_ref=src_ref,
        dst_ref=dst_ref,
        send_sem=send_sem,
        recv_sem=recv_sem,
        device_id=target,
        device_id_type=MESH_ID,
    )


class Bag:
    def __init__(self, items):
        self.__dict__.update(items)


class Spot:
    def __init__(self):
        ctx = lax.axis_index("ctx")
        self.grp, self.ctx, self.wsh = lax.axis_index("grp"), ctx, lax.axis_index("wsh")
        self.row, self.col = ctx // 2, lax.rem(ctx, 2)
        self.core_peer = (1 - self.grp, ctx, self.wsh)
        self.wsh_peer = (self.grp, ctx, 1 - self.wsh)
        self.col_peer = self.at_row_col(self.row, 1 - self.col)
        self.cross_peer = (self.grp, self.row * 2 + 1 - self.col, 1 - self.wsh)
        self.rows_by_step = [lax.rem(self.row + step, ROWS) for step in range(ROWS)]
        self.row_peers = [self.at_row_col(row, self.col) for row in self.rows_by_step]
        self.far_peers = [(1 - self.grp, peer[1], self.wsh) for peer in self.row_peers]
        self.ways = [
            (self.wsh_peer, self.col, 1 - self.wsh),
            (self.col_peer, 1 - self.col, self.wsh),
            (self.cross_peer, 1 - self.col, 1 - self.wsh),
        ]
        self.ctx_by_step = [lax.rem(ctx + step, HEADS) for step in range(HEADS)]
        self.ctx_peers = [(self.grp, peer, self.wsh) for peer in self.ctx_by_step]

    def at_row_col(self, row, col):
        return (self.grp, row * 2 + col, self.wsh)

    def greet(self):
        barrier = pltpu.get_barrier_semaphore()
        targets = [self.core_peer, self.wsh_peer, self.cross_peer]
        targets += self.ctx_peers[1:] + self.far_peers[1:]
        for target in targets:
            pl.semaphore_signal(barrier, inc=1, device_id=target, device_id_type=MESH_ID)
        return len(targets)


class Exchange:
    def __init__(self, spot, source, sems, parts):
        self.spot, self.source, self.sems, self.parts = spot, source, sems, parts
        self.copies = [[] for _ in parts]

    def start(self, part=0):
        spot, own_blocks = self.spot, self.source.shape[1]
        first, count, rows, target, target_rows = self.parts[part]
        here = (pl.ds(spot.ctx * own_blocks + first, count), target_rows)
        there = (pl.ds(first, count), rows)
        for step in range(1, HEADS):
            copy = remote(
                self.source.at[(spot.ctx_by_step[step],) + there], target.at[here],
                self.sems.at[0, step, part], self.sems.at[1, step, part], spot.ctx_peers[step],
            )
            copy.start()
            self.copies[part].append(copy)
        target[here] = self.source[(spot.ctx,) + there]

    def wait(self, part=0):
        for copy in self.copies[part]:
            copy.wait()


class Piece:
    def __init__(self, spot, turn, refs, outs):
        self.spot, self.turn, self.sems, self.outs = spot, turn, refs.sems, outs
        self.part, self.core_land, self.hop_land = refs.part, refs.core_land, refs.hop_land
        self.turn_land, self.row_land = refs.turn_land, refs.row_land
        self.turn_sum = self.core_land.at[:, 0]
        self.copies = []
        self.stage = 0

    def copy(self, index, source, target_ref, target):
        copy = remote(source, target_ref, self.sems.at[0, index], self.sems.at[1, index], target)
        copy.start()
        self.copies.append(copy)

    def finish(self):
        for copy in self.copies:
            copy.wait()
        self.copies = []

    def send_rows(self):
        spot = self.spot
        for step in range(1, ROWS):
            self.copy(
                2 + step, self.turn_land.at[spot.rows_by_step[step]],
                self.row_land.at[step - 1], spot.row_peers[step],
            )

    def steps(self, stage):
        while self.stage < stage:
            self.step()

    def step(self):
        spot, part = self.spot, self.part
        own = spot.grp
        if self.stage == 0:
            self.copy(0, part.at[1 - own], self.core_land, spot.core_peer)
        elif self.stage == 1:
            self.finish()
            part[own] = plus(part[own], self.core_land[...]).astype(LOW)
            if self.turn == 2:
                for way, (target, to_col, to_wsh) in enumerate(spot.ways):
                    self.copy(
                        1 + way, part.at[own, :, to_col, to_wsh], self.hop_land.at[way],
                        target,
                    )
            elif self.turn == 0:
                self.copy(1, part.at[own, :, :, 1 - spot.wsh], self.hop_land, spot.wsh_peer)
            else:
                self.copy(1, part.at[own, :, 1 - spot.col], self.hop_land, spot.col_peer)
        elif self.stage == 2:
            self.finish()
            if self.turn == 2:
                total = part[own, :, spot.col, spot.wsh].astype(WIDE)
                for way in range(3):
                    total = total + self.hop_land[way].astype(WIDE)
                self.turn_land[...] = total.astype(LOW)
                self.row_land[own, spot.row] = self.turn_land[spot.row]
                for step in range(ROWS):
                    for side, peers in enumerate((spot.row_peers, spot.far_peers)):
                        if step + side > 0:
                            self.copy(
                                4 + 2 * step + side, self.turn_land.at[spot.rows_by_step[step]],
                                self.row_land.at[own, spot.row], peers[step],
                            )
                self.stage = 4
                return
            if self.turn == 0:
                mine = part[own, :, :, spot.wsh]
                away, target = 1 - spot.col, spot.col_peer
            else:
                mine = part[own, :, spot.col]
                away, target = 1 - spot.wsh, spot.wsh_peer
            self.turn_sum[...] = plus(mine, self.hop_land[...]).astype(LOW)
            self.copy(2, self.turn_sum.at[:, away], self.turn_land, target)
        elif self.stage == 3:
            self.finish()
            keep = spot.col if self.turn == 0 else spot.wsh
            self.turn_land[...] = plus(self.turn_sum[:, keep], self.turn_land[...]).astype(LOW)
            self.send_rows()
        elif self.stage == 4:
            self.finish()
            if self.turn == 2:
                (out_ref, _, column, width), = self.outs
                for half in range(2):
                    total = self.row_land[half, 0].astype(WIDE)
                    for row in range(1, ROWS):
                        total = total + self.row_land[half, row].astype(WIDE)
                    out_ref[half * HALF : (half + 1) * HALF, column : column + width] = total
                self.stage = 6
                return
            total = self.turn_land[spot.row].astype(WIDE)
            for step in range(ROWS - 1):
                total = total + self.row_land[step].astype(WIDE)
            at = 0
            for index, (out_ref, row, column, width) in enumerate(self.outs):
                here = (
                    pl.ds(pl.multiple_of(row + own * HALF, HALF), HALF),
                    slice(column, column + width),
                )
                out_ref[here] = total[:, at : at + width]
                at += width
                self.copy(7 + index, out_ref.at[here], out_ref.at[here], spot.core_peer)
        elif self.stage == 5:
            self.finish()
        self.stage += 1


def layer_kernel(
    prompt_blocks,
    deal_ref, offset_ref, open_ref, tokens_ref, memory_ref, cot_ref,
    w_qkv_hbm, w_out_hbm, w_cq_hbm, w_ckv_hbm, w_cout_hbm, w_up_hbm, w_down_hbm,
    b_up_ref, gains_ref, biases_ref,
    output_ref, g_stream_ref, g_memory_ref, o_qkv_ref, o_out_ref, o_cq_ref, o_ckv_ref, o_cout_ref,
    o_up_ref, o_down_ref, o_b_up_ref, o_gains_ref, o_biases_ref,
    refs,
):
    spot = Spot()
    greeted = spot.greet()
    row_count, width = tokens_ref.shape
    own_blocks = row_count // BLK
    head = width // HEADS
    blocks = own_blocks * HEADS
    mem_rows = memory_ref.shape[0]
    mem_total = mem_rows * HEADS
    hidden_width = b_up_ref.shape[1]
    chunks = hidden_width // width
    pairs = HEADS // 2
    score_scale = head ** (-0.5)
    prompt_tiles = prompt_blocks * BLK // TILE
    tiles = blocks * BLK // TILE

    sources = dict(
        w_qkv=w_qkv_hbm, w_ckv=w_ckv_hbm, w_out=w_out_hbm, w_cq=w_cq_hbm, w_cout=w_cout_hbm,
        w_up=w_up_hbm, w_down=w_down_hbm,
    )
    loads = Bag(
        {
            name: pltpu.make_async_copy(source, getattr(refs, name), refs.load_sem.at[index])
            for index, (name, source) in enumerate(sources.items())
        }
    )
    for name in sources:
        getattr(loads, name).start()

    outs = dict(
        up0=[(o_up_ref, 0, 0, 1024)],
        up1=[(o_up_ref, 0, 1024, 1024)],
        down0=[(o_down_ref, 0, 0, 512), (o_down_ref, 32, 0, 512)],
        down1=[(o_down_ref, 64, 0, 512), (o_down_ref, 96, 0, 512)],
        cross=[(o_cout_ref, 0, 0, 512), (o_cq_ref, 0, 0, 512)],
        out=[(o_out_ref, 0, 0, 512)],
        ckv=[(o_ckv_ref, 0, 0, 1024)],
        wq=[(o_qkv_ref, 0, 0, 512)],
        wk=[(o_qkv_ref, 0, 512, 512)],
        wv=[(o_qkv_ref, 0, 1024, 512)],
    )
    piece = Bag(
        {
            name: Piece(spot, TURNS[name], Bag(refs.pieces[name]), outs[name])
            for name in PIECES
        }
    )
    ups, downs = (piece.up0, piece.up1), (piece.down0, piece.down1)

    def put_rows(to, values, column):
        span = values.shape[1]
        split = values.astype(LOW).reshape(ROWS, 2, 2, 2, HALF, span)
        for half in range(2):
            to.part[half, :, :, :, :, column : column + span] = split[:, :, :, half]

    few_ref = refs.few_sum
    few_ref[...] = jnp.zeros_like(few_ref)

    def few(row, values):
        few_ref[row : row + 1, :] = values

    def gain(row):
        return gains_ref[row : row + 1, :]

    def bias(row):
        return biases_ref[row : row + 1, :]

    send_ref = refs.head_send
    loads.w_qkv.wait()
    zeros_row = jnp.zeros((1, width), WIDE)
    pair_rows, last_rows = slice(0, 2 * head), slice(2 * head, 3 * head)
    pair_land, last_land = refs.pair_land, refs.last_land
    to_heads_copy = Exchange(
        spot, send_ref, refs.to_heads_sem,
        [(block, 1, pair_rows, pair_land, pair_rows) for block in range(own_blocks)]
        + [(0, own_blocks, last_rows, last_land, slice(0, head))],
    )
    pair_bias = jnp.concatenate([bias(0), zeros_row], axis=1)
    for block in range(own_blocks):
        rows = slice(block * BLK, (block + 1) * BLK)
        projected = (nn(tokens_ref[rows, :], refs.w_qkv[:, : 2 * width]) + pair_bias).astype(LOW)
        turned = projected.astype(WIDE).T
        turned = jnp.concatenate([turned[:width] * score_scale, turned[width:]], axis=0).astype(LOW)
        for h in range(HEADS):
            for kind in range(2):
                at = kind * width + h * head
                send_ref[h, block, kind * head : (kind + 1) * head, :] = turned[at : at + head]
        if block == 0:
            pl.semaphore_wait(pltpu.get_barrier_semaphore(), greeted)
        to_heads_copy.start(block)
    for block in range(own_blocks):
        rows = slice(block * BLK, (block + 1) * BLK)
        turned = swap((nn(tokens_ref[rows, :], refs.w_qkv[:, 2 * width :]) + bias(1)).astype(LOW))
        for h in range(HEADS):
            send_ref[h, block, last_rows, :] = turned[h * head : (h + 1) * head]
    to_heads_copy.start(own_blocks)
    all_ref = refs.memory_all
    all_ref[spot.col, spot.row] = memory_ref[...]

    def pass_on(step):
        row = lax.rem(spot.row + ROWS - step, ROWS)
        copy = remote(
            all_ref.at[spot.col, row], all_ref.at[spot.col, row],
            refs.spread_sem.at[0, ROWS + step], refs.spread_sem.at[1, ROWS + step], spot.col_peer,
        )
        copy.start()
        return copy

    passed = [pass_on(0)]
    inv_ref = refs.inverse
    for pos in range(blocks):
        row = jnp.int32(0)
        for other in range(1, blocks):
            row = jnp.where(deal_ref[other] == pos, other, row)
        inv_ref[pos] = row
    for block in range(own_blocks):
        to_heads_copy.wait(block)

    q_ref, kv_ref = refs.q, refs.kv
    no_head = jnp.zeros((head, BLK), LOW)
    no_tile = jnp.zeros((head, TILE), LOW)
    qt_ref, kt_ref, vt_ref = refs.qt, refs.kt, refs.vt
    exact_ref, lse_ref = refs.exact, refs.lse
    for pos in range(blocks):
        block = pair_land[inv_ref[pos]]
        at = slice(pos * BLK, (pos + 1) * BLK)
        qt_ref[:, at] = block[:head]
        kt_ref[:, at] = block[head:]
        kv_ref[at, :] = swap(jnp.concatenate([block[head:], no_head], axis=0))

    prompt_chunks = prompt_blocks * BLK // KEYS
    group = KEYS // TILE

    def key_spans(chunk, tile, step, state):
        base = 0 if chunk < prompt_chunks else prompt_chunks
        lead = tile * TILE - chunk * KEYS
        state = step(chunk, state, lambda s, c: hide_later(s, lead))
        for other in range(base, chunk):
            state = step(other, state, lambda s, c: s)
        for other in range(base):
            state = step(
                other,
                state,
                lambda s, c: hide_prompt(s, offset_ref, open_ref, tile, c, prompt_blocks),
            )
        return state

    def top_tile(chunk, tile):
        here = pl.ds(pl.multiple_of(tile * TILE, TILE), TILE)
        queries = jnp.concatenate([qt_ref[:, here], no_tile], axis=0)

        def top_step(other, top, hide):
            scores = nn(kv_ref[other * KEYS : (other + 1) * KEYS, :], queries)
            scores = hide(scores, other).reshape(KEYS // 8, 8, TILE)
            return jnp.maximum(top, jnp.max(scores, axis=0))

        top = key_spans(chunk, tile, top_step, jnp.full((8, TILE), NEG_FILL, WIDE))
        lse_ref[:, here] = jnp.max(top, axis=0, keepdims=True)

    def each_tile(chunk, step):
        def body(tile, carry):
            step(chunk, tile)
            return carry

        lax.fori_loop(chunk * group, (chunk + 1) * group, body, 0)

    for chunk in range(tiles // group):
        each_tile(chunk, top_tile)
    to_heads_copy.wait(own_blocks)
    spread = []
    for step in range(1, ROWS):
        copy = remote(
            memory_ref, all_ref.at[spot.col, spot.row],
            refs.spread_sem.at[0, step], refs.spread_sem.at[1, step], spot.row_peers[step],
        )
        copy.start()
        spread.append(copy)
    for pos in range(blocks):
        vt_ref[:, pos * BLK : (pos + 1) * BLK] = last_land[inv_ref[pos]]

    def tile_spans(tile, chunk_step, state):
        state = chunk_step(tile, state, lambda s, c: hide_later(s, 0))
        first = jnp.where(tile >= prompt_tiles, prompt_tiles, 0)
        state = lax.fori_loop(first, tile, lambda c, s: chunk_step(c, s, lambda x, _: x), state)
        return lax.fori_loop(
            0,
            first,
            lambda c, s: chunk_step(
                c, s, lambda x, cc: hide_prompt(x, offset_ref, open_ref, tile, cc, prompt_blocks)
            ),
            state,
        )

    def mix_tile(chunk, tile):
        here = pl.ds(pl.multiple_of(tile * TILE, TILE), TILE)
        queries = jnp.concatenate([qt_ref[:, here], no_tile], axis=0)
        top = lse_ref[:, here]

        def mix_step(other, state, hide):
            total, mixed = state
            there = slice(other * KEYS, (other + 1) * KEYS)
            weights = jnp.exp(hide(nn(kv_ref[there, :], queries), other) - top)
            total = total + jnp.sum(weights.reshape(KEYS // 8, 8, TILE), axis=0)
            return total, mixed + nn(vt_ref[:, there], weights.astype(LOW))

        total, mixed = key_spans(
            chunk, tile, mix_step, (jnp.zeros((8, TILE), WIDE), jnp.zeros((head, TILE), WIDE))
        )
        total = jnp.sum(total, axis=0, keepdims=True)
        exact = mixed / total
        for sub in range(TILE // BLK):
            exact_ref[tile * (TILE // BLK) + sub] = exact[:, sub * BLK : (sub + 1) * BLK]
        lse_ref[:, here] = top + jnp.log(total)

    for chunk in range(tiles // group):
        if chunk == tiles // group - 1:
            spread[0].wait()
            passed.append(pass_on(1))
        each_tile(chunk, mix_tile)
    for step in range(2, ROWS):
        spread[step - 1].wait()
        passed.append(pass_on(step))
    mixed_ref = refs.mixed_send
    for row in range(blocks):
        mixed_ref[row // own_blocks, row % own_blocks] = exact_ref[deal_ref[row]].astype(LOW)
    all_rows = slice(0, head)
    from_heads_copy = Exchange(
        spot, mixed_ref, refs.from_heads_sem,
        [(0, own_blocks, all_rows, refs.mixed_land, all_rows)],
    )
    from_heads_copy.start()

    for pos in range(blocks):
        at = slice(pos * BLK, (pos + 1) * BLK)
        kv_ref[at, :] = swap(jnp.concatenate([kt_ref[:, at], vt_ref[:, at]], axis=0))

    ck_ref, cv_ref, ckt_ref, cvt_ref = refs.ck, refs.cv, refs.ckt, refs.cvt
    loads.w_ckv.wait()

    def encode(col, row):
        rows = pl.ds(pl.multiple_of((row * 2 + col) * mem_rows, mem_rows), mem_rows)
        both = nn(all_ref[col, row], refs.w_ckv[...])
        keys = both[:, :width].astype(LOW)
        values = (both[:, width:] + bias(5)).astype(LOW)
        ck_ref[rows, :] = keys
        cv_ref[rows, :] = values
        ckt_ref[:, rows] = swap(keys)
        cvt_ref[:, rows] = swap(values)

    for row in range(ROWS):
        encode(spot.col, row)
    for copy in passed:
        copy.wait()
    for row in range(ROWS):
        encode(1 - spot.col, row)

    loads.w_out.wait()
    from_heads_copy.wait()
    attended_t_ref = refs.attended_t
    unit_one_ref, unit_two_ref = refs.unit_one, refs.unit_two
    low_one_ref, low_two_ref = refs.low_one, refs.low_two
    for block in range(own_blocks):
        at = slice(block * BLK, (block + 1) * BLK)
        for h in range(HEADS):
            attended_t_ref[h * head : (h + 1) * head, at] = refs.mixed_land[h * own_blocks + block]
    cq_ref, cqt_ref = refs.cq, refs.cqt
    loads.w_cq.wait()

    def rows_at(block):
        return pl.ds(pl.multiple_of(block * BLK, BLK), BLK)

    def first_norm(block, carry):
        rows = rows_at(block)
        attended = swap(attended_t_ref[:, rows])
        first_sum = tokens_ref[rows, :].astype(WIDE) + nn(attended, refs.w_out[...]) + bias(2)
        unit, scale = norm_parts(first_sum)
        unit_one_ref[rows, :] = unit
        refs.scale_one[rows, :] = scale
        low_one = (unit * gain(0) + bias(3)).astype(LOW)
        low_one_ref[rows, :] = low_one
        cross_query = (nn(low_one, refs.w_cq[...]) + bias(4)).astype(LOW).astype(WIDE)
        cross_query = cross_query * score_scale
        cq_ref[rows, :] = cross_query.astype(LOW)
        cqt_ref[:, rows] = cross_query.T.astype(LOW)
        return carry

    lax.fori_loop(0, own_blocks, first_norm, 0)

    pair_width = 2 * head
    cross_exact_ref, cross_lse_ref = refs.cross_exact, refs.cross_lse
    steps = mem_total // STEP

    def pair_at(pair):
        return pl.ds(pl.multiple_of(pair * pair_width, pair_width), pair_width)

    def step_at(step):
        return pl.ds(pl.multiple_of(step * STEP, STEP), STEP)

    def cross_forward(h, carry):
        lanes = pair_at(h // 2)
        at = pl.ds(pl.multiple_of(h * head, head), head)
        own_rows = lax.broadcasted_iota(jnp.int32, (pair_width, row_count), 0) // head
        queries = jnp.where(own_rows == lax.rem(h, 2), cqt_ref[lanes, :].astype(WIDE), 0.0)
        queries = queries.astype(LOW)

        def first_pass(step, top):
            scores = nn(ck_ref[step_at(step), lanes], queries)
            return jnp.maximum(top, jnp.max(scores.reshape(STEP // 8, 8, row_count), axis=0))

        top = lax.fori_loop(
            0, steps, first_pass, jnp.full((8, row_count), NEG_FILL, WIDE), unroll=True
        )
        top = jnp.max(top, axis=0, keepdims=True)

        def second_pass(step, state):
            total, mixed = state
            weights = jnp.exp(nn(ck_ref[step_at(step), lanes], queries) - top)
            total = total + jnp.sum(weights.reshape(STEP // 8, 8, row_count), axis=0)
            return total, mixed + nn(cvt_ref[at, step_at(step)], weights.astype(LOW))

        total, mixed = lax.fori_loop(
            0, steps, second_pass,
            (jnp.zeros((8, row_count), WIDE), jnp.zeros((head, row_count), WIDE)), unroll=True,
        )
        total = jnp.sum(total, axis=0, keepdims=True)
        cross_lse_ref[h] = top + jnp.log(total)
        cross_exact_ref[at, :] = mixed / total
        return carry

    lax.fori_loop(0, HEADS, cross_forward, 0)
    cross_low_ref = refs.cross_low
    total_ref, hidden_ref, slope_ref = g_stream_ref, refs.hidden, refs.slope
    loads.w_cout.wait()

    def second_norm(block, carry):
        rows = rows_at(block)
        cross_low = cross_exact_ref[:, rows].T.astype(LOW)
        cross_low_ref[rows, :] = cross_low
        normed_one = unit_one_ref[rows, :] * gain(0) + bias(3)
        unit, scale = norm_parts(normed_one + nn(cross_low, refs.w_cout[...]) + bias(6))
        unit_two_ref[rows, :] = unit
        refs.scale_two[rows, :] = scale
        normed_two = unit * gain(1) + bias(7)
        low_two_ref[rows, :] = normed_two.astype(LOW)
        total_ref[rows, :] = normed_two + bias(8)
        return carry

    lax.fori_loop(0, own_blocks, second_norm, 0)

    loads.w_up.wait()
    loads.w_down.wait()
    w_up_ref, w_down_ref = refs.w_up, refs.w_down

    def chunk_at(chunk):
        return pl.ds(pl.multiple_of(chunk * width, width), width)

    def up_step(chunk, carry):
        pre = nn(low_two_ref[...], w_up_ref[:, chunk_at(chunk)]) + b_up_ref[:, chunk_at(chunk)]
        normal = 0.5 + 0.5 * lax.erf(pre * (2.0**-0.5))
        hidden = (pre * normal).astype(LOW)
        hidden_ref[chunk] = hidden
        slope = normal + pre * jnp.exp(-0.5 * pre * pre) * ((2.0 * jnp.pi) ** -0.5)
        slope_ref[chunk] = slope.astype(LOW)
        total_ref[...] += nn(hidden, w_down_ref[chunk_at(chunk), :])
        return carry

    lax.fori_loop(0, chunks, up_step, 0)

    low_third_ref = refs.low_third
    no_sums = (zeros_row, zeros_row, zeros_row)

    def third_norm(block, sums):
        rows = rows_at(block)
        unit, scale = norm_parts(total_ref[rows, :])
        output_ref[rows, :] = unit * gain(2) + bias(9)
        upstream = cot_ref[rows, :].astype(WIDE)
        grad = norm_pull(unit, scale, gain(2), upstream)
        low = grad.astype(LOW)
        low_third_ref[rows, :] = low
        total_ref[rows, :] = grad
        return (
            sums[0] + column_sums(upstream * unit),
            sums[1] + column_sums(upstream),
            sums[2] + column_sums(low),
        )

    sums = lax.fori_loop(0, own_blocks, third_norm, no_sums)
    few(6, sums[0])
    few(16, sums[1])
    few(15, sums[2])

    turned_ref = refs.turned
    turned_ref[...] = swap(low_two_ref[...])
    for chunk in range(chunks):
        rows = slice(chunk * width, (chunk + 1) * width)
        grad_hidden = nt(low_third_ref[...], w_down_ref[rows, :])
        grad_pre = (grad_hidden * slope_ref[chunk].astype(WIDE)).astype(LOW)
        few(chunk, column_sums(grad_pre))
        total_ref[...] += nt(grad_pre, w_up_ref[:, rows])
        grad_up = nn(turned_ref[...], grad_pre)
        put_rows(ups[chunk // 2], grad_up, (chunk % 2) * width)
        if chunk % 2 == 1:
            ups[chunk // 2].step()
        if chunk == 2:
            piece.up0.step()
        grad_down = nn(swap(hidden_ref[chunk]), low_third_ref[...])
        split = grad_down.astype(LOW).reshape(2, 2, 4, 2, HALF, width)
        for part in range(4):
            to = downs[part // 2].part
            column = (part % 2) * width
            for half in range(2):
                to[half, chunk, :, :, :, column : column + width] = split[:, :, part, half]
    piece.down0.step()
    piece.down1.step()

    dco_ref, dcot_ref = refs.dco, refs.dcot

    def second_back(block, sums):
        rows = rows_at(block)
        upstream = total_ref[rows, :]
        unit = unit_two_ref[rows, :]
        grad = norm_pull(unit, refs.scale_two[rows, :], gain(1), upstream)
        low = grad.astype(LOW)
        total_ref[rows, :] = grad
        low_third_ref[rows, :] = low
        dco_ref[rows, :] = nt(low, refs.w_cout[...]).astype(LOW)
        dcot_ref[:, rows] = nt(refs.w_cout[...], low).astype(LOW)
        return (
            sums[0] + column_sums(upstream * unit),
            sums[1] + column_sums(upstream),
            sums[2] + column_sums(low),
        )

    sums = lax.fori_loop(0, own_blocks, second_back, no_sums)
    few(5, sums[0])
    few(14, sums[1])
    few(13, sums[2])
    put_rows(piece.cross, nn(swap(cross_low_ref[...]), low_third_ref[...]), 0)
    piece.up1.step()
    piece.down0.step()
    piece.down1.step()

    dcqt_ref = refs.dcqt
    def cross_backward(pair, carry):
        lanes = pair_at(pair)
        low_half = pl.ds(pl.multiple_of(pair * pair_width, head), head)
        high_half = pl.ds(pl.multiple_of(pair * pair_width + head, head), head)
        queries_t = apart(cqt_ref[low_half, :], cqt_ref[high_half, :])
        upstream_t = apart(dcot_ref[low_half, :], dcot_ref[high_half, :])
        queries = apart_columns(cq_ref[:, lanes])
        upstream = apart_columns(dco_ref[:, lanes])
        dots = cross_exact_ref[lanes, :] * dcot_ref[lanes, :].astype(WIDE)
        delta = jnp.concatenate(
            [column_sums(dots[:head]), column_sums(dots[head:])], axis=1
        )
        lse = jnp.concatenate([cross_lse_ref[2 * pair], cross_lse_ref[2 * pair + 1]], axis=1)
        dcqt_ref[lanes, :] = jnp.zeros((pair_width, row_count), WIDE)

        def backward_step(step, carry):
            there = step_at(step)
            weights = jnp.exp(nn(ck_ref[there, lanes], queries_t) - lse)
            grad_weights = nn(cv_ref[there, lanes], upstream_t)
            grad_scores = (weights * (grad_weights - delta)).astype(LOW)
            ck_ref[there, lanes] = nn(grad_scores, queries).astype(LOW)
            cv_ref[there, lanes] = nn(weights.astype(LOW), upstream).astype(LOW)
            dcqt_ref[low_half, :] += nn(ckt_ref[low_half, there], grad_scores[:, :row_count])
            dcqt_ref[high_half, :] += nn(ckt_ref[high_half, there], grad_scores[:, row_count:])
            return carry

        lax.fori_loop(0, steps, backward_step, 0)
        return carry

    lax.fori_loop(0, pairs, cross_backward, 0)
    upstream_send = refs.mixed_send

    def first_back(block, sums):
        rows = rows_at(block)
        grad_cq = (dcqt_ref[:, rows].T * score_scale).astype(LOW)
        dco_ref[rows, :] = grad_cq
        upstream = total_ref[rows, :] + nt(grad_cq, refs.w_cq[...])
        unit = unit_one_ref[rows, :]
        grad = norm_pull(unit, refs.scale_one[rows, :], gain(0), upstream)
        low = grad.astype(LOW)
        total_ref[rows, :] = grad
        low_third_ref[rows, :] = low
        grad_attended_t = nt(refs.w_out[...], low).astype(LOW)
        for h in range(HEADS):
            upstream_send[h, block] = grad_attended_t[h * head : (h + 1) * head, :]
        return (
            sums[0] + column_sums(upstream * unit),
            sums[1] + column_sums(upstream),
            sums[2] + column_sums(low),
            sums[3] + column_sums(grad_cq),
        )

    sums = lax.fori_loop(0, own_blocks, first_back, no_sums + (zeros_row,))
    few(4, sums[0])
    few(10, sums[1])
    few(9, sums[2])
    few(11, sums[3])
    up_heads_copy = Exchange(
        spot, upstream_send, refs.up_heads_sem,
        [(0, own_blocks, all_rows, refs.up_land, all_rows)],
    )
    up_heads_copy.start()
    turned_ref[...] = swap(low_one_ref[...])
    put_rows(piece.cross, nn(turned_ref[...], dco_ref[...]), width)
    piece.cross.steps(1)
    put_rows(piece.out, nn(attended_t_ref[...], low_third_ref[...]), 0)
    piece.out.steps(1)
    for part in range(HEADS):
        rows = slice(part * mem_rows, (part + 1) * mem_rows)
        ckt_ref[:, rows] = swap(all_ref[part % 2, part // 2])
        grad = nt(ck_ref[rows, :], refs.w_ckv[:, :width]) + nt(cv_ref[rows, :], refs.w_ckv[:, width:])
        w_up_ref[
            (part // 2) * mem_rows : (part // 2 + 1) * mem_rows,
            (part % 2) * width : (part % 2 + 1) * width,
        ] = grad.astype(LOW)
    g_land = refs.memory_land
    other_side = pl.ds(pl.multiple_of((1 - spot.col) * width, width), width)
    own_side = pl.ds(pl.multiple_of(spot.col * width, width), width)
    memory_copy = remote(
        w_up_ref.at[:, other_side], g_land, refs.memory_sem.at[0, 0], refs.memory_sem.at[1, 0],
        spot.col_peer,
    )
    put_rows(piece.ckv, nn(ckt_ref[...], ck_ref[...]), 0)
    put_rows(piece.ckv, nn(ckt_ref[...], cv_ref[...]), width)
    few(12, column_sums(cv_ref[...]))
    piece.ckv.steps(1)
    for pos in range(blocks):
        at = slice(pos * BLK, (pos + 1) * BLK)
        q_ref[at, :] = swap(jnp.concatenate([qt_ref[:, at], no_head], axis=0))
    up_heads_copy.wait()
    for item in ups + downs:
        item.steps(3)
    memory_copy.start()
    for item in (piece.cross, piece.out, piece.ckv):
        item.steps(2)

    upq_ref, upt_ref = refs.up, refs.upt
    dkv_ref, dqt_ref = refs.dkv, refs.dqt
    for pos in range(blocks):
        block = refs.up_land[inv_ref[pos]]
        at = slice(pos * BLK, (pos + 1) * BLK)
        upt_ref[:, at] = block
        upq_ref[at, :] = swap(jnp.concatenate([no_head, block], axis=0))
    dkv_ref[...] = jnp.zeros_like(dkv_ref)

    def backward_tile(tile, carry):
        here = pl.ds(pl.multiple_of(tile * TILE, TILE), TILE)
        queries_t = jnp.concatenate([qt_ref[:, here], no_tile], axis=0)
        upstream_t = jnp.concatenate([no_tile, upt_ref[:, here]], axis=0)
        both = jnp.concatenate([q_ref[here, :], upq_ref[here, :]], axis=0)
        lse = lse_ref[:, here]
        exact = jnp.concatenate(
            [exact_ref[tile * (TILE // BLK) + sub] for sub in range(TILE // BLK)], axis=1
        )
        delta = column_sums(exact * upt_ref[:, here].astype(WIDE))

        def chunk_step(chunk, grad_q, hide):
            there = pl.ds(pl.multiple_of(chunk * TILE, TILE), TILE)
            scores = hide(nn(kv_ref[there, :], queries_t), chunk)
            weights = jnp.exp(scores - lse)
            grad_weights = nn(kv_ref[there, :], upstream_t)
            grad_scores = (weights * (grad_weights - delta)).astype(LOW)
            sides = jnp.concatenate([grad_scores, weights.astype(LOW)], axis=1)
            spread_at = pl.ds(chunk * (TILE // BLK), TILE // BLK)
            dkv_ref[spread_at] += nn(sides, both).reshape(TILE // BLK, BLK, 2 * head)
            return grad_q + nn(kt_ref[:, there], grad_scores)

        grad_q = tile_spans(tile, chunk_step, jnp.zeros((head, TILE), WIDE))
        grad_q = (grad_q * score_scale).astype(LOW)
        for sub in range(TILE // BLK):
            dqt_ref[tile * (TILE // BLK) + sub] = grad_q[:, sub * BLK : (sub + 1) * BLK]
        return carry

    lax.fori_loop(0, tiles // 2, backward_tile, 0)
    for item in ups + downs:
        item.steps(4)
    lax.fori_loop(tiles // 2, tiles, backward_tile, 0)

    back_send = refs.head_send
    back_copy = Exchange(
        spot, back_send, refs.back_sem,
        [
            (0, own_blocks, slice(0, head), pair_land, slice(0, head)),
            (0, own_blocks, slice(head, 2 * head), pair_land, slice(head, 2 * head)),
            (0, own_blocks, last_rows, last_land, slice(0, head)),
        ],
    )
    for row in range(blocks):
        back_send[row // own_blocks, row % own_blocks, :head] = dqt_ref[deal_ref[row]]
    back_copy.start(0)
    for row in range(blocks):
        back_send[row // own_blocks, row % own_blocks, head:] = dkv_ref[deal_ref[row]].T.astype(LOW)
    back_copy.start(1)
    back_copy.start(2)

    ones = jnp.ones((8, BLK), LOW)
    query_sums = jnp.zeros((8, head), WIDE)
    both_sums = jnp.zeros((1, 2 * head), WIDE)
    for pos in range(blocks):
        query_sums = query_sums + nt(ones, dqt_ref[pos])
        both_sums = both_sums + column_sums(dkv_ref[pos])
    own_lanes = lax.broadcasted_iota(jnp.int32, (1, width), 1) // head == spot.ctx
    few(7, jnp.where(own_lanes, jnp.concatenate([query_sums[:1]] * HEADS, axis=1), 0.0))
    few(8, jnp.where(own_lanes, jnp.concatenate([both_sums[:, head:]] * HEADS, axis=1), 0.0))

    few_core, few_plane, few_rows = refs.few_core, refs.few_plane, refs.few_rows
    few_sem = refs.few_sem
    core_copy = remote(few_ref, few_core, few_sem.at[0, 0], few_sem.at[1, 0], spot.core_peer)
    core_copy.start()
    for item in ups + downs:
        item.steps(5)
    core_copy.wait()
    own_place = spot.col * 2 + spot.wsh
    few_plane[own_place] = few_ref[...] + few_core[...]
    plane_copies = []
    for way, (target, _, _) in enumerate(spot.ways):
        copy = remote(
            few_plane.at[own_place], few_plane.at[own_place],
            few_sem.at[0, 1 + way], few_sem.at[1, 1 + way], target,
        )
        copy.start()
        plane_copies.append(copy)
    piece.cross.steps(3)
    piece.out.steps(3)
    for copy in plane_copies:
        copy.wait()
    few_rows[spot.row] = few_plane[0] + few_plane[1] + few_plane[2] + few_plane[3]
    row_copies = []
    for step in range(1, ROWS):
        copy = remote(
            few_rows.at[spot.row], few_rows.at[spot.row],
            few_sem.at[0, 3 + step], few_sem.at[1, 3 + step], spot.row_peers[step],
        )
        copy.start()
        row_copies.append(copy)
    piece.ckv.steps(3)
    memory_copy.wait()
    g_land[...] = plus(w_up_ref[:, own_side], g_land[...]).astype(LOW)
    for item in ups + downs:
        item.steps(6)

    turned_ref[...] = swap(tokens_ref[...])
    kinds = (piece.wq, piece.wk, piece.wv)
    for kind in range(3):
        back_copy.wait(kind)
        for block in range(own_blocks):
            turned = jnp.concatenate(
                [
                    (pair_land, pair_land, last_land)[kind][
                        h * own_blocks + block, kind % 2 * head : (kind % 2 + 1) * head, :
                    ]
                    for h in range(HEADS)
                ],
                axis=0,
            )
            hidden_ref[kind, block * BLK : (block + 1) * BLK, :] = swap(turned)
        put_rows(kinds[kind], nn(turned_ref[...], hidden_ref[kind]), 0)
        kinds[kind].steps(1)
        if kind > 0:
            kinds[kind - 1].steps(2)
    for item in (piece.cross, piece.out, piece.ckv):
        item.steps(4)
    memory_copies = []
    for step in range(1, ROWS):
        copy = remote(
            g_land.at[pl.ds(spot.rows_by_step[step] * mem_rows, mem_rows)], refs.memory_row.at[step - 1],
            refs.memory_sem.at[0, step], refs.memory_sem.at[1, step], spot.row_peers[step],
        )
        copy.start()
        memory_copies.append(copy)
    grad_stream = total_ref[...]
    for kind in range(3):
        if kind == 1:
            kinds[2].steps(2)
        lanes = slice(kind * width, (kind + 1) * width)
        grad_stream = grad_stream + nt(hidden_ref[kind], refs.w_qkv[:, lanes])
    g_stream_ref[...] = grad_stream
    for item in kinds:
        item.steps(3)
    for copy in row_copies:
        copy.wait()
    total = few_rows[0] + few_rows[1] + few_rows[2] + few_rows[3]
    own_shard = spot.ctx * 2 + spot.wsh
    part, long_part = width // SHARDS, hidden_width // SHARDS
    picked, long_picked = total[:, :part], total[:1, :long_part]
    for shard in range(1, SHARDS):
        picked = jnp.where(own_shard == shard, total[:, shard * part : (shard + 1) * part], picked)
        row, at = divmod(shard * long_part, width)
        long_picked = jnp.where(
            own_shard == shard, total[row : row + 1, at : at + long_part], long_picked
        )
    o_b_up_ref[...] = long_picked
    o_gains_ref[...] = picked[4:7]
    o_biases_ref[...] = picked[7:17]
    for item in (piece.cross, piece.out, piece.ckv):
        item.steps(5)
    for copy in memory_copies:
        copy.wait()
    total = g_land[pl.ds(spot.row * mem_rows, mem_rows), :].astype(WIDE)
    for step in range(ROWS - 1):
        total = total + refs.memory_row[step].astype(WIDE)
    g_memory_ref[...] = total
    for item in kinds + (piece.cross, piece.out, piece.ckv):
        item.steps(6)


def layer_scratch(row_count, width, hidden_width, mem_rows):
    own_blocks = row_count // BLK
    blocks = own_blocks * HEADS
    head = width // HEADS
    tokens = blocks * BLK
    mem_total = mem_rows * HEADS
    dma = pltpu.SemaphoreType.DMA
    scratch = dict(
        w_qkv=((width, 3 * width), LOW), w_ckv=((width, 2 * width), LOW),
        w_out=((width, width), LOW), w_cq=((width, width), LOW),
        w_cout=((width, width), LOW), w_up=((width, hidden_width), LOW),
        w_down=((hidden_width, width), LOW),
        head_send=((HEADS, own_blocks, 3 * head, BLK), LOW),
        pair_land=((blocks, 2 * head, BLK), LOW), last_land=((blocks, head, BLK), LOW),
        memory_all=((2, ROWS, mem_rows, width), LOW),
        q=((tokens, 2 * head), LOW), kv=((tokens, 2 * head), LOW),
        qt=((head, tokens), LOW), kt=((head, tokens), LOW), vt=((head, tokens), LOW),
        exact=((blocks, head, BLK), WIDE), lse=((1, tokens), WIDE),
        mixed_send=((HEADS, own_blocks, head, BLK), LOW),
        mixed_land=((blocks, head, BLK), LOW),
        ck=((mem_total, width), LOW), cv=((mem_total, width), LOW),
        ckt=((width, mem_total), LOW), cvt=((width, mem_total), LOW),
        attended_t=((width, row_count), LOW),
        unit_one=((row_count, width), WIDE), unit_two=((row_count, width), WIDE),
        scale_one=((row_count, 1), WIDE), scale_two=((row_count, 1), WIDE),
        low_one=((row_count, width), LOW), low_two=((row_count, width), LOW),
        cq=((row_count, width), LOW), cqt=((width, row_count), LOW),
        cross_exact=((width, row_count), WIDE),
        cross_lse=((HEADS, 1, row_count), WIDE),
        cross_low=((row_count, width), LOW),
        hidden=((hidden_width // width, row_count, width), LOW),
        slope=((hidden_width // width, row_count, width), LOW),
        low_third=((row_count, width), LOW),
        turned=((width, row_count), LOW),
        dco=((row_count, width), LOW), dcot=((width, row_count), LOW),
        dcqt=((width, row_count), WIDE),
        memory_land=((ROWS * mem_rows, width), LOW),
        memory_row=((ROWS - 1, mem_rows, width), LOW),
        up_land=((blocks, head, BLK), LOW),
        up=((tokens, 2 * head), LOW), upt=((head, tokens), LOW),
        dkv=((blocks, BLK, 2 * head), WIDE), dqt=((blocks, head, BLK), LOW),
        few_sum=((FEW_ROWS, width), WIDE), few_core=((FEW_ROWS, width), WIDE),
        few_plane=((4, FEW_ROWS, width), WIDE), few_rows=((ROWS, FEW_ROWS, width), WIDE),
    )
    out = {name: pltpu.VMEM(shape, kind) for name, (shape, kind) in scratch.items()}
    out.update(
        load_sem=dma((7,)), to_heads_sem=dma((2, HEADS, 4)), from_heads_sem=dma((2, HEADS, 1)),
        up_heads_sem=dma((2, HEADS, 1)), back_sem=dma((2, HEADS, 3)), spread_sem=dma((2, 2 * ROWS)),
        inverse=pltpu.SMEM((blocks,), jnp.int32),
        memory_sem=dma((2, ROWS)), few_sem=dma((2, 7)),
    )
    out.update(
        pieces={
            name: dict(
                part=pltpu.VMEM((2, ROWS, 2, 2, HALF, span), LOW),
                core_land=pltpu.VMEM((ROWS, 2, 2, HALF, span), LOW),
                hop_land=pltpu.VMEM(
                    (3, ROWS, HALF, span) if TURNS[name] == 2 else (ROWS, 2, HALF, span), LOW
                ),
                turn_land=pltpu.VMEM((ROWS, HALF, span), LOW),
                row_land=pltpu.VMEM(
                    (2, ROWS, HALF, span) if TURNS[name] == 2 else (ROWS - 1, HALF, span), LOW
                ),
                sems=dma((2, 12)),
            )
            for name, span in PIECES.items()
        }
    )
    return out


def layer_call(deal_ids, offsets, opened, tokens, memory, cotangent, weights, b_up, gains, biases, prompt_blocks):
    row_count, width = tokens.shape
    hidden_width = b_up.shape[1]
    mem_rows = memory.shape[0]
    smem = pl.BlockSpec(memory_space=pltpu.SMEM)
    vmem = pl.BlockSpec(memory_space=pltpu.VMEM)
    hbm = pl.BlockSpec(memory_space=pl.ANY)
    scratch = layer_scratch(row_count, width, hidden_width, mem_rows)
    leaves, tree = jax.tree.flatten(scratch, is_leaf=lambda leaf: not isinstance(leaf, dict))
    out_shapes = [
        (row_count, width), (row_count, width), (mem_rows, width),
        (32, 3 * width), (32, width), (32, width), (32, 2 * width), (32, width),
        (32, hidden_width), (hidden_width // SHARDS, width),
        (1, hidden_width // SHARDS), (3, width // SHARDS), (10, width // SHARDS),
    ]

    def body(*args):
        count = len(args) - len(leaves)
        refs = Bag(jax.tree.unflatten(tree, args[count:]))
        layer_kernel(prompt_blocks, *args[:count], refs)

    return pl.pallas_call(
        body,
        out_shape=[jax.ShapeDtypeStruct(shape, WIDE) for shape in out_shapes],
        in_specs=[smem] * 3 + [vmem] * 3 + [hbm] * 7 + [vmem] * 3,
        out_specs=[vmem] * len(out_shapes),
        scratch_shapes=leaves,
        compiler_params=pltpu.CompilerParams(
            collective_id=0, has_side_effects=True, vmem_limit_bytes=BIG_VMEM
        ),
        name="layer",
    )(deal_ids, offsets, opened, tokens, memory, cotangent, *weights, b_up, gains, biases)


def hand_out_kernel(count, *refs):
    for index in range(count):
        refs[count + index][...] = refs[index][...]


def hand_out(arrays):
    count = len(arrays)
    vmem = pl.BlockSpec(memory_space=pltpu.VMEM)
    return pl.pallas_call(
        functools.partial(hand_out_kernel, count),
        out_shape=[jax.ShapeDtypeStruct(a.shape, a.dtype) for a in arrays],
        in_specs=[vmem] * count,
        out_specs=[vmem] * count,
        compiler_params=pltpu.CompilerParams(vmem_limit_bytes=BIG_VMEM),
        name="hand_out",
    )(*arrays)


def layer_shards(
    stream, memory, cotangent, deal_order, offsets, context_mask,
    w_qkv, w_out, w_cq, w_ckv, w_cout, w_up, w_down, b_up, gains, biases,
):
    results = layer_call(
        deal_order[0, 0], offsets[0, 0], context_mask[0, 0],
        stream[0, 0], memory[0, 0], cotangent[0, 0],
        (w_qkv, w_out, w_cq, w_ckv, w_cout, w_up, w_down),
        b_up[None, :], gains, biases, context_mask.shape[3],
    )
    output, grad_stream, grad_memory, *grads = hand_out(results)
    grads[7] = grads[7].reshape(-1)
    return (output[None, None], grad_stream[None, None], grad_memory[None, None], *grads)


def gelu_exact(values):
    return jax.nn.gelu(values, approximate=False)


def norm_rows(values, gain_vec, shift_vec):
    center = values - jnp.mean(values, axis=-1, keepdims=True)
    spread = jnp.mean(center * center, axis=-1, keepdims=True)
    return center * lax.rsqrt(spread + EPS_NORM) * gain_vec + shift_vec


def norm_back(values, gain_vec, shift_vec, upstream):
    _, pullback = jax.vjp(norm_rows, values, gain_vec, shift_vec)
    return pullback(upstream)


def seq_index(positions, prompt_len, cont_len):
    later = jnp.int32(1) + (positions - jnp.int32(prompt_len)) // jnp.int32(cont_len)
    return jnp.where(positions < prompt_len, jnp.zeros_like(later), later)


def visible(query_pos, key_ids, offsets, context_mask, block_len, prompt_blocks, cont_blocks):
    prompt_len = prompt_blocks * block_len
    cont_len = cont_blocks * block_len
    cont_count = offsets.shape[0]
    key_pos = (
        key_ids[:, None] * jnp.int32(block_len) + jnp.arange(block_len, dtype=jnp.int32)[None, :]
    ).reshape(-1)
    query_seq = seq_index(query_pos, prompt_len, cont_len)
    key_seq = seq_index(key_pos, prompt_len, cont_len)
    inside = (query_seq[:, None] == key_seq[None, :]) & (key_pos[None, :] <= query_pos[:, None])
    cont_pick = jnp.clip(query_seq - 1, 0, cont_count - 1)
    prompt_limit = jnp.take(offsets, cont_pick)
    query_block = jnp.clip(
        (query_pos - jnp.int32(prompt_len)) // jnp.int32(block_len), 0, cont_count * cont_blocks - 1
    )
    mask_rows = jnp.take(context_mask, query_block, axis=0)
    key_block = jnp.clip(key_ids, 0, prompt_blocks - 1)
    block_open = jnp.take(mask_rows, key_block, axis=1) > 0
    block_open = jnp.repeat(block_open, block_len, axis=1) | (key_pos[None, :] < block_len)
    from_prompt = (
        (query_seq[:, None] > 0)
        & (key_seq[None, :] == 0)
        & (key_pos[None, :] < prompt_limit[:, None])
        & block_open
    )
    return inside | from_prompt


def dot_first(left, right):
    return lax.dot_general(
        left, right, (((0,), (0,)), ((), ())), preferred_element_type=jnp.float32
    )


def dot_last(left, right):
    return lax.dot_general(
        left, right, (((1,), (1,)), ((), ())), preferred_element_type=jnp.float32
    )


def to_heads(matrix, head_count):
    row_count, model_width = matrix.shape
    return matrix.reshape(row_count, head_count, model_width // head_count).transpose(1, 0, 2)


def from_heads(stacked):
    head_count, row_count, head_width = stacked.shape
    return stacked.transpose(1, 0, 2).reshape(row_count, head_count * head_width)


def pair_heads(key_rows, value_rows, head_count):
    return jnp.concatenate(
        [to_heads(key_rows, head_count), to_heads(value_rows, head_count)], axis=2
    )


def head_scores(queries, key_rows, allowed):
    score_scale = queries.shape[1] ** (-0.5)
    scores = dot_last(queries, key_rows) * score_scale
    if allowed is not None:
        scores = jnp.where(allowed, scores, NEG_FILL)
    return scores


def head_forward(queries, keyval, allowed):
    head_width = queries.shape[1]
    scores = head_scores(queries, keyval[:, :head_width], allowed)
    row_top = jnp.max(scores, axis=1, keepdims=True)
    exp_scores = jnp.exp(scores - row_top)
    row_total = jnp.sum(exp_scores, axis=1, keepdims=True)
    soft_weights = (exp_scores / row_total).astype(jnp.bfloat16)
    mixed_heads = jnp.dot(soft_weights, keyval[:, head_width:], preferred_element_type=jnp.float32)
    return (mixed_heads, row_top + jnp.log(row_total))


def head_backward(queries, keyval, upstream, log_total, allowed):
    head_width = queries.shape[1]
    score_scale = head_width ** (-0.5)
    key_rows = keyval[:, :head_width]
    scores = head_scores(queries, key_rows, allowed)
    soft_weights = jnp.exp(scores - log_total)
    grad_soft = dot_last(upstream, keyval[:, head_width:])
    row_delta = jnp.sum(soft_weights * grad_soft, axis=1, keepdims=True)
    grad_scores = (soft_weights * (grad_soft - row_delta)).astype(jnp.bfloat16)
    grad_query = jnp.dot(grad_scores, key_rows, preferred_element_type=jnp.float32) * score_scale
    grad_keys = dot_first(grad_scores, queries) * score_scale
    grad_values = dot_first(soft_weights.astype(jnp.bfloat16), upstream)
    return (grad_query, jnp.concatenate([grad_keys, grad_values], axis=1))


def shards(
    stream,
    memory,
    cotangent,
    deal_order,
    offsets,
    context_mask,
    w_qkv,
    w_out,
    w_cq,
    w_ckv,
    w_cout,
    w_up,
    w_down,
    b_up,
    gains,
    biases,
):
    tokens = stream[0, 0]
    row_count, model_width = tokens.shape
    head_width = model_width // HEADS
    deal_ids = deal_order[0, 0]
    prompt_blocks = context_mask.shape[3]
    own_blocks = row_count // BLK
    own_ids = lax.dynamic_slice_in_dim(deal_ids, lax.axis_index("ctx") * own_blocks, own_blocks)
    query_pos = (
        own_ids[:, None] * jnp.int32(BLK) + jnp.arange(BLK, dtype=jnp.int32)[None, :]
    ).reshape(-1)
    allowed = visible(
        query_pos, deal_ids, offsets[0, 0], context_mask[0, 0], BLK, prompt_blocks, CBLK
    )
    zeros_row = jnp.zeros((model_width,), jnp.float32)
    projected = (
        jnp.dot(tokens, w_qkv, preferred_element_type=jnp.float32)
        + jnp.concatenate([biases[0], zeros_row, biases[1]])
    ).astype(jnp.bfloat16)
    query_heads = to_heads(projected[:, :model_width], HEADS)
    keyval_own = pair_heads(
        projected[:, model_width : 2 * model_width], projected[:, 2 * model_width :], HEADS
    )
    keyval_all = lax.all_gather(keyval_own, "ctx", axis=1, tiled=True)

    def self_forward(pieces):
        return head_forward(pieces[0], pieces[1], allowed)

    self_out, self_lse = lax.map(self_forward, (query_heads, keyval_all))
    attended = from_heads(self_out).astype(jnp.bfloat16)
    first_sum = (
        tokens.astype(jnp.float32)
        + jnp.dot(attended, w_out, preferred_element_type=jnp.float32)
        + biases[2]
    )
    normed_one = norm_rows(first_sum, gains[0], biases[3])
    normed_low = normed_one.astype(jnp.bfloat16)
    cross_query = (
        jnp.dot(normed_low, w_cq, preferred_element_type=jnp.float32) + biases[4]
    ).astype(jnp.bfloat16)
    cross_bias = jnp.concatenate([zeros_row, biases[5]])
    memory_own = memory[0, 0]
    memory_all = lax.all_gather(memory_own, "ctx", axis=0, tiled=True)
    cross_kv = (jnp.dot(memory_all, w_ckv, preferred_element_type=jnp.float32) + cross_bias).astype(
        jnp.bfloat16
    )
    cross_heads = pair_heads(cross_kv[:, :model_width], cross_kv[:, model_width:], HEADS)
    cross_query_heads = to_heads(cross_query, HEADS)

    def cross_forward(pieces):
        return head_forward(pieces[0], pieces[1], None)

    cross_out, cross_lse = lax.map(cross_forward, (cross_query_heads, cross_heads))
    cross_attended = from_heads(cross_out).astype(jnp.bfloat16)
    second_sum = (
        normed_one + jnp.dot(cross_attended, w_cout, preferred_element_type=jnp.float32) + biases[6]
    )
    normed_two = norm_rows(second_sum, gains[1], biases[7])
    normed_two_low = normed_two.astype(jnp.bfloat16)
    hidden_pre = jnp.dot(normed_two_low, w_up, preferred_element_type=jnp.float32) + b_up
    hidden = gelu_exact(hidden_pre).astype(jnp.bfloat16)
    third_sum = normed_two + jnp.dot(hidden, w_down, preferred_element_type=jnp.float32) + biases[8]
    output = norm_rows(third_sum, gains[2], biases[9])
    grad_third, grad_gain_three, grad_shift_three = norm_back(
        third_sum, gains[2], biases[9], cotangent[0, 0].astype(jnp.float32)
    )
    grad_down_in = grad_third.astype(jnp.bfloat16)
    grad_w_down = dot_first(hidden, grad_down_in)
    grad_b_down = jnp.sum(grad_down_in.astype(jnp.float32), axis=0)
    grad_hidden = dot_last(grad_down_in, w_down)
    _, gelu_pull = jax.vjp(gelu_exact, hidden_pre)
    grad_pre = gelu_pull(grad_hidden)[0].astype(jnp.bfloat16)
    grad_w_up = dot_first(normed_two_low, grad_pre)
    grad_b_up = jnp.sum(grad_pre.astype(jnp.float32), axis=0)
    grad_normed_two = grad_third + dot_last(grad_pre, w_up)
    grad_second, grad_gain_two, grad_shift_two = norm_back(
        second_sum, gains[1], biases[7], grad_normed_two
    )
    grad_cross_in = grad_second.astype(jnp.bfloat16)
    grad_w_cout = dot_first(cross_attended, grad_cross_in)
    grad_b_co = jnp.sum(grad_cross_in.astype(jnp.float32), axis=0)
    grad_cross_heads = to_heads(dot_last(grad_cross_in, w_cout).astype(jnp.bfloat16), HEADS)

    def cross_backward(pieces):
        return head_backward(pieces[0], pieces[1], pieces[2], pieces[3], None)

    grad_cq_heads, grad_ckv_all = lax.map(
        cross_backward, (cross_query_heads, cross_heads, grad_cross_heads, cross_lse)
    )
    grad_ckv_own = lax.psum_scatter(
        grad_ckv_all.astype(jnp.bfloat16), "ctx", scatter_dimension=1, tiled=True
    )
    grad_cv = from_heads(grad_ckv_own[:, :, head_width:])
    grad_ckv = jnp.concatenate([from_heads(grad_ckv_own[:, :, :head_width]), grad_cv], axis=1)
    grad_w_ckv = dot_first(memory_own, grad_ckv)
    grad_b_cv = jnp.sum(grad_cv.astype(jnp.float32), axis=0)
    grad_memory = dot_last(grad_ckv, w_ckv)
    grad_cq = from_heads(grad_cq_heads).astype(jnp.bfloat16)
    grad_w_cq = dot_first(normed_low, grad_cq)
    grad_b_cq = jnp.sum(grad_cq.astype(jnp.float32), axis=0)
    grad_normed_one = grad_second + dot_last(grad_cq, w_cq)
    grad_first, grad_gain_one, grad_shift_one = norm_back(
        first_sum, gains[0], biases[3], grad_normed_one
    )
    grad_att_in = grad_first.astype(jnp.bfloat16)
    grad_w_out = dot_first(attended, grad_att_in)
    grad_b_o = jnp.sum(grad_att_in.astype(jnp.float32), axis=0)
    grad_self_heads = to_heads(dot_last(grad_att_in, w_out).astype(jnp.bfloat16), HEADS)

    def self_backward(pieces):
        return head_backward(pieces[0], pieces[1], pieces[2], pieces[3], allowed)

    grad_q_heads, grad_kv_all = lax.map(
        self_backward, (query_heads, keyval_all, grad_self_heads, self_lse)
    )
    grad_kv_own = lax.psum_scatter(
        grad_kv_all.astype(jnp.bfloat16), "ctx", scatter_dimension=1, tiled=True
    )
    grad_values = from_heads(grad_kv_own[:, :, head_width:])
    grad_queries = from_heads(grad_q_heads).astype(jnp.bfloat16)
    grad_proj = jnp.concatenate(
        [grad_queries, from_heads(grad_kv_own[:, :, :head_width]), grad_values], axis=1
    )
    grad_w_qkv = dot_first(tokens, grad_proj)
    grad_b_q = jnp.sum(grad_queries.astype(jnp.float32), axis=0)
    grad_b_v = jnp.sum(grad_values.astype(jnp.float32), axis=0)
    grad_tokens = grad_first + dot_last(grad_proj, w_qkv)
    gain_grads = jnp.stack([grad_gain_one, grad_gain_two, grad_gain_three])
    shift_grads = jnp.stack(
        [
            grad_b_q,
            grad_b_v,
            grad_b_o,
            grad_shift_one,
            grad_b_cq,
            grad_b_cv,
            grad_b_co,
            grad_shift_two,
            grad_b_down,
            grad_shift_three,
        ]
    )
    (
        part_qkv,
        part_out,
        part_cq,
        part_ckv,
        part_cout,
        part_up,
        part_down,
        part_b_up,
        part_gains,
        part_biases,
    ) = (
        lax.psum_scatter(grad_w_qkv, ("ctx", "wsh"), scatter_dimension=0, tiled=True),
        lax.psum_scatter(grad_w_out, ("ctx", "wsh"), scatter_dimension=0, tiled=True),
        lax.psum_scatter(grad_w_cq, ("ctx", "wsh"), scatter_dimension=0, tiled=True),
        lax.psum_scatter(grad_w_ckv, ("ctx", "wsh"), scatter_dimension=0, tiled=True),
        lax.psum_scatter(grad_w_cout, ("ctx", "wsh"), scatter_dimension=0, tiled=True),
        lax.psum_scatter(grad_w_up, ("ctx", "wsh"), scatter_dimension=0, tiled=True),
        lax.psum_scatter(grad_w_down, ("ctx", "wsh"), scatter_dimension=0, tiled=True),
        lax.psum_scatter(grad_b_up, ("ctx", "wsh"), scatter_dimension=0, tiled=True),
        lax.psum_scatter(gain_grads, ("ctx", "wsh"), scatter_dimension=1, tiled=True),
        lax.psum_scatter(shift_grads, ("ctx", "wsh"), scatter_dimension=1, tiled=True),
    )
    (
        total_qkv,
        total_out,
        total_cq,
        total_ckv,
        total_cout,
        total_up,
        total_down,
        total_b_up,
        total_gains,
        total_biases,
    ) = (
        lax.psum(part_qkv.astype(jnp.bfloat16), "grp").astype(jnp.float32),
        lax.psum(part_out.astype(jnp.bfloat16), "grp").astype(jnp.float32),
        lax.psum(part_cq.astype(jnp.bfloat16), "grp").astype(jnp.float32),
        lax.psum(part_ckv.astype(jnp.bfloat16), "grp").astype(jnp.float32),
        lax.psum(part_cout.astype(jnp.bfloat16), "grp").astype(jnp.float32),
        lax.psum(part_up.astype(jnp.bfloat16), "grp").astype(jnp.float32),
        lax.psum(part_down.astype(jnp.bfloat16), "grp").astype(jnp.float32),
        lax.psum(part_b_up.astype(jnp.bfloat16), "grp").astype(jnp.float32),
        lax.psum(part_gains.astype(jnp.bfloat16), "grp").astype(jnp.float32),
        lax.psum(part_biases.astype(jnp.bfloat16), "grp").astype(jnp.float32),
    )
    return (
        output[None, None],
        grad_tokens[None, None],
        grad_memory[None, None],
        total_qkv,
        total_out,
        total_cq,
        total_ckv,
        total_cout,
        total_up,
        total_down,
        total_b_up,
        total_gains,
        total_biases,
    )


def solution(mesh):
    in_specs = (
        P("grp", "wsh", "ctx", None),
        P("grp", "wsh", "ctx", None),
        P("grp", "wsh", "ctx", None),
        P("grp", "wsh", None),
        P("grp", "wsh", None),
        P("grp", "wsh", None, None),
        P(),
        P(),
        P(),
        P(),
        P(),
        P(),
        P(),
        P(),
        P(),
        P(),
    )
    out_specs = (
        P("grp", "wsh", "ctx", None),
        P("grp", "wsh", "ctx", None),
        P("grp", "wsh", "ctx", None),
        P(("ctx", "wsh"), None),
        P(("ctx", "wsh"), None),
        P(("ctx", "wsh"), None),
        P(("ctx", "wsh"), None),
        P(("ctx", "wsh"), None),
        P(("ctx", "wsh"), None),
        P(("ctx", "wsh"), None),
        P(("ctx", "wsh")),
        P(None, ("ctx", "wsh")),
        P(None, ("ctx", "wsh")),
    )
    body = layer_shards if mesh.shape["ctx"] == HEADS else shards
    return jax.shard_map(body, mesh=mesh, in_specs=in_specs, out_specs=out_specs, check_vma=False)
```
